32 devices in a mesh: dp: 16 (over z, y, x), chan: 2 (over core).
Axes of the slice: x: 2, y: 2, z: 4, core: 2. Of those that a mesh axis runs over, the one named last changes fastest.
Arguments:
- counts: int32 [16], P('dp'), may hold values from 1 to 2, as said below
- features_in: bfloat16 [32, 16, 16, 512], P('dp', None, None, 'chan'), may hold values from -6 to 6
- rgb_in: float32 [32, 3, 16, 16], P('dp'), may hold values from -6 to 6
- latent: bfloat16 [32, 512], P('dp'), may hold values from -6 to 6
- affine_one: bfloat16 [512, 512], P(None, 'chan'), may hold values from -0.25 to 0.25
- affine_bias_one: float32 [512], P('chan'), may hold values from 0.5 to 1.5
- affine_two: bfloat16 [512, 512], P(None, 'chan'), may hold values from -0.25 to 0.25
- affine_bias_two: float32 [512], P('chan'), may hold values from 0.5 to 1.5
- affine_three: bfloat16 [512, 512], P(None, 'chan'), may hold values from -0.25 to 0.25
- affine_bias_three: float32 [512], P('chan'), may hold values from 0.5 to 1.5
- kernel_one: bfloat16 [3, 3, 512, 512], P(None, None, 'chan'), may hold values from -0.09375 to 0.09375
- bias_one: float32 [512], P('chan'), may hold values from -2 to 2
- kernel_two: bfloat16 [3, 3, 512, 512], P(None, None, 'chan'), may hold values from -0.09375 to 0.09375
- bias_two: float32 [512], P('chan'), may hold values from -2 to 2
- rgb_weight: bfloat16 [3, 512], P(None, 'chan'), may hold values from -0.25 to 0.25
- rgb_bias: float32 [3], replicated, may hold values from -2 to 2
- noise_gain: float32 [2], replicated, may hold values from 0.3 to 1
- noise_one: float32 [32, 32, 32], P('dp'), may hold values from -6 to 6
- noise_two: float32 [32, 32, 32], P('dp'), may hold values from -6 to 6
- grad_features: bfloat16 [32, 32, 32, 512], P('dp', None, None, 'chan'), may hold values from -6 to 6
- grad_rgb: bfloat16 [32, 3, 32, 32], P('dp'), may hold values from -6 to 6
Outputs:
- features_out: bfloat16 [32, 32, 32, 512], P('dp', None, None, 'chan')
- rgb_out: float32 [32, 3, 32, 32], P('dp')
- grad_features_in: float32 [32, 16, 16, 512], P('dp', None, None, 'chan')
- grad_rgb_in: float32 [32, 3, 16, 16], P('dp')
- grad_latent: float32 [32, 512], P('dp')
- grad_affine_one: float32 [512, 512], P(None, 'chan')
- grad_affine_bias_one: float32 [512], P('chan')
- grad_affine_two: float32 [512, 512], P(None, 'chan')
- grad_affine_bias_two: float32 [512], P('chan')
- grad_affine_three: float32 [512, 512], P(None, 'chan')
- grad_affine_bias_three: float32 [512], P('chan')
- grad_kernel_one: float32 [3, 3, 512, 512], P(None, None, 'chan')
- grad_bias_one: float32 [512], P('chan')
- grad_kernel_two: float32 [3, 3, 512, 512], P(None, None, 'chan')
- grad_bias_two: float32 [512], P('chan')
- grad_rgb_weight: float32 [3, 512], P(None, 'chan')
- grad_rgb_bias: float32 [3], replicated
- grad_noise_gain: float32 [2], replicated
- rms_values: float32 [3], replicated
The draws below stay inside these ranges and needn't reach their ends.
Inputs may be any that keep to these rules, and one draw needn't show every extreme that they name: counts gives each index of dp its number of real images among its 2 slots; in every draw some index holds 2 and some other holds 1.
All inputs are finite; a program needn't handle non-finite values.
Results may differ from the reference program's by a relative error of at most 0.0058.
Values may be sent and summed in bfloat16 or wider, within the bound.
No kernel may reach another device: no remote copies, remote signals or barrier semaphores. Data moves between devices by JAX's collectives and lax.ppermute only.
A program may use at most 128 MiB of HBM per device.

```python
import jax
import jax.numpy as jnp
from jax import lax

C = 512
WDIM = 512
RES = 32
IMG_DEV = 2
HALF = 16
IMAGES = 32
N_DP = 16


def draw_counts(key, part):
    key = jax.random.fold_in(key, 11)
    subkeys = jax.random.split(key, 4)
    surplus = jax.random.randint(subkeys[0], (N_DP,), 0, IMG_DEV)
    frequent = jax.random.randint(subkeys[1], (N_DP,), 0, 4) == 0
    drawn = 1 + jnp.where(frequent, surplus, 0)
    fullest = jax.random.randint(subkeys[2], (), 0, N_DP)
    distance = jax.random.randint(subkeys[3], (), 1, N_DP)
    emptiest = (fullest + distance) % N_DP
    drawn = drawn.at[fullest].set(IMG_DEV).at[emptiest].set(1)
    return drawn.astype(jnp.int32)


def block_levels(own_key, shape, cuts, least, high):
    loudness, own = 1.0, jax.random.fold_in(own_key, 6)
    for axis_at, parts in cuts:
        draws = jnp.exp(jax.random.uniform(jax.random.fold_in(own, axis_at), (parts,), jnp.float32, least / len(cuts), high / len(cuts)))
        loudness = loudness * jnp.repeat(draws, shape[axis_at] // parts).reshape([-1 if axis == axis_at else 1 for axis in range(len(shape))])
    return loudness


def normal_values(own_key, dims, scale, bound, cuts=(), kind=jnp.bfloat16):
    factor_of = block_levels(own_key, dims, cuts, -0.22, 0.18) if cuts else 1.0
    result = jax.random.normal(own_key, dims, jnp.float32) * scale * factor_of
    return jnp.minimum(jnp.maximum(result, -bound), bound).astype(kind)


def setup_inputs(seed: int = 0) -> dict:
    splits = jax.random.split(jax.random.key(seed), 22)
    return {
        "counts": draw_counts(jax.random.fold_in(splits[21], 71), 0),
        "features_in": normal_values(splits[1], (IMAGES, HALF, HALF, C), 1.0, 6.0, ((0, 16), (3, 2))),
        "rgb_in": normal_values(splits[2], (IMAGES, 3, HALF, HALF), 1.0, 6.0, ((0, 16),), jnp.float32),
        "latent": normal_values(splits[3], (IMAGES, WDIM), 1.0, 6.0, ((0, 16),)),
        "affine_one": normal_values(splits[4], (WDIM, C), WDIM ** -0.5, 0.25, ((1, 2),)),
        "affine_bias_one": jnp.clip(1.0 + 0.1 * jax.random.normal(splits[5], (C,), jnp.float32), 0.5, 1.5),
        "affine_two": normal_values(splits[6], (WDIM, C), WDIM ** -0.5, 0.25, ((1, 2),)),
        "affine_bias_two": jnp.clip(1.0 + 0.1 * jax.random.normal(splits[7], (C,), jnp.float32), 0.5, 1.5),
        "affine_three": normal_values(splits[8], (WDIM, C), WDIM ** -0.5, 0.25, ((1, 2),)),
        "affine_bias_three": jnp.clip(1.0 + 0.1 * jax.random.normal(splits[9], (C,), jnp.float32), 0.5, 1.5),
        "kernel_one": normal_values(splits[10], (3, 3, C, C), (9 * C) ** -0.5, 0.09375, ((2, 2),)),
        "bias_one": normal_values(splits[11], (C,), 0.3, 2.0, ((0, 2),), jnp.float32),
        "kernel_two": normal_values(splits[12], (3, 3, C, C), (9 * C) ** -0.5, 0.09375, ((2, 2),)),
        "bias_two": normal_values(splits[13], (C,), 0.3, 2.0, ((0, 2),), jnp.float32),
        "rgb_weight": normal_values(splits[14], (3, C), C ** -0.5, 0.25, ((1, 2),)),
        "rgb_bias": normal_values(splits[15], (3,), 0.5, 2.0, (), jnp.float32),
        "noise_gain": jnp.clip(jax.random.uniform(splits[16], (2,), jnp.float32, 0.3, 1.0), 0.3, 1.0),
        "noise_one": normal_values(splits[17], (IMAGES, RES, RES), 1.0, 6.0, ((0, 16),), jnp.float32),
        "noise_two": normal_values(splits[18], (IMAGES, RES, RES), 1.0, 6.0, ((0, 16),), jnp.float32),
        "grad_features": normal_values(splits[19], (IMAGES, RES, RES, C), 1.0, 6.0, ((0, 16), (3, 2))),
        "grad_rgb": normal_values(splits[20], (IMAGES, 3, RES, RES), 1.0, 6.0, ((0, 16),)),
    }


@jax.custom_vjp
def low(v):
    return lax.optimization_barrier(v.astype(jnp.bfloat16)).astype(jnp.float32)

@jax.custom_vjp
def low_back(v):
    return v

def low_keep(v):
    return (low(v), None)

def low_pass(kept, grad):
    return (grad,)

def back_keep(v):
    return (v, None)

def back_low(kept, grad):
    return (low(grad),)
low.defvjp(low_keep, low_pass)
low_back.defvjp(back_keep, back_low)
SQRT_TWO = 1.4142135623730951
EPSILON = 1e-08

def smooth_leaky(values):
    return SQRT_TWO * (0.2 * values + 0.8 * jax.nn.softplus(values))

def upsample_axis(values, axis_dim):
    length = values.shape[axis_dim]
    widths = [(0, 0)] * values.ndim
    widths[axis_dim] = (1, 1)
    padded = jnp.pad(values, widths)
    previous = lax.slice_in_dim(padded, 0, length, axis=axis_dim)
    following = lax.slice_in_dim(padded, 2, length + 2, axis=axis_dim)
    even_part = 0.25 * previous + 0.75 * values
    odd_part = 0.75 * values + 0.25 * following
    joined = jnp.stack([even_part, odd_part], axis=axis_dim + 1)
    new_shape = list(values.shape)
    new_shape[axis_dim] = 2 * length
    return joined.reshape(new_shape)

def upsample_rgb(values):
    return upsample_axis(upsample_axis(values, 2), 3)

def modulated(inputs, styles, kernel, biases, noise_map, gain_value, dilation, padding):
    scaled = low(inputs * styles[:, None, None, :])
    output = low_back(lax.conv_general_dilated(scaled, kernel, (1, 1), padding, lhs_dilation=dilation, dimension_numbers=('NHWC', 'HWIO', 'NHWC'), precision=lax.Precision.HIGHEST))
    squares = lax.optimization_barrier(jnp.sum(kernel * kernel, axis=(0, 1)))
    demod = lax.rsqrt(jnp.dot(styles * styles, squares, precision=lax.Precision.HIGHEST) + EPSILON)
    pre_act = output * demod[:, None, None, :] + gain_value * noise_map[..., None] + biases
    return smooth_leaky(pre_act)

def forward(weights, features_in, rgb_in, latent, noise_first, noise_second):
    affine_one, affine_bias_one, affine_two, affine_bias_two, affine_three, affine_bias_three, kernel_one, bias_one, kernel_two, bias_two, rgb_weight, rgb_bias, noise_gain = weights
    style_one = jnp.dot(latent, affine_one, precision=lax.Precision.HIGHEST) + affine_bias_one
    style_two = jnp.dot(latent, affine_two, precision=lax.Precision.HIGHEST) + affine_bias_two
    style_three = jnp.dot(latent, affine_three, precision=lax.Precision.HIGHEST) + affine_bias_three
    hidden_one = modulated(features_in, style_one, kernel_one, bias_one, noise_first, noise_gain[0], (2, 2), ((1, 2), (1, 2)))
    hidden_two = modulated(hidden_one, style_two, kernel_two, bias_two, noise_second, noise_gain[1], (1, 1), ((1, 1), (1, 1)))
    to_rgb = low(hidden_two * style_three[:, None, None, :])
    rgb_image = upsample_rgb(rgb_in) + jnp.einsum('bhwi,ki->bkhw', to_rgb, rgb_weight, precision=lax.Precision.HIGHEST) + rgb_bias[None, :, None, None]
    return ((hidden_two, rgb_image), hidden_one)

def reference(counts, features_in, rgb_in, latent, affine_one, affine_bias_one, affine_two, affine_bias_two, affine_three, affine_bias_three, kernel_one, bias_one, kernel_two, bias_two, rgb_weight, rgb_bias, noise_gain, noise_one, noise_two, grad_features, grad_rgb):
    slot_ids = jnp.arange(IMAGES, dtype=jnp.int32)
    valid_mask = (slot_ids % IMG_DEV < counts[slot_ids // IMG_DEV]).astype(jnp.float32)
    weights = tuple((member.astype(jnp.float32) for member in (affine_one, affine_bias_one, affine_two, affine_bias_two, affine_three, affine_bias_three, kernel_one, bias_one, kernel_two, bias_two, rgb_weight, rgb_bias, noise_gain)))

    def one_image(running, image_items):
        totals, squares = running
        image_row, rgb_row, latent_row, noise_first, noise_second, grad_image, grad_colour, keep_flag = image_items

        def run_block(weight_set, image_in, rgb_image_in, latent_in):
            return forward(weight_set, image_in, rgb_image_in, latent_in, noise_first[None], noise_second[None])
        outputs, pullback, hidden_one = jax.vjp(run_block, weights, image_row.astype(jnp.float32)[None], rgb_row[None], latent_row.astype(jnp.float32)[None], has_aux=True)
        hidden_two, rgb_image = outputs
        grad_sets = pullback((grad_image.astype(jnp.float32)[None] * keep_flag, grad_colour.astype(jnp.float32)[None] * keep_flag))
        totals = jax.tree.map(jnp.add, totals, grad_sets[0])
        squares = squares + keep_flag * jnp.stack([jnp.sum(hidden_one * hidden_one), jnp.sum(hidden_two * hidden_two), jnp.sum(rgb_image * rgb_image)])
        image_outs = ((hidden_two[0] * keep_flag).astype(jnp.bfloat16), rgb_image[0] * keep_flag, grad_sets[1][0], grad_sets[2][0], grad_sets[3][0])
        return ((totals, squares), image_outs)
    start_state = (jax.tree.map(jnp.zeros_like, weights), jnp.zeros((3,), jnp.float32))
    (totals, squares), stacked = lax.scan(one_image, start_state, (features_in, rgb_in, latent, noise_one, noise_two, grad_features, grad_rgb, valid_mask))
    real_images = jnp.sum(valid_mask)
    entries = jnp.array([RES * RES * C, RES * RES * C, 3 * RES * RES], jnp.float32)
    rms_values = jnp.sqrt(squares / (real_images * entries))
    return (stacked[0], stacked[1], stacked[2], stacked[3], stacked[4], totals[0], totals[1], totals[2], totals[3], totals[4], totals[5], totals[6], totals[7], totals[8], totals[9], totals[10], totals[11], totals[12], rms_values)
```

```python
import jax
import jax.numpy as jnp
from jax import lax
from jax.sharding import Mesh, PartitionSpec as P

C = 512
RES = 32
SQRT_TWO = 1.4142135623730951
EPSILON = 1e-08
DP = ("z", "y", "x")
SWAP = [(0, 1), (1, 0)]


def smooth_leaky(values):
    return SQRT_TWO * (0.2 * values + 0.8 * jax.nn.softplus(values))


def leaky_slope(values):
    return SQRT_TWO * (0.2 + 0.8 * jax.nn.sigmoid(values))


def upsample_axis(values, axis_dim):
    length = values.shape[axis_dim]
    widths = [(0, 0)] * values.ndim
    widths[axis_dim] = (1, 1)
    padded = jnp.pad(values, widths)
    previous = lax.slice_in_dim(padded, 0, length, axis=axis_dim)
    following = lax.slice_in_dim(padded, 2, length + 2, axis=axis_dim)
    even_part = 0.25 * previous + 0.75 * values
    odd_part = 0.75 * values + 0.25 * following
    joined = jnp.stack([even_part, odd_part], axis=axis_dim + 1)
    new_shape = list(values.shape)
    new_shape[axis_dim] = 2 * length
    return joined.reshape(new_shape)


def upsample_rgb(values):
    return upsample_axis(upsample_axis(values, 2), 3)


def pick(stacked, index):
    return lax.dynamic_index_in_dim(stacked, index, 0, keepdims=False)


def place(index, own, other):
    return jnp.where(index == 0, jnp.stack([own, other]), jnp.stack([other, own]))


def swap_core(values):
    return lax.ppermute(values, "chan", SWAP)


def join_chan(values, axis):
    other = swap_core(values)
    me = lax.axis_index("chan")
    return jnp.where(
        me == 0,
        jnp.concatenate([values, other], axis=axis),
        jnp.concatenate([other, values], axis=axis),
    )


def shift_by(step, size):
    return [(i, (i + step) % size) for i in range(size)]


def add_halves(parts, axis_name):
    me = lax.axis_index(axis_name)
    got = lax.ppermute(pick(parts, 1 - me).astype(jnp.bfloat16), axis_name, SWAP)
    return pick(parts, me).astype(jnp.float32) + got.astype(jnp.float32)


def scatter_line(parts, axis_name):
    size = lax.axis_size(axis_name)
    if size > 4:
        return lax.psum_scatter(parts.astype(jnp.float32), axis_name, scatter_dimension=0)
    me = lax.axis_index(axis_name)
    total = pick(parts, me).astype(jnp.float32)
    for step in range(1, size):
        target = lax.rem(me + step, size)
        got = lax.ppermute(
            pick(parts, target).astype(jnp.bfloat16), axis_name, shift_by(step, size)
        )
        total = total + got.astype(jnp.float32)
    return total


def gather_line(part, axis_name):
    size = lax.axis_size(axis_name)
    if size > 4:
        return lax.all_gather(part, axis_name, axis=0)
    me = lax.axis_index(axis_name)
    got = [part] + [lax.ppermute(part, axis_name, shift_by(s, size)) for s in range(1, size)]
    stacked = jnp.stack(got)
    order = lax.rem(me - jnp.arange(size) + size, size)
    return jnp.take(stacked, order, axis=0)


def gather_pair(part, axis_name):
    return place(lax.axis_index(axis_name), part, lax.ppermute(part, axis_name, SWAP))


def reduce_kernel(grads):
    rows, cols = grads.shape
    half = cols // 2
    line = lax.axis_size("z")
    outs = []
    for order, block in enumerate((grads[:, :half], grads[:, half:])):
        first, second = ("x", "y") if order == 0 else ("y", "x")
        parts = block.reshape(2, 2, line, rows // (4 * line), half)
        own = add_halves(add_halves(parts, first), second)
        own = scatter_line(own, "z").astype(jnp.bfloat16)
        full = gather_line(own, "z")
        full = gather_pair(gather_pair(full, second), first)
        outs.append(full.reshape(rows, half).astype(jnp.float32))
    return jnp.concatenate(outs, axis=1)


def gather_small(vector):
    stacked = vector[None]
    for axis_name in ("x", "y"):
        got = gather_pair(stacked, axis_name)
        stacked = got.reshape((-1,) + vector.shape)
    got = gather_line(stacked, "z")
    return got.reshape((-1,) + vector.shape)


DIMS = ("NHWC", "HWIO", "NHWC")


def conv(source, kernel, strides=(1, 1), padding=((1, 1), (1, 1)), dilation=(1, 1), dims=DIMS):
    return lax.conv_general_dilated(
        source,
        kernel,
        strides,
        padding,
        lhs_dilation=dilation,
        dimension_numbers=dims,
        preferred_element_type=jnp.float32,
    )


def per_device(
    counts,
    features_in,
    rgb_in,
    latent,
    affine_one,
    affine_bias_one,
    affine_two,
    affine_bias_two,
    affine_three,
    affine_bias_three,
    kernel_one,
    bias_one,
    kernel_two,
    bias_two,
    rgb_weight,
    rgb_bias,
    noise_gain,
    noise_one,
    noise_two,
    grad_features,
    grad_rgb,
):
    share = features_in.shape[3]
    slots_here = features_in.shape[0]
    chan_count = lax.axis_size("chan")
    me = lax.axis_index("chan")
    own_start = me * share
    other_start = (1 - me) * share
    valid_mask = (jnp.arange(slots_here, dtype=jnp.int32) < counts[0]).astype(jnp.float32)
    keep_four = valid_mask[:, None, None, None]

    def forward_kernel(kernel):
        mine = lax.dynamic_slice_in_dim(kernel, own_start, share, 3)
        theirs = swap_core(lax.dynamic_slice_in_dim(kernel, other_start, share, 3))
        return jnp.concatenate([mine, theirs], axis=2)

    full_one = forward_kernel(kernel_one)
    full_two = forward_kernel(kernel_two)
    style_one = jnp.dot(latent, affine_one, preferred_element_type=jnp.float32) + affine_bias_one
    style_two = jnp.dot(latent, affine_two, preferred_element_type=jnp.float32) + affine_bias_two
    style_three = (
        jnp.dot(latent, affine_three, preferred_element_type=jnp.float32) + affine_bias_three
    )
    squares_one = jnp.sum(jnp.square(kernel_one.astype(jnp.float32)), axis=(0, 1))
    squares_two = jnp.sum(jnp.square(kernel_two.astype(jnp.float32)), axis=(0, 1))
    demod_parts = jnp.stack(
        [
            jnp.dot(style_one * style_one, squares_one, precision=lax.Precision.HIGHEST),
            jnp.dot(style_two * style_two, squares_two, precision=lax.Precision.HIGHEST),
        ]
    )
    demod_sums = lax.dynamic_slice_in_dim(demod_parts + swap_core(demod_parts), own_start, share, 2)
    demod_one, demod_two = lax.rsqrt(demod_sums + EPSILON)

    input_values = features_in.astype(jnp.float32)
    scaled_one = (input_values * style_one[:, None, None, :]).astype(jnp.bfloat16)
    scaled_one_all = jnp.concatenate([scaled_one, swap_core(scaled_one)], axis=3)
    conv_one = conv(scaled_one_all, full_one, padding=((1, 2), (1, 2)), dilation=(2, 2))
    pre_one = (
        conv_one * demod_one[:, None, None, :] + noise_gain[0] * noise_one[..., None] + bias_one
    )
    act_one = smooth_leaky(pre_one)
    scaled_two = (act_one * style_two[:, None, None, :]).astype(jnp.bfloat16)
    scaled_two_all = jnp.concatenate([scaled_two, swap_core(scaled_two)], axis=3)
    conv_two = conv(scaled_two_all, full_two)
    pre_two = (
        conv_two * demod_two[:, None, None, :] + noise_gain[1] * noise_two[..., None] + bias_two
    )
    act_two = smooth_leaky(pre_two)
    features_out = (act_two * keep_four).astype(jnp.bfloat16)
    to_rgb = (act_two * style_three[:, None, None, :]).astype(jnp.bfloat16)
    rgb_part = jnp.einsum("bhwi,ki->bkhw", to_rgb, rgb_weight, preferred_element_type=jnp.float32)
    rgb_linear = rgb_part + swap_core(rgb_part)
    rgb_out = (upsample_rgb(rgb_in) + rgb_linear + rgb_bias[None, :, None, None]) * keep_four
    local_squares = jnp.stack(
        [
            jnp.sum(act_one * act_one * keep_four),
            jnp.sum(act_two * act_two * keep_four),
            jnp.sum(rgb_out * rgb_out) / chan_count,
            counts[0].astype(jnp.float32) / chan_count,
        ]
    )

    grad_colour = (grad_rgb.astype(jnp.float32) * keep_four).astype(jnp.bfloat16)
    grad_rgb_weight = jnp.einsum(
        "bhwi,bkhw->ki", to_rgb, grad_colour, preferred_element_type=jnp.float32
    )
    grad_rgb_bias = jnp.sum(grad_colour.astype(jnp.float32), axis=(0, 2, 3))
    grad_to_rgb = jnp.einsum(
        "bkhw,ki->bhwi", grad_colour, rgb_weight, preferred_element_type=jnp.float32
    )
    upsample_pull = jax.vjp(upsample_rgb, rgb_in)[1]
    grad_rgb_in = upsample_pull(grad_colour.astype(jnp.float32))[0]
    grad_act_two = (
        grad_features.astype(jnp.float32) * keep_four + grad_to_rgb * style_three[:, None, None, :]
    )
    grad_style_three = jnp.sum(grad_to_rgb * act_two, axis=(1, 2))

    def points_back(grad_act, pre, noise_map, conv_out, demod):
        grad_pre = grad_act * leaky_slope(pre)
        grad_bias = jnp.sum(grad_pre, axis=(0, 1, 2))
        gain_part = jnp.sum(grad_pre * noise_map[..., None])
        grad_conv = (grad_pre * demod[:, None, None, :]).astype(jnp.bfloat16)
        grad_square = jnp.sum(grad_pre * conv_out, axis=(1, 2)) * -0.5 * demod**3
        return grad_conv, grad_bias, gain_part, join_chan(grad_square, 1)

    grad_conv_two, grad_bias_two, gain_two, grad_square_two = points_back(
        grad_act_two, pre_two, noise_two, conv_two, demod_two
    )
    grad_conv_two = join_chan(grad_conv_two, 3)
    grad_kernel_two = conv(scaled_two, grad_conv_two, dims=("CHWN", "IHWO", "HWNC"))
    grad_kernel_two = grad_kernel_two + 2.0 * kernel_two.astype(jnp.float32) * jnp.dot(
        (style_two * style_two).T, grad_square_two, precision=lax.Precision.HIGHEST
    )
    grad_scaled_two = conv(
        grad_conv_two, jnp.flip(kernel_two, (0, 1)), dims=("NHWC", "HWOI", "NHWC")
    )
    grad_style_two = jnp.sum(grad_scaled_two * act_one, axis=(1, 2)) + 2.0 * style_two * jnp.dot(
        grad_square_two, squares_two.T, precision=lax.Precision.HIGHEST
    )
    grad_act_one = grad_scaled_two * style_two[:, None, None, :]
    grad_conv_one, grad_bias_one, gain_one, grad_square_one = points_back(
        grad_act_one, pre_one, noise_one, conv_one, demod_one
    )
    grad_conv_one = join_chan(grad_conv_one, 3)
    grad_kernel_one = conv(
        scaled_one,
        grad_conv_one,
        padding=((1, 2), (1, 2)),
        dilation=(2, 2),
        dims=("CHWN", "IHWO", "HWNC"),
    )
    grad_kernel_one = grad_kernel_one + 2.0 * kernel_one.astype(jnp.float32) * jnp.dot(
        (style_one * style_one).T, grad_square_one, precision=lax.Precision.HIGHEST
    )
    grad_scaled_one = conv(
        grad_conv_one,
        jnp.flip(kernel_one, (0, 1)),
        strides=(2, 2),
        padding=((1, 0), (1, 0)),
        dims=("NHWC", "HWOI", "NHWC"),
    )
    grad_style_one = jnp.sum(
        grad_scaled_one * input_values, axis=(1, 2)
    ) + 2.0 * style_one * jnp.dot(grad_square_one, squares_one.T, precision=lax.Precision.HIGHEST)
    grad_features_in = grad_scaled_one * style_one[:, None, None, :]

    shape = kernel_two.shape
    sum_two = reduce_kernel(grad_kernel_two.reshape(-1, shape[3])).reshape(shape)
    sum_one = reduce_kernel(grad_kernel_one.reshape(-1, shape[3])).reshape(shape)

    latent_values = latent.astype(jnp.float32)
    latent_part = (
        jnp.dot(grad_style_one, affine_one.astype(jnp.float32).T, precision=lax.Precision.HIGHEST)
        + jnp.dot(grad_style_two, affine_two.astype(jnp.float32).T, precision=lax.Precision.HIGHEST)
        + jnp.dot(
            grad_style_three, affine_three.astype(jnp.float32).T, precision=lax.Precision.HIGHEST
        )
    )
    crossing = jnp.concatenate(
        [latent_part.reshape(-1), local_squares, jnp.stack([gain_one, gain_two])]
    )
    crossing = crossing + swap_core(crossing)
    grad_latent = crossing[: latent_part.size].reshape(latent_part.shape)
    pieces = [
        latent_values,
        grad_style_one,
        grad_style_two,
        grad_style_three,
        grad_bias_one,
        grad_bias_two,
        grad_rgb_weight,
        grad_rgb_bias,
        crossing[latent_part.size :],
    ]
    flat = jnp.concatenate([member.reshape(-1) for member in pieces])
    flat = jnp.pad(flat, (0, -flat.size % 1024))
    gathered = gather_small(flat.reshape(-1, 128)).reshape(-1, flat.size)
    split, offset = [], 0
    for member in pieces:
        block = gathered[:, offset : offset + member.size]
        split.append(block.reshape((-1,) + member.shape))
        offset += member.size
    latent_all = split[0].reshape(-1, latent.shape[1])
    affine_grads = []
    for block in split[1:4]:
        rows = block.reshape(-1, share)
        affine_grads.append(jnp.dot(latent_all.T, rows, precision=lax.Precision.HIGHEST))
        affine_grads.append(jnp.sum(rows, axis=0))
    totals = [jnp.sum(block, axis=0) for block in split[4:]]
    squares, images, gains = totals[4][:3], totals[4][3], totals[4][4:]
    entries = jnp.array([RES * RES * C, RES * RES * C, 3 * RES * RES], jnp.float32)
    rms_values = jnp.sqrt(squares / (images * entries))
    return (
        features_out,
        rgb_out,
        grad_features_in,
        grad_rgb_in,
        grad_latent,
        *affine_grads,
        sum_one,
        totals[0],
        sum_two,
        totals[1],
        totals[2],
        totals[3],
        gains,
        rms_values,
    )


def solution(mesh):
    count = mesh.shape["dp"]
    wide = 2 if count % 2 == 0 else 1
    tall = 2 if count % 4 == 0 else 1
    grid = mesh.devices.reshape(count // (wide * tall), tall, wide, mesh.shape["chan"])
    split_mesh = Mesh(grid, DP + ("chan",))
    in_specs = (
        P(DP),
        P(DP, None, None, "chan"),
        P(DP, None, None, None),
        P(DP, None),
        P(None, "chan"),
        P("chan"),
        P(None, "chan"),
        P("chan"),
        P(None, "chan"),
        P("chan"),
        P(None, None, "chan", None),
        P("chan"),
        P(None, None, "chan", None),
        P("chan"),
        P(None, "chan"),
        P(),
        P(),
        P(DP, None, None),
        P(DP, None, None),
        P(DP, None, None, "chan"),
        P(DP, None, None, None),
    )
    out_specs = (
        P(DP, None, None, "chan"),
        P(DP, None, None, None),
        P(DP, None, None, "chan"),
        P(DP, None, None, None),
        P(DP, None),
        P(None, "chan"),
        P("chan"),
        P(None, "chan"),
        P("chan"),
        P(None, "chan"),
        P("chan"),
        P(None, None, "chan", None),
        P("chan"),
        P(None, None, "chan", None),
        P("chan"),
        P(None, "chan"),
        P(),
        P(),
        P(),
    )
    return jax.shard_map(
        per_device, mesh=split_mesh, in_specs=in_specs, out_specs=out_specs, check_vma=False
    )
```

```python
import functools

import jax
import jax.numpy as jnp
from jax import lax
from jax.experimental import pallas as pl
from jax.experimental.pallas import tpu as pltpu
from jax.sharding import Mesh, PartitionSpec as P

RES = 32
HALF = 16
PLANE = HALF * HALF
SQRT_TWO = 1.4142135623730951
EPSILON = 1e-08
DP = ("z", "y", "x")
SWAP = [(0, 1), (1, 0)]
F32 = jnp.float32
BF16 = jnp.bfloat16
VMEM_BYTES = 16 * 2**20
VMEM = pl.BlockSpec(memory_space=pltpu.VMEM)
SMEM = pl.BlockSpec(memory_space=pltpu.SMEM)
UP_TAPS = (((0, 1),), ((0, 0), (1, 2)))


def dot(left, right, left_dim, right_dim):
    return lax.dot_general(
        left, right, (((left_dim,), (right_dim,)), ((), ())), preferred_element_type=F32
    )


def source(parity, tap):
    return (parity + tap - 1) & 1, (parity + tap - 1) >> 1


def rows_from(values, shift):
    if shift == 0:
        return values
    blank = jnp.zeros((HALF, values.shape[1]), values.dtype)
    if shift == 1:
        return jnp.concatenate([values[HALF:], blank], 0)
    return jnp.concatenate([blank, values[:-HALF]], 0)


def columns_from(values, shift):
    if shift == 0:
        return values
    moved = pltpu.roll(values, (-shift) % values.shape[0], 0)
    column = lax.broadcasted_iota(jnp.int32, values.shape, 0) % HALF
    return jnp.where(column == (HALF - 1 if shift == 1 else 0), 0.0, moved)


def gather_terms(terms):
    total = None
    for shift, group in terms.items():
        part = None
        for left, right, right_dim in group:
            product = dot(left, right, 1, right_dim)
            part = product if part is None else part + product
        part = columns_from(part, shift)
        total = part if total is None else total + part
    return total


def split_three(values):
    high = values.astype(BF16)
    rest = values - high.astype(F32)
    middle = rest.astype(BF16)
    low = (rest - middle.astype(F32)).astype(BF16)
    return high, middle, low


def style_kernel(latent, a1, b1, a2, b2, a3, b3, features, styles, scaled):
    for index, (affine, bias) in enumerate(((a1, b1), (a2, b2), (a3, b3))):
        styles[index] = dot(latent[...], affine[...], 1, 0) + bias[...]
    for image in range(features.shape[0]):
        row = styles[0, image : image + 1, :]
        scaled[image] = (features[image].astype(F32) * row).astype(BF16)


def pixel_planes(rasters):
    count = len(rasters)
    stacked = jnp.concatenate(rasters, 0)
    lane = lax.broadcasted_iota(jnp.int32, (RES, PLANE), 1)
    line = lax.broadcasted_iota(jnp.int32, (RES, PLANE), 0)
    found = [[None] * 4 for _ in range(count)]
    for qx in range(2):
        choose = jnp.where(line == 2 * (lane % HALF) + qx, 1.0, 0.0).astype(BF16)
        spread_out = dot(stacked, choose, 1, 0)
        for qy in range(2):
            mask = jnp.where(line == 2 * (lane // HALF) + qy, 1.0, 0.0)
            for index in range(count):
                block = spread_out[RES * index : RES * (index + 1)]
                found[index][2 * qy + qx] = jnp.sum(block * mask, axis=0, keepdims=True)
    return found


def planes_kernel(counts, gain, noise_one, noise_two, grad_rgb, planes_one, planes_two, colours):
    images = noise_one.shape[0]
    ones = jnp.ones((3, PLANE), F32)
    blank = jnp.zeros((7, PLANE), F32)
    for image in range(images):
        rasters = []
        for index, noise in enumerate((noise_one, noise_two)):
            value = noise[image]
            rasters += list(split_three(value)) + list(split_three(value * gain[index]))
        valid = jnp.where(image < counts[0], 1.0, 0.0)
        for colour in range(3):
            rasters.append((grad_rgb[image, colour].astype(F32) * valid).astype(BF16))
        found = pixel_planes(rasters)
        for plane in range(4):
            rows = [member[plane] for member in found]
            planes_one[image, plane] = jnp.concatenate(rows[:6] + [ones, blank], 0).astype(BF16)
            planes_two[image, plane] = jnp.concatenate(rows[6:12] + [ones, blank], 0).astype(BF16)
            colours[image, plane] = jnp.concatenate(rows[12:] * 3 + [blank], 0).astype(BF16)


def squares_kernel(
    place, styles, kernel, bias, rgb, squares, mine, theirs, add, colour, parts, *, layer
):
    total = None
    for tap in range(kernel.shape[0]):
        value = kernel[tap].astype(F32)
        total = value * value if total is None else total + value * value
    squares[...] = total
    style = styles[layer]
    parts[...] = lax.dot_general(
        style * style,
        total,
        (((1,), (0,)), ((), ())),
        precision=lax.Precision.HIGHEST,
        preferred_element_type=F32,
    )
    share = bias.shape[1]
    mine[...] = parts[:, pl.ds(pl.multiple_of(place[2] * share, share), share)]
    theirs[...] = parts[:, pl.ds(pl.multiple_of((1 - place[2]) * share, share), share)]
    add[...] = jnp.concatenate(
        [jnp.zeros((3, share), F32), jnp.full((3, share), 0.5, F32)]
        + [part.astype(F32) for part in split_three(0.5 * bias[...])]
        + [jnp.zeros((7, share), F32)],
        0,
    ).astype(BF16)
    for image in range(styles.shape[1]):
        weight = rgb[...].astype(F32) * styles[2, image : image + 1, :]
        colour[image] = jnp.concatenate(
            [part.astype(F32) for part in split_three(weight)] + [jnp.zeros((7, share), F32)], 0
        ).astype(BF16)


def scale_half(rows, add, image, plane, demod, weights):
    return rows * (0.5 * demod) + dot(add[image, plane], weights, 0, 0)


def smooth_leaky(half_pre):
    size = jnp.abs(half_pre)
    soft = jnp.maximum(half_pre, 0.0) * 2.0 + jnp.log(1.0 + jnp.exp(-2.0 * size))
    return (0.4 * SQRT_TWO) * half_pre + (0.8 * SQRT_TWO) * soft


def leaky_slope(half_pre):
    return (0.6 * SQRT_TWO) + (0.4 * SQRT_TWO) * jnp.tanh(half_pre)


def conv_one_kernel(
    place,
    own,
    other,
    k_own,
    k_other,
    sums_own,
    sums_other,
    add,
    weights,
    styles,
    conv,
    scaled,
    demod,
):
    share = own.shape[-1]
    columns = pl.ds(pl.multiple_of(place[2] * share, share), share)
    demod[...] = lax.rsqrt(sums_own[...] + sums_other[...] + EPSILON)
    for qy in range(2):
        for qx in range(2):
            plane = 2 * qy + qx
            terms = {}
            for shift_y, tap_y in UP_TAPS[qy]:
                for shift_x, tap_x in UP_TAPS[qx]:
                    tap = 3 * tap_y + tap_x
                    for source_ref, right in (
                        (own, k_own[tap, :, columns]),
                        (other, k_other[tap]),
                    ):
                        left = jnp.concatenate(
                            [rows_from(source_ref[b], shift_y) for b in range(own.shape[0])], 0
                        )
                        terms.setdefault(shift_x, []).append((left, right, 0))
            total = gather_terms(terms)
            for image in range(own.shape[0]):
                rows = total[image * PLANE : (image + 1) * PLANE]
                conv[image, plane] = rows
                half_pre = scale_half(
                    rows, add, image, plane, demod[image : image + 1, :], weights[...]
                )
                act = smooth_leaky(half_pre)
                scaled[image, plane] = (act * styles[1, image : image + 1, :]).astype(BF16)


def spread(raster, image, wide):
    for block in range(wide.shape[0]):
        lanes = raster[image, :, :, block * 128 : (block + 1) * 128]
        wide[block] = lanes.reshape(wide.shape[1:]).astype(F32)


def read_plane(wide, qy, qx):
    cells = [wide[block, :, qy, pl.ds(qx, HALF, stride=2), :] for block in range(wide.shape[0])]
    return jnp.concatenate([cell.reshape(PLANE, 128) for cell in cells], 1)


def write_plane(wide, qy, qx, values):
    for block in range(wide.shape[0]):
        cell = values[:, block * 128 : (block + 1) * 128].reshape(HALF, HALF, 128)
        wide[block, :, qy, pl.ds(qx, HALF, stride=2), :] = cell


def store_raster(wide, out, image):
    for block in range(wide.shape[0]):
        lanes = wide[block].reshape(RES, RES, 128)
        out[image, :, :, block * 128 : (block + 1) * 128] = lanes.astype(out.dtype)


def conv_two_kernel(
    place,
    own,
    other,
    k_own,
    k_other,
    sums_own,
    sums_other,
    valid,
    add,
    weights,
    colours,
    colour_weights,
    cotangent,
    conv,
    grad_conv,
    demod,
    wide,
):
    share = own.shape[-1]
    columns = pl.ds(pl.multiple_of(place[2] * share, share), share)
    demod[...] = lax.rsqrt(sums_own[...] + sums_other[...] + EPSILON)
    for image in range(own.shape[0]):
        spread(cotangent, image, wide)
        for qy in range(2):
            for qx in range(2):
                plane = 2 * qy + qx
                terms = {}
                for tap_x in range(3):
                    px, shift_x = source(qx, tap_x)
                    for tap_y in range(3):
                        py, shift_y = source(qy, tap_y)
                        tap = 3 * tap_y + tap_x
                        for source_ref, right in (
                            (own, k_own[tap, :, columns]),
                            (other, k_other[tap]),
                        ):
                            left = rows_from(source_ref[image, 2 * py + px], shift_y)
                            terms.setdefault(shift_x, []).append((left, right, 0))
                rows = gather_terms(terms)
                conv[image, plane] = rows
                half_pre = scale_half(
                    rows, add, image, plane, demod[image : image + 1, :], weights[...]
                )
                grad = read_plane(wide, qy, qx) + dot(colours[image, plane], colour_weights[image], 0, 0)
                row = demod[image : image + 1, :] * valid[image : image + 1, :]
                grad = grad * leaky_slope(half_pre) * row
                grad_conv[image, plane] = grad.astype(BF16)


def shifted_copy(source_ref, moved, shift_of):
    for image in range(source_ref.shape[0]):
        for plane in range(source_ref.shape[1]):
            value = columns_from(source_ref[image, plane].astype(F32), shift_of(plane))
            moved[image, plane] = value.astype(BF16)


def kernel_two_grad(place, scaled, g_own, g_other, s_own, k_own, s_other, k_other, moved):
    half = scaled.shape[3] // 2
    shifted_copy(scaled, moved, lambda plane: 1 if plane % 2 == 0 else -1)
    for tap_y in range(3):
        for tap_x in range(3):
            tap = 3 * tap_y + tap_x
            for axis, grads, send, keep in ((0, g_own, s_own, k_own), (1, g_other, s_other, k_other)):
                away = pl.multiple_of((1 - place[axis]) * half, half)
                here = pl.multiple_of(place[axis] * half, half)
                left, right = [], []
                for image in range(scaled.shape[0]):
                    for qy in range(2):
                        for qx in range(2):
                            py, shift_y = source(qy, tap_y)
                            px, shift_x = source(qx, tap_x)
                            ref = scaled if shift_x == 0 else moved
                            value = jnp.concatenate(
                                [
                                    ref[image, 2 * py + px, :, pl.ds(away, half)],
                                    ref[image, 2 * py + px, :, pl.ds(here, half)],
                                ],
                                1,
                            )
                            left.append(rows_from(value, shift_y))
                            right.append(grads[image, 2 * qy + qx])
                total = dot(jnp.concatenate(left, 0), jnp.concatenate(right, 0), 0, 0)
                send[tap] = total[:half].astype(BF16)
                keep[tap] = total[half:]


def kernel_one_grad(place, scaled, g_own, g_other, s_own, k_own, s_other, k_other, moved):
    half = scaled.shape[2] // 2
    for image in range(scaled.shape[0]):
        moved[image] = columns_from(scaled[image].astype(F32), 1).astype(BF16)
    for qy in range(2):
        for qx in range(2):
            for shift_y, tap_y in UP_TAPS[qy]:
                for shift_x, tap_x in UP_TAPS[qx]:
                    tap = 3 * tap_y + tap_x
                    ref = moved if shift_x else scaled
                    for axis, grads, send, keep in (
                        (0, g_own, s_own, k_own),
                        (1, g_other, s_other, k_other),
                    ):
                        away = pl.multiple_of((1 - place[axis]) * half, half)
                        here = pl.multiple_of(place[axis] * half, half)
                        left, right = [], []
                        for image in range(scaled.shape[0]):
                            value = jnp.concatenate(
                                [ref[image, :, pl.ds(away, half)], ref[image, :, pl.ds(here, half)]],
                                1,
                            )
                            left.append(rows_from(value, shift_y))
                            right.append(grads[image, 2 * qy + qx])
                        total = dot(jnp.concatenate(left, 0), jnp.concatenate(right, 0), 0, 0)
                        send[tap] = total[:half].astype(BF16)
                        keep[tap] = total[half:]


def input_two_grad(
    place,
    g_own,
    g_other,
    kernel,
    conv,
    demod,
    add,
    weights,
    styles,
    grad_scaled,
    grad_conv,
):
    share = g_own.shape[3]
    mine = pl.multiple_of(place[2] * share, share)
    theirs = pl.multiple_of((1 - place[2]) * share, share)
    for image in range(g_own.shape[0]):
        for py in range(2):
            for px in range(2):
                plane = 2 * py + px
                terms = {}
                for tap_x in range(3):
                    qx = (px - tap_x + 1) & 1
                    shift_x = source(qx, tap_x)[1]
                    for tap_y in range(3):
                        qy = (py - tap_y + 1) & 1
                        shift_y = source(qy, tap_y)[1]
                        tap = 3 * tap_y + tap_x
                        for grads, start in ((g_own, mine), (g_other, theirs)):
                            left = rows_from(grads[image, 2 * qy + qx], -shift_y)
                            right = kernel[tap, :, pl.ds(start, share)]
                            terms.setdefault(-shift_x, []).append((left, right, 1))
                rows = gather_terms(terms)
                grad_scaled[image, plane] = rows
                half_pre = scale_half(
                    conv[image, plane],
                    add,
                    image,
                    plane,
                    demod[image : image + 1, :],
                    weights[...],
                )
                row = demod[image : image + 1, :] * styles[1, image : image + 1, :]
                grad = rows * leaky_slope(half_pre) * row
                grad_conv[image, plane] = grad.astype(BF16)


def input_one_grad(
    place, g_own, g_other, kernel, features, styles, grad_features, sums
):
    share = g_own.shape[3]
    mine = pl.multiple_of(place[2] * share, share)
    theirs = pl.multiple_of((1 - place[2]) * share, share)
    images = g_own.shape[0]
    terms = {}
    for qy in range(2):
        for qx in range(2):
            for shift_y, tap_y in UP_TAPS[qy]:
                for shift_x, tap_x in UP_TAPS[qx]:
                    tap = 3 * tap_y + tap_x
                    for grads, start in ((g_own, mine), (g_other, theirs)):
                        left = jnp.concatenate(
                            [rows_from(grads[b, 2 * qy + qx], -shift_y) for b in range(images)], 0
                        )
                        right = kernel[tap, :, pl.ds(start, share)]
                        terms.setdefault(-shift_x, []).append((left, right, 1))
    total = gather_terms(terms)
    for image in range(images):
        rows = total[image * PLANE : (image + 1) * PLANE]
        grad_features[image] = rows * styles[0, image : image + 1, :]
        product = rows * features[image].astype(F32)
        sums[image : image + 1, :] = jnp.sum(product, axis=0, keepdims=True)


def noise_rows(add, image, plane, share):
    pick = lax.broadcasted_iota(jnp.int32, (add.shape[2], share), 0) < 3
    return dot(add[image, plane], jnp.where(pick, 1.0, 0.0).astype(BF16), 0, 0)


def column_sum(values):
    return jnp.sum(values, axis=0, keepdims=True)


def point_sums(image, totals, out):
    for row, total in enumerate(totals):
        out[image, row : row + 1, :] = total
    out[image, len(totals) :, :] = jnp.zeros((8 - len(totals), out.shape[2]), F32)


def outputs_two_kernel(
    conv,
    demod,
    valid,
    add,
    weights,
    colours,
    cotangent,
    styles,
    rgb,
    features_out,
    rgb_rows,
    rgb_grad,
    sums,
    wide,
):
    share = conv.shape[3]
    grad_weight = None
    for image in range(conv.shape[0]):
        spread(cotangent, image, wide)
        totals = None
        for plane in range(4):
            qy, qx = plane // 2, plane % 2
            rows = conv[image, plane]
            half_pre = scale_half(rows, add, image, plane, demod[image : image + 1, :], weights[...])
            act = smooth_leaky(half_pre)
            style = styles[2, image : image + 1, :]
            keep = valid[image : image + 1, :]
            from_rgb = dot(colours[image, plane], rgb[...], 0, 0)
            grad = (read_plane(wide, qy, qx) + from_rgb * style) * keep * leaky_slope(half_pre)
            write_plane(wide, qy, qx, act * keep)
            to_rgb = (act * style).astype(BF16)
            rgb_rows[image, plane] = dot(rgb[...], to_rgb, 1, 1)[:8]
            product = dot(colours[image, plane], to_rgb, 1, 0)
            grad_weight = product if grad_weight is None else grad_weight + product
            own = [
                column_sum(grad),
                column_sum(grad * noise_rows(add, image, plane, share)),
                column_sum(grad * rows),
                column_sum(from_rgb * act),
                column_sum(act * act) * keep,
            ]
            totals = own if totals is None else [a + b for a, b in zip(totals, own)]
        store_raster(wide, features_out, image)
        point_sums(image, totals, sums)
    rgb_grad[...] = grad_weight


def outputs_one_kernel(
    conv, grad_scaled, demod, valid, add, weights, styles, sums
):
    share = conv.shape[3]
    for image in range(conv.shape[0]):
        totals = None
        for plane in range(4):
            rows = conv[image, plane]
            half_pre = scale_half(rows, add, image, plane, demod[image : image + 1, :], weights[...])
            act = smooth_leaky(half_pre)
            back = grad_scaled[image, plane]
            grad = back * styles[1, image : image + 1, :] * leaky_slope(half_pre)
            own = [
                column_sum(grad),
                column_sum(grad * noise_rows(add, image, plane, share)),
                column_sum(grad * rows),
                column_sum(back * act),
                column_sum(act * act) * valid[image : image + 1, :],
            ]
            totals = own if totals is None else [a + b for a, b in zip(totals, own)]
        point_sums(image, totals, sums)


def exact(left, right, left_dim, right_dim):
    return lax.dot_general(
        left,
        right,
        (((left_dim,), (right_dim,)), ((), ())),
        precision=lax.Precision.HIGHEST,
        preferred_element_type=F32,
    )


def upsampling(rows, cols):
    line = lax.broadcasted_iota(jnp.int32, (rows, cols), 0)
    column = lax.broadcasted_iota(jnp.int32, (rows, cols), 1)
    centre, near = line // 2, line // 2 + 2 * (line % 2) - 1
    return jnp.where(column == centre, 0.75, 0.0) + jnp.where(column == near, 0.25, 0.0)


def rgb_kernel(counts, bias, own, other, rgb_in, grad_rgb, rgb_out, grad_in, sums, raster):
    images = rgb_in.shape[0]
    double = upsampling(RES, HALF)
    lane = lax.broadcasted_iota(jnp.int32, (HALF, PLANE), 1)
    line = lax.broadcasted_iota(jnp.int32, (HALF, PLANE), 0)
    mask = jnp.where(lane // HALF == line, 1.0, 0.0)
    for qx in range(2):
        pixel = lax.broadcasted_iota(jnp.int32, (PLANE, 128), 0) % HALF
        column = lax.broadcasted_iota(jnp.int32, (PLANE, 128), 1)
        choose = jnp.where(column == 2 * pixel + qx, 1.0, 0.0)
        for qy in range(2):
            plane = 2 * qy + qx
            rows = []
            for image in range(images):
                both = own[image, plane] + other[image, plane]
                rows += [mask * both[colour : colour + 1] for colour in range(3)]
            found = exact(jnp.concatenate(rows, 0), choose, 1, 0)
            for index in range(3 * images):
                cell = found[HALF * index : HALF * (index + 1)]
                place = (index, pl.ds(qy, HALF, stride=2), slice(None))
                raster[place] = cell if qx == 0 else raster[place] + cell
    squares = jnp.zeros((1, 1), F32)
    biases = [jnp.zeros((1, 1), F32) for _ in range(3)]
    for image in range(images):
        keep = jnp.where(image < counts[0], 1.0, 0.0)
        for colour in range(3):
            skip = exact(exact(double, rgb_in[image, colour], 1, 0), double, 1, 1)
            value = (skip + raster[3 * image + colour, :, :RES] + bias[colour]) * keep
            rgb_out[image, colour] = value
            squares = squares + jnp.sum(value * value, keepdims=True)
            grad = grad_rgb[image, colour].astype(F32) * keep
            grad_in[image, colour] = exact(exact(double, grad, 0, 0), double, 1, 0)
            biases[colour] = biases[colour] + jnp.sum(grad, keepdims=True)
    sums[...] = jnp.concatenate(
        [jnp.broadcast_to(member, (1, 128)) for member in [squares] + biases]
        + [jnp.zeros((4, 128), F32)],
        0,
    )


def square_grads_kernel(sums_one, sums_two, demod_one, demod_two, out):
    rows = []
    for sums, demod in ((sums_one, demod_one), (sums_two, demod_two)):
        for image in range(demod.shape[0]):
            row = demod[image : image + 1, :]
            rows.append(-0.5 * sums[image, 2:3, :] * row * row * row)
    out[...] = jnp.concatenate(rows, 0)


def style_grads_kernel(
    place,
    own,
    other,
    squares_one,
    squares_two,
    styles,
    style_sums,
    sums_one,
    sums_two,
    a1,
    a2,
    a3,
    grads,
    crossing,
):
    images, share = style_sums.shape
    mine, theirs = rows_at(place[2], share), rows_at(1 - place[2], share)
    rows = []
    for layer, (squares, sums) in enumerate(((squares_one, style_sums), (squares_two, None))):
        at = slice(layer * images, (layer + 1) * images)
        back = exact(own[at, :], squares[:, mine], 1, 1) + exact(
            other[at, :], squares[:, theirs], 1, 1
        )
        if sums is None:
            direct = jnp.concatenate([sums_one[b, 3:4, :] for b in range(images)], 0)
        else:
            direct = sums[...]
        rows.append(direct + 2.0 * styles[layer] * back)
    rows.append(jnp.concatenate([sums_two[b, 3:4, :] for b in range(images)], 0))
    grads[...] = jnp.concatenate(rows, 0)
    latent = None
    for row, affine in zip(rows, (a1, a2, a3)):
        part = exact(row, affine[...].astype(F32), 1, 1)
        latent = part if latent is None else latent + part
    lane = lax.broadcasted_iota(jnp.int32, (1, share), 1)
    scalars = jnp.zeros((1, share), F32)
    for index, (sums, row) in enumerate(
        ((sums_one, 4), (sums_two, 4), (sums_one, 1), (sums_two, 1))
    ):
        total = sums[0, row : row + 1, :]
        for image in range(1, images):
            total = total + sums[image, row : row + 1, :]
        scalars = scalars + jnp.where(lane == index, jnp.sum(total, keepdims=True), 0.0)
    pieces = [latent[b : b + 1, h * share : (h + 1) * share] for b in range(images) for h in (0, 1)]
    blank = jnp.zeros((crossing.shape[0] - len(pieces) - 1, share), F32)
    crossing[...] = jnp.concatenate(pieces + [scalars, blank], 0)


def pack_kernel(
    place,
    counts,
    own,
    other,
    square_own,
    square_other,
    grads,
    latent,
    styles,
    sums_one,
    sums_two,
    rgb_grad,
    rgb_sums,
    grad_latent,
    pack,
):
    images, share = latent.shape[0], styles.shape[2]
    total = own[...] + other[...]
    count = 2 * images
    for image in range(images):
        grad_latent[image : image + 1, :] = jnp.concatenate(
            [total[2 * image : 2 * image + 1], total[2 * image + 1 : 2 * image + 2]], 1
        )
    values = latent[...].astype(F32)
    rows = [values[:, :share], values[:, share:], grads[...]]
    rows += [styles[0] * styles[0], styles[1] * styles[1]]
    first = place[2] == 0
    for layer in range(2):
        at = slice(layer * images, (layer + 1) * images)
        mine, theirs = square_own[at, :], square_other[at, :]
        rows += [jnp.where(first, mine, theirs), jnp.where(first, theirs, mine)]
    for sums in (sums_one, sums_two):
        bias = sums[0, 0:1, :]
        for image in range(1, images):
            bias = bias + sums[image, 0:1, :]
        rows.append(bias)
    rows.append(rgb_grad[:3, :])
    lane = lax.broadcasted_iota(jnp.int32, (1, share), 1)
    scalars = total[count : count + 1]
    wide = jnp.concatenate([rgb_sums[...]] * (share // 128), 1)
    for index in range(4):
        scalars = scalars + jnp.where(lane == 4 + index, wide[index : index + 1], 0.0)
    scalars = scalars + jnp.where(lane == 8, counts[0].astype(F32), 0.0)
    rows.append(scalars)
    used = sum(member.shape[0] for member in rows)
    rows.append(jnp.zeros((pack.shape[0] - used, share), F32))
    pack[...] = jnp.concatenate(rows, 0)


def spread_kernel(place, *refs, images, line):
    packs = refs[: 1 if line is None else 3 + line - 1]
    outs = refs[len(packs) :]
    grads, biases, outers, points, rgb_grad, gains, rms, rgb_bias, everything = (
        outs[0:3],
        outs[3:6],
        outs[6:8],
        outs[8:10],
        *outs[10:],
    )
    if line is None:
        everything[...] = packs[0][...]
    else:
        own, along_x, along_y = packs[:3]
        ix, iy, iz = place[0], place[1], place[3]
        near = ((own, None), (along_x, None), (along_y, 0), (along_y, 1))
        for index, (ref, at) in enumerate(near):
            y = iy if index < 2 else 1 - iy
            x = ix if index % 2 == 0 else 1 - ix
            everything[(iz * 2 + y) * 2 + x] = ref[...] if at is None else ref[at]
        for step, ref in enumerate(packs[3:], 1):
            z = lax.rem(iz - step + line, line)
            for index in range(4):
                y = iy if index < 2 else 1 - iy
                x = ix if index % 2 == 0 else 1 - ix
                everything[(z * 2 + y) * 2 + x] = ref[index]
    count = everything.shape[0]

    def rows(start, size):
        return jnp.concatenate([everything[d, start : start + size, :] for d in range(count)], 0)

    latent = jnp.concatenate([rows(0, images), rows(images, images)], 1)
    at = 2 * images
    for layer in range(3):
        grad = rows(at, images)
        grads[layer][...] = exact(latent, grad, 0, 0)
        biases[layer][...] = jnp.sum(grad, axis=0, keepdims=True)
        at += images
    for layer in range(2):
        start = at + 2 * images + 2 * images * layer
        squares = jnp.concatenate([rows(start, images), rows(start + images, images)], 1)
        outers[layer][...] = 2.0 * exact(rows(at + images * layer, images), squares, 0, 0)
    at += 6 * images
    total = everything[0]
    for device in range(1, count):
        total = total + everything[device]
    points[0][...] = total[at : at + 1]
    points[1][...] = total[at + 1 : at + 2]
    rgb_grad[...] = total[at + 2 : at + 5]
    scalars = total[at + 5 : at + 6]
    lane = lax.broadcasted_iota(jnp.int32, scalars.shape, 1)

    def scalar(index):
        return jnp.sum(jnp.where(lane == index, scalars, 0.0))

    share = scalars.shape[1]
    real = jnp.sum(jnp.where(lane == 8, scalars, 0.0), keepdims=True)
    entries = jnp.where(lane == 4, 3.0 * RES * RES, 2.0 * share * RES * RES)
    roots = jnp.sqrt(scalars / (real * entries))

    def root(index):
        return jnp.sum(jnp.where(lane == index, roots, 0.0))

    for index, lane_at in enumerate((0, 1, 4)):
        rms[index] = root(lane_at)
    for index in range(2):
        gains[index] = scalar(2 + index)
    for index in range(3):
        rgb_bias[index] = scalar(5 + index)


def rows_at(index, count):
    return pl.ds(pl.multiple_of(index * count, count), count)


def second_kernel(
    place, keep_own, got_own, keep_other, got_other, s_own, k_own, s_other, k_other
):
    count = s_own.shape[1]
    for axis, keep, got, send, kept in (
        (1, keep_own, got_own, s_own, k_own),
        (0, keep_other, got_other, s_other, k_other),
    ):
        away, here = rows_at(1 - place[axis], count), rows_at(place[axis], count)
        for tap in range(keep.shape[0]):
            total = keep[tap, away, :] + got[tap, away, :].astype(F32)
            send[tap] = total.astype(BF16)
            kept[tap] = keep[tap, here, :] + got[tap, here, :].astype(F32)


def line_kernel(place, keep_own, got_own, keep_other, got_other, *pieces):
    size = len(pieces)
    count = pieces[0].shape[2]
    for order, (keep, got) in enumerate(((keep_own, got_own), (keep_other, got_other))):
        for step, piece in enumerate(pieces):
            rows = rows_at(lax.rem(place[3] + step, size), count)
            for tap in range(keep.shape[0]):
                total = keep[tap, rows, :] + got[tap, rows, :].astype(F32)
                piece[order, tap] = total.astype(piece.dtype)


def total_kernel(own, *rest):
    total = own[...]
    for piece in rest[:-1]:
        total = total + piece[...].astype(F32)
    rest[-1][...] = total.astype(BF16)


def join_line_kernel(place, *refs):
    pieces, outs = refs[:-2], refs[-2:]
    size, count = len(pieces), pieces[0].shape[2]
    for order, out in enumerate(outs):
        for step, piece in enumerate(pieces):
            rows = rows_at(lax.rem(place[3] - step + size, size), count)
            for tap in range(out.shape[0]):
                out[tap, rows, :] = piece[order, tap]


def join_pair_kernel(place, own, got_own, other, got_other, half_own, half_other):
    count = own.shape[1]
    for axis, mine, theirs, out in ((1, own, got_own, half_own), (0, other, got_other, half_other)):
        here, away = rows_at(place[axis], count), rows_at(1 - place[axis], count)
        for tap in range(out.shape[0]):
            out[tap, here, :] = mine[tap]
            out[tap, away, :] = theirs[tap]


def finish_kernel(place, half_own, got_own, half_other, got_other, kernel, outer, out, held, sems):
    half, share = half_own.shape[1], half_own.shape[2]
    taps = kernel.shape[0]
    copies = [pltpu.make_async_copy(held.at[t], out.at[t], sems.at[t]) for t in range(taps)]
    for tap in range(taps):
        for axis, column, parts in (
            (0, place[2], (half_own, got_own)),
            (1, 1 - place[2], (half_other, got_other)),
        ):
            lanes = rows_at(column, share)
            for part, row in zip(parts, (place[axis], 1 - place[axis])):
                rows = rows_at(row, half)
                term = kernel[tap, rows, lanes].astype(F32) * outer[rows, lanes]
                held[tap, rows, lanes] = part[tap].astype(F32) + term
        copies[tap].start()
    for copy in copies:
        copy.wait()


def call(body, outs, scratch=(), smem=0, after=(), hbm=(), scalars=(), plain=(), loose=(), micros=0):
    outs = outs if isinstance(outs, tuple) else (outs,)
    any_space = pl.BlockSpec(memory_space=pl.ANY)

    def run(*operands):
        count = len(operands)
        values = [
            member
            if index < smem or index in loose
            else pltpu.with_memory_space_constraint(member, pltpu.VMEM)
            for index, member in enumerate(operands)
        ]

        def inner(*refs):
            body(*refs[:count], *refs[count + len(after) : -1 - len(scratch)], *refs[len(refs) - len(scratch) :])

        results = pl.pallas_call(
            inner,
            out_shape=tuple(
                member if index in hbm + scalars + plain else pltpu.VMEM(member.shape, member.dtype)
                for index, member in enumerate(outs)
            )
            + (shape(8, 128),),
            in_specs=[SMEM] * smem + [VMEM] * (count - smem) + [any_space] * len(after),
            out_specs=tuple(
                any_space if index in hbm else SMEM if index in scalars else VMEM
                for index in range(len(outs))
            )
            + (any_space,),
            scratch_shapes=scratch,
            compiler_params=pltpu.CompilerParams(vmem_limit_bytes=VMEM_BYTES),
            cost_estimate=pl.CostEstimate(
                flops=2**10 + int(micros * 1.1e9), bytes_accessed=2**10, transcendentals=0
            ),
        )(*values, *after)
        found, token = results[:-1], results[-1]
        return (found if len(found) > 1 else found[0]), token

    return run


def shape(*dims, kind=F32):
    return jax.ShapeDtypeStruct(dims, kind)


def kernel_shapes(taps, rows, cols):
    return (shape(taps, rows, cols, kind=BF16), shape(taps, rows, cols))


def swap(values, axis_name):
    return lax.ppermute(values, axis_name, SWAP)


def part_of(values, axis, index, size):
    return lax.dynamic_slice_in_dim(values, index * size, size, axis)


def place_pair(index, own, other, axis):
    return jnp.where(
        index == 0,
        jnp.concatenate([own, other], axis=axis),
        jnp.concatenate([other, own], axis=axis),
    )


def shift_by(step, size):
    return [(i, (i + step) % size) for i in range(size)]


def along_line(pieces):
    size = lax.axis_size("z")
    return [
        lax.ppermute(piece, "z", shift_by(step, size)) for step, piece in enumerate(pieces, 1)
    ]


class Reduction:
    def __init__(self, place, parts):
        self.place = place
        self.sent_own, self.keep_own, self.sent_other, self.keep_other = parts
        self.got = swap(self.sent_own, "x"), swap(self.sent_other, "y")

    def second(self, token, micros=0):
        taps, rows, cols = self.keep_own.shape
        parts, token = call(
            second_kernel,
            kernel_shapes(taps, rows // 2, cols) * 2,
            smem=1,
            after=(token,),
            micros=micros,
        )(self.place, self.keep_own, self.got[0], self.keep_other, self.got[1])
        sent_own, self.keep_own, sent_other, self.keep_other = parts
        self.got = swap(sent_own, "y"), swap(sent_other, "x")
        return token

    def line(self, token):
        size = lax.axis_size("z")
        taps, rows, cols = self.keep_own.shape
        if size > 4:
            self.quarter = jnp.stack(
                [
                    self.keep_own + self.got[0].astype(F32),
                    self.keep_other + self.got[1].astype(F32),
                ]
            )
            return token
        piece = (2, taps, rows // size, cols)
        parts, token = call(
            line_kernel,
            (shape(*piece),) + (shape(*piece, kind=BF16),) * (size - 1),
            smem=1,
            after=(token,),
        )(self.place, self.keep_own, self.got[0], self.keep_other, self.got[1])
        self.own, self.got = parts[0], along_line(parts[1:])
        return token

    def total(self, token):
        if lax.axis_size("z") > 4:
            piece = lax.psum_scatter(self.quarter, "z", scatter_dimension=2, tiled=True)
            self.quarter = lax.all_gather(piece.astype(BF16), "z", axis=2, tiled=True)
            return token
        self.own, token = call(
            total_kernel, shape(*self.own.shape, kind=BF16), after=(token,)
        )(self.own, *self.got)
        self.got = along_line([self.own] * len(self.got))
        return token

    def join_line(self, token):
        if lax.axis_size("z") > 4:
            self.own = self.quarter[0], self.quarter[1]
        else:
            _, taps, rows, cols = self.own.shape
            quarter = shape(taps, rows * (1 + len(self.got)), cols, kind=BF16)
            self.own, token = call(join_line_kernel, (quarter,) * 2, smem=1, after=(token,))(
                self.place, self.own, *self.got
            )
        self.got = swap(self.own[0], "y"), swap(self.own[1], "x")
        return token

    def join_pair(self, token):
        taps, rows, cols = self.own[0].shape
        half = shape(taps, 2 * rows, cols, kind=BF16)
        self.own, token = call(join_pair_kernel, (half,) * 2, smem=1, after=(token,))(
            self.place, self.own[0], self.got[0], self.own[1], self.got[1]
        )
        self.got = swap(self.own[0], "x"), swap(self.own[1], "y")
        return token

    def finish(self, token, kernel, outer):
        return call(
            finish_kernel,
            shape(*kernel.shape),
            [pltpu.VMEM(kernel.shape, F32), pltpu.SemaphoreType.DMA((kernel.shape[0],))],
            smem=1,
            after=(token,),
            hbm=(0,),
        )(self.place, self.own[0], self.got[0], self.own[1], self.got[1], kernel, outer)


def gather_packs(pack):
    size = lax.axis_size("z")
    along_x = swap(pack, "x")
    pair = jnp.stack([pack, along_x])
    along_y = swap(pair, "y")
    if size <= 4:
        plane = jnp.concatenate([pair, along_y], 0)
        return [pack, along_x, along_y] + along_line([plane] * (size - 1)), size
    pair = place_pair(lax.axis_index("x"), pack[None], along_x[None], 0)
    plane = place_pair(lax.axis_index("y"), pair, swap(pair, "y"), 0)
    return [lax.all_gather(plane, "z", axis=0, tiled=True)], None


def per_device(
    counts,
    features_in,
    rgb_in,
    latent,
    affine_one,
    affine_bias_one,
    affine_two,
    affine_bias_two,
    affine_three,
    affine_bias_three,
    kernel_one,
    bias_one,
    kernel_two,
    bias_two,
    rgb_weight,
    rgb_bias,
    noise_gain,
    noise_one,
    noise_two,
    grad_features,
    grad_rgb,
):
    images, share = features_in.shape[0], features_in.shape[3]
    channels = share * lax.axis_size("chan")
    me = lax.axis_index("chan")
    place = jnp.stack([lax.axis_index(name) for name in ("x", "y", "chan", "z")])
    place = place.astype(jnp.int32)
    valid = (jnp.arange(images, dtype=jnp.int32) < counts[0]).astype(F32)
    valid_rows = jnp.broadcast_to(valid[:, None], (images, share))
    features = features_in.reshape(images, PLANE, share)
    flat_one = kernel_one.reshape(9, share, channels)
    flat_two = kernel_two.reshape(9, share, channels)
    plane_shape = (images, 4, PLANE, share)
    half = share // 2
    wide = pltpu.VMEM((share // 128, HALF, 2, RES, 128), F32)

    send_one = part_of(flat_one, 2, 1 - me, share)
    received_one = swap(send_one, "chan")
    (styles, scaled_one), token = call(
        style_kernel,
        (shape(3, images, share), shape(images, PLANE, share, kind=BF16)),
        after=(send_one,),
        loose=tuple(range(8)),
    )(
        latent,
        affine_one,
        affine_bias_one.reshape(1, -1),
        affine_two,
        affine_bias_two.reshape(1, -1),
        affine_three,
        affine_bias_three.reshape(1, -1),
        features,
    )
    scaled_one_other = swap(scaled_one, "chan")

    def layer_squares(layer, kernel, bias, token):
        (squares, mine, theirs, add, colour), token = call(
            functools.partial(squares_kernel, layer=layer),
            (
                shape(share, channels),
                shape(images, share),
                shape(images, share),
                shape(16, share, kind=BF16),
                shape(images, 16, share, kind=BF16),
            ),
            [pltpu.VMEM((images, channels), F32)],
            smem=1,
            after=(token,),
            loose=(3, 4),
        )(place, styles, kernel, bias.reshape(1, -1), rgb_weight)
        return squares, mine, swap(theirs, "chan"), add, colour, token

    squares_one, mine_one, theirs_one, add_one, _, token = layer_squares(
        0, flat_one, bias_one, token
    )
    (noise_planes_one, noise_planes_two, colours), token = call(
        planes_kernel,
        (shape(images, 4, 16, PLANE, kind=BF16),) * 3,
        smem=2,
        after=(token,),
        loose=(2, 3, 4),
    )(counts, noise_gain, noise_one, noise_two, grad_rgb)
    received_two = swap(part_of(flat_two, 2, 1 - me, share), "chan")
    rgb_rows_in = jnp.pad(rgb_weight, ((0, 13), (0, 0)))

    (conv_one, scaled_two, demod_one), token = call(
        conv_one_kernel,
        (shape(*plane_shape), shape(*plane_shape, kind=BF16), shape(images, share)),
        smem=1,
        after=(token,),
    )(
        place,
        scaled_one,
        scaled_one_other,
        flat_one,
        received_one,
        mine_one,
        theirs_one,
        noise_planes_one,
        add_one,
        styles,
    )
    scaled_two_other = swap(scaled_two, "chan")
    squares_two, mine_two, theirs_two, add_two, colour_weights, token = layer_squares(
        1, flat_two, bias_two, token
    )
    (conv_two, grad_conv_two, demod_two), token = call(
        conv_two_kernel,
        (shape(*plane_shape), shape(*plane_shape, kind=BF16), shape(images, share)),
        [wide],
        smem=1,
        after=(token,),
    )(
        place,
        scaled_two,
        scaled_two_other,
        flat_two,
        received_two,
        mine_two,
        theirs_two,
        valid_rows,
        noise_planes_two,
        add_two,
        colours,
        colour_weights,
        grad_features,
    )
    grad_conv_two_other = swap(grad_conv_two, "chan")
    parts_two, token = call(
        kernel_two_grad,
        kernel_shapes(9, half, share) * 2,
        [pltpu.VMEM(plane_shape, BF16)],
        smem=1,
        after=(token,),
    )(place, scaled_two, grad_conv_two, grad_conv_two_other)
    reduce_two = Reduction(place, parts_two)
    (grad_scaled_two, grad_conv_one), token = call(
        input_two_grad,
        (shape(*plane_shape), shape(*plane_shape, kind=BF16)),
        smem=1,
        after=(token,),
    )(
        place,
        grad_conv_two,
        grad_conv_two_other,
        flat_two,
        conv_one,
        demod_one,
        noise_planes_one,
        add_one,
        styles,
    )
    grad_conv_one_other = swap(grad_conv_one, "chan")
    token = reduce_two.second(token, 60)
    parts_one, token = call(
        kernel_one_grad,
        kernel_shapes(9, half, share) * 2,
        [pltpu.VMEM((images, PLANE, share), BF16)],
        smem=1,
        after=(token,),
    )(place, scaled_one, grad_conv_one, grad_conv_one_other)
    reduce_one = Reduction(place, parts_one)
    token = reduce_two.line(token)
    (features_out, rgb_planes, rgb_grad, sums_two), token = call(
        outputs_two_kernel,
        (
            shape(images, RES, RES, share, kind=BF16),
            shape(images, 4, 8, PLANE),
            shape(16, share),
            shape(images, 8, share),
        ),
        [wide],
        after=(token,),
        plain=(0,),
        loose=(8,),
        micros=60,
    )(
        conv_two,
        demod_two,
        valid_rows,
        noise_planes_two,
        add_two,
        colours,
        grad_features,
        styles,
        rgb_rows_in,
    )
    token = reduce_one.second(token)
    sums_one, token = call(
        outputs_one_kernel, shape(images, 8, share), after=(token,)
    )(
        conv_one,
        grad_scaled_two,
        demod_one,
        valid_rows,
        noise_planes_one,
        add_one,
        styles,
    )
    rgb_planes_other = swap(rgb_planes, "chan")
    square_grads, token = call(
        square_grads_kernel, shape(2 * images, share), after=(token,)
    )(sums_one, sums_two, demod_one, demod_two)
    square_grads_other = swap(square_grads, "chan")
    token = reduce_two.total(token)
    (grad_features_in, style_sums), token = call(
        input_one_grad,
        (shape(images, PLANE, share), shape(images, share)),
        smem=1,
        after=(token,),
        plain=(0,),
    )(place, grad_conv_one, grad_conv_one_other, flat_one, features, styles)
    token = reduce_one.line(token)
    (style_grads, crossing), token = call(
        style_grads_kernel,
        (shape(3 * images, share), shape(-(-(2 * images + 1) // 8) * 8, share)),
        smem=1,
        after=(token,),
    )(
        place,
        square_grads,
        square_grads_other,
        squares_one,
        squares_two,
        styles,
        style_sums,
        sums_one,
        sums_two,
        affine_one,
        affine_two,
        affine_three,
    )
    crossing_other = swap(crossing, "chan")
    (rgb_out, grad_rgb_in, rgb_sums), token = call(
        rgb_kernel,
        (shape(*grad_rgb.shape), shape(*rgb_in.shape), shape(8, 128)),
        [pltpu.VMEM((3 * images, RES, 128), F32)],
        smem=2,
        after=(token,),
        plain=(0, 1),
        loose=(4, 5),
    )(counts, rgb_bias, rgb_planes, rgb_planes_other, rgb_in, grad_rgb)
    (grad_latent, pack), token = call(
        pack_kernel,
        (shape(images, channels), shape(-(-(13 * images + 6) // 8) * 8, share)),
        smem=2,
        after=(token,),
        plain=(0,),
    )(
        place,
        counts,
        crossing,
        crossing_other,
        square_grads,
        square_grads_other,
        style_grads,
        latent,
        styles,
        sums_one,
        sums_two,
        rgb_grad,
        rgb_sums,
    )
    packs, line = gather_packs(pack)
    token = reduce_two.join_line(token)
    token = reduce_one.total(token)
    token = reduce_two.join_pair(token)
    token = reduce_one.join_line(token)
    devices = lax.axis_size("z") * lax.axis_size("y") * lax.axis_size("x")
    spread_out, token = call(
        functools.partial(spread_kernel, images=images, line=line),
        (shape(channels, share),) * 3
        + (shape(1, share),) * 3
        + (shape(share, channels),) * 2
        + (shape(1, share),) * 2
        + (shape(3, share), shape(2), shape(3), shape(3)),
        [pltpu.VMEM((devices,) + pack.shape, F32)],
        smem=1,
        after=(token,),
        scalars=(11, 12, 13),
        plain=(0, 1, 2, 3, 4, 5, 8, 9, 10),
    )(place, *packs)
    affine_grads, affine_biases, outers, points = (
        spread_out[0:3],
        spread_out[3:6],
        spread_out[6:8],
        spread_out[8:10],
    )
    rgb_total, gains, rms_values, rgb_bias_grad = spread_out[10:]
    token = reduce_one.join_pair(token)
    sum_two, token = reduce_two.finish(token, flat_two, outers[1])
    sum_one, token = reduce_one.finish(token, flat_one, outers[0])
    affine_outs = []
    for grad, bias in zip(affine_grads, affine_biases):
        affine_outs += [grad, bias.reshape(-1)]
    return (
        features_out,
        rgb_out,
        grad_features_in.reshape(features_in.shape),
        grad_rgb_in,
        grad_latent,
        *affine_outs,
        sum_one.reshape(kernel_one.shape),
        points[0].reshape(-1),
        sum_two.reshape(kernel_two.shape),
        points[1].reshape(-1),
        rgb_total,
        rgb_bias_grad,
        gains,
        rms_values,
    )


def solution(mesh):
    count = mesh.shape["dp"]
    wide = 2 if count % 2 == 0 else 1
    tall = 2 if count % 4 == 0 else 1
    grid = mesh.devices.reshape(count // (wide * tall), tall, wide, mesh.shape["chan"])
    split_mesh = Mesh(grid, DP + ("chan",))
    in_specs = (
        P(DP),
        P(DP, None, None, "chan"),
        P(DP, None, None, None),
        P(DP, None),
        P(None, "chan"),
        P("chan"),
        P(None, "chan"),
        P("chan"),
        P(None, "chan"),
        P("chan"),
        P(None, None, "chan", None),
        P("chan"),
        P(None, None, "chan", None),
        P("chan"),
        P(None, "chan"),
        P(),
        P(),
        P(DP, None, None),
        P(DP, None, None),
        P(DP, None, None, "chan"),
        P(DP, None, None, None),
    )
    out_specs = (
        P(DP, None, None, "chan"),
        P(DP, None, None, None),
        P(DP, None, None, "chan"),
        P(DP, None, None, None),
        P(DP, None),
        P(None, "chan"),
        P("chan"),
        P(None, "chan"),
        P("chan"),
        P(None, "chan"),
        P("chan"),
        P(None, None, "chan", None),
        P("chan"),
        P(None, None, "chan", None),
        P("chan"),
        P(None, "chan"),
        P(),
        P(),
        P(),
    )
    return jax.shard_map(
        per_device, mesh=split_mesh, in_specs=in_specs, out_specs=out_specs, check_vma=False
    )
```

```python
import functools

import jax
import jax.numpy as jnp
from jax import lax
from jax.experimental import pallas as pl
from jax.experimental.pallas import tpu as pltpu
from jax.sharding import Mesh, PartitionSpec as P

RES = 32
HALF = 16
PLANE = HALF * HALF
SQRT_TWO = 1.4142135623730951
EPSILON = 1e-08
STAGE = 60
DP = ("block", "far", "near", "y", "x")
SWAP = [(0, 1), (1, 0)]
F32 = jnp.float32
BF16 = jnp.bfloat16
VMEM_BYTES = 16 * 2**20
VMEM = pl.BlockSpec(memory_space=pltpu.VMEM)
SMEM = pl.BlockSpec(memory_space=pltpu.SMEM)
UP_TAPS = (((0, 1),), ((0, 0), (1, 2)))


def dot(left, right, left_dim, right_dim):
    return lax.dot_general(
        left, right, (((left_dim,), (right_dim,)), ((), ())), preferred_element_type=F32
    )


def exact(left, right, left_dim, right_dim):
    return lax.dot_general(
        left,
        right,
        (((left_dim,), (right_dim,)), ((), ())),
        precision=lax.Precision.HIGHEST,
        preferred_element_type=F32,
    )


def source(parity, tap):
    return (parity + tap - 1) & 1, (parity + tap - 1) >> 1


def each(count, body):
    lax.fori_loop(0, count, lambda index, carry: (body(index), carry)[1], 0)


def row_of(ref, index):
    return ref[pl.ds(index, 1), :]


def rows_at(index, count):
    return pl.ds(pl.multiple_of(index * count, count), count)


def rows_from(values, shift):
    if shift == 0:
        return values
    blank = jnp.zeros((HALF, values.shape[1]), values.dtype)
    if shift == 1:
        return jnp.concatenate([values[HALF:], blank], 0)
    return jnp.concatenate([blank, values[:-HALF]], 0)


def columns_from(values, shift):
    if shift == 0:
        return values
    moved = pltpu.roll(values, (-shift) % values.shape[0], 0)
    column = lax.broadcasted_iota(jnp.int32, values.shape, 0) % HALF
    return jnp.where(column == (HALF - 1 if shift == 1 else 0), 0.0, moved)


def gather_terms(terms):
    total = None
    for shift, group in terms.items():
        part = None
        for left, right, right_dim in group:
            product = dot(left, right, 1, right_dim)
            part = product if part is None else part + product
        part = columns_from(part, shift)
        total = part if total is None else total + part
    return total


def split_three(values):
    high = values.astype(BF16)
    rest = values - high.astype(F32)
    middle = rest.astype(BF16)
    low = (rest - middle.astype(F32)).astype(BF16)
    return high, middle, low


def fetch(place, kernel, out, sem):
    share = out.shape[2]
    return pltpu.make_async_copy(kernel.at[:, :, rows_at(1 - place[2], share)], out, sem)


def style_kernel(
    place, kernel, latent, a1, b1, a2, b2, a3, b3, features, styles, scaled, send, sem
):
    fetch(place, kernel, send, sem).start()
    for index, (affine, bias) in enumerate(((a1, b1), (a2, b2), (a3, b3))):
        styles[index] = dot(latent[...], affine[...], 1, 0) + bias[...]
    for image in range(features.shape[0]):
        row = styles[0, image : image + 1, :]
        scaled[image] = (features[image].astype(F32) * row).astype(BF16)
    fetch(place, kernel, send, sem).wait()


def pixel_planes(rasters):
    count = len(rasters)
    stacked = jnp.concatenate(rasters, 0)
    lane = lax.broadcasted_iota(jnp.int32, (RES, PLANE), 1)
    line = lax.broadcasted_iota(jnp.int32, (RES, PLANE), 0)
    found = [[None] * 4 for _ in range(count)]
    for qx in range(2):
        choose = jnp.where(line == 2 * (lane % HALF) + qx, 1.0, 0.0).astype(BF16)
        spread_out = dot(stacked, choose, 1, 0)
        for qy in range(2):
            mask = jnp.where(line == 2 * (lane // HALF) + qy, 1.0, 0.0)
            for index in range(count):
                block = spread_out[RES * index : RES * (index + 1)]
                found[index][2 * qy + qx] = jnp.sum(block * mask, axis=0, keepdims=True)
    return found


def planes_kernel(
    place,
    valid,
    gain,
    kernel,
    noise_one,
    noise_two,
    grad_rgb,
    planes_one,
    planes_two,
    colours,
    send,
    sem,
):
    fetch(place, kernel, send, sem).start()
    images = noise_one.shape[0]
    ones = jnp.ones((3, PLANE), F32)
    blank = jnp.zeros((7, PLANE), F32)
    for image in range(images):
        rasters = []
        for index, noise in enumerate((noise_one, noise_two)):
            value = noise[image]
            rasters += list(split_three(value)) + list(split_three(value * gain[:, index : index + 1]))
        keep = valid[image : image + 1, :RES]
        for colour in range(3):
            rasters.append((grad_rgb[image, colour].astype(F32) * keep).astype(BF16))
        found = pixel_planes(rasters)
        for plane in range(4):
            rows = [member[plane] for member in found]
            planes_one[image, plane] = jnp.concatenate(rows[:6] + [ones, blank], 0).astype(BF16)
            planes_two[image, plane] = jnp.concatenate(rows[6:12] + [ones, blank], 0).astype(BF16)
            colours[image, plane] = jnp.concatenate(rows[12:] * 3 + [blank], 0).astype(BF16)
    fetch(place, kernel, send, sem).wait()


def squares_kernel(
    place, styles, kernel, bias, rgb, squares, mine, theirs, add, colour, parts, *, layer
):
    total = None
    for tap in range(kernel.shape[0]):
        value = kernel[tap].astype(F32)
        total = value * value if total is None else total + value * value
    squares[...] = total
    style = styles[layer]
    parts[...] = lax.dot_general(
        style * style,
        total,
        (((1,), (0,)), ((), ())),
        precision=lax.Precision.HIGHEST,
        preferred_element_type=F32,
    )
    share = bias.shape[1]
    mine[...] = parts[:, pl.ds(pl.multiple_of(place[2] * share, share), share)]
    theirs[...] = parts[:, pl.ds(pl.multiple_of((1 - place[2]) * share, share), share)]
    add[...] = jnp.concatenate(
        [jnp.zeros((3, share), F32), jnp.full((3, share), 0.5, F32)]
        + [part.astype(F32) for part in split_three(0.5 * bias[...])]
        + [jnp.zeros((7, share), F32)],
        0,
    ).astype(BF16)
    for image in range(styles.shape[1]):
        weight = rgb[...].astype(F32) * styles[2, image : image + 1, :]
        colour[image] = jnp.concatenate(
            [part.astype(F32) for part in split_three(weight)] + [jnp.zeros((7, share), F32)], 0
        ).astype(BF16)


def scale_half(rows, add, image, plane, demod, weights):
    return rows * (0.5 * demod) + dot(add[image, plane], weights, 0, 0)


def smooth_leaky(half_pre):
    size = jnp.abs(half_pre)
    soft = jnp.maximum(half_pre, 0.0) * 2.0 + jnp.log(1.0 + jnp.exp(-2.0 * size))
    return (0.4 * SQRT_TWO) * half_pre + (0.8 * SQRT_TWO) * soft


def leaky_slope(half_pre):
    return (0.6 * SQRT_TWO) + (0.4 * SQRT_TWO) * jnp.tanh(half_pre)


def column_sum(values):
    return jnp.sum(values, axis=0, keepdims=True)


def square_grad(products, demod):
    return -0.5 * products * demod * demod


def conv_one_kernel(
    place,
    own,
    other,
    k_own,
    k_other,
    sums_own,
    sums_other,
    add,
    weights,
    styles,
    conv,
    scaled,
    demod,
):
    share = own.shape[-1]
    columns = pl.ds(pl.multiple_of(place[2] * share, share), share)
    demod[...] = lax.rsqrt(sums_own[...] + sums_other[...] + EPSILON)
    for qy in range(2):
        for qx in range(2):
            plane = 2 * qy + qx
            terms = {}
            for shift_y, tap_y in UP_TAPS[qy]:
                for shift_x, tap_x in UP_TAPS[qx]:
                    tap = 3 * tap_y + tap_x
                    for source_ref, right in (
                        (own, k_own[tap, :, columns]),
                        (other, k_other[tap]),
                    ):
                        left = jnp.concatenate(
                            [rows_from(source_ref[b], shift_y) for b in range(own.shape[0])], 0
                        )
                        terms.setdefault(shift_x, []).append((left, right, 0))
            total = gather_terms(terms)
            for image in range(own.shape[0]):
                rows = total[image * PLANE : (image + 1) * PLANE]
                conv[image, plane] = rows
                half_pre = scale_half(
                    rows, add, image, plane, demod[image : image + 1, :], weights[...]
                )
                act = smooth_leaky(half_pre)
                scaled[image, plane] = (act * styles[1, image : image + 1, :]).astype(BF16)


def spread(raster, image, wide):
    for block in range(wide.shape[0]):
        lanes = raster[image, :, :, block * 128 : (block + 1) * 128]
        wide[block] = lanes.reshape(wide.shape[1:]).astype(F32)


def read_plane(wide, qy, qx):
    cells = [wide[block, :, qy, pl.ds(qx, HALF, stride=2), :] for block in range(wide.shape[0])]
    return jnp.concatenate([cell.reshape(PLANE, 128) for cell in cells], 1)


def write_plane(wide, qy, qx, values):
    for block in range(wide.shape[0]):
        cell = values[:, block * 128 : (block + 1) * 128].reshape(HALF, HALF, 128)
        wide[block, :, qy, pl.ds(qx, HALF, stride=2), :] = cell


def store_raster(wide, out, image):
    for block in range(wide.shape[0]):
        lanes = wide[block].reshape(RES, RES, 128)
        out[image, :, :, block * 128 : (block + 1) * 128] = lanes.astype(out.dtype)


def conv_two_kernel(
    place,
    own,
    other,
    k_own,
    k_other,
    sums_own,
    sums_other,
    valid,
    add,
    weights,
    colours,
    colour_weights,
    cotangent,
    conv,
    grad_conv,
    demod,
    square,
    wide,
):
    share = own.shape[-1]
    columns = pl.ds(pl.multiple_of(place[2] * share, share), share)
    demod[...] = lax.rsqrt(sums_own[...] + sums_other[...] + EPSILON)

    def one(image):
        spread(cotangent, image, wide)
        products = None
        for qy in range(2):
            for qx in range(2):
                plane = 2 * qy + qx
                terms = {}
                for tap_x in range(3):
                    px, shift_x = source(qx, tap_x)
                    for tap_y in range(3):
                        py, shift_y = source(qy, tap_y)
                        tap = 3 * tap_y + tap_x
                        for source_ref, right in (
                            (own, k_own[tap, :, columns]),
                            (other, k_other[tap]),
                        ):
                            left = rows_from(source_ref[image, 2 * py + px], shift_y)
                            terms.setdefault(shift_x, []).append((left, right, 0))
                rows = gather_terms(terms)
                conv[image, plane] = rows
                half_pre = scale_half(
                    rows, add, image, plane, row_of(demod, image), weights[...]
                )
                grad = read_plane(wide, qy, qx) + dot(colours[image, plane], colour_weights[image], 0, 0)
                row = row_of(demod, image) * row_of(valid, image)
                grad = grad * leaky_slope(half_pre) * row
                grad_conv[image, plane] = grad.astype(BF16)
                product = column_sum(grad * rows)
                products = product if products is None else products + product
        square[pl.ds(image, 1), :] = square_grad(products, row_of(demod, image))

    each(own.shape[0], one)


def add_term(total, place, axis, kernel, tap, column, terms, outs):
    at = tap
    while at >= outs[0].shape[0]:
        at, outs = at - outs[0].shape[0], outs[4:]
    send, keep = outs[2 * axis : 2 * axis + 2]
    half, share = send.shape[1], send.shape[2]
    columns = rows_at(column, share)
    for start, index, out in ((0, 1 - place[axis], send), (half, place[axis], keep)):
        weight = kernel[tap, rows_at(index, half), columns].astype(F32)
        value = total[start : start + half] + weight * terms[start : start + half]
        out[at] = value.astype(out.dtype)


def square_terms(place, axis, squared, grads):
    half = squared.shape[1] // 2
    rows = [squared[:, rows_at(1 - place[axis], half)], squared[:, rows_at(place[axis], half)]]
    return 2.0 * exact(jnp.concatenate(rows, 1), grads[...], 0, 0)


def shifted_kernel(scaled, moved):
    def one(image):
        for plane in range(scaled.shape[1]):
            value = scaled[image, plane].astype(F32)
            moved[image, plane] = columns_from(value, 1 if plane % 2 == 0 else -1).astype(BF16)

    each(scaled.shape[0], one)


def kernel_two_grad(
    place,
    scaled,
    moved,
    g_own,
    g_other,
    kernel,
    styles,
    q_own,
    q_other,
    *refs,
):
    outs, squared = refs[:-1], refs[-1]
    half = scaled.shape[3] // 2
    squared[...] = styles[1] * styles[1]
    for axis, column, grads, squares in (
        (0, place[2], g_own, q_own),
        (1, 1 - place[2], g_other, q_other),
    ):
        terms = square_terms(place, axis, squared, squares)
        lanes = (rows_at(1 - place[axis], half), rows_at(place[axis], half))
        for tap_y in range(3):
            for tap_x in range(3):
                left, right = [], []
                for image in range(scaled.shape[0]):
                    for qy in range(2):
                        for qx in range(2):
                            py, shift_y = source(qy, tap_y)
                            px, shift_x = source(qx, tap_x)
                            ref = scaled if shift_x == 0 else moved
                            value = jnp.concatenate(
                                [ref[image, 2 * py + px, :, at] for at in lanes], 1
                            )
                            left.append(rows_from(value, shift_y))
                            right.append(grads[image, 2 * qy + qx])
                total = dot(jnp.concatenate(left, 0), jnp.concatenate(right, 0), 0, 0)
                tap = 3 * tap_y + tap_x
                add_term(total, place, axis, kernel, tap, column, terms, outs)


def kernel_one_grad(
    place,
    scaled,
    g_own,
    g_other,
    kernel,
    styles,
    q_own,
    q_other,
    *refs,
):
    outs, (moved, squared) = refs[:-2], refs[-2:]
    half = scaled.shape[2] // 2
    images = scaled.shape[0]
    for image in range(images):
        moved[image] = columns_from(scaled[image].astype(F32), 1).astype(BF16)
    squared[...] = styles[0] * styles[0]
    for axis, column, grads, squares in (
        (0, place[2], g_own, q_own),
        (1, 1 - place[2], g_other, q_other),
    ):
        terms = square_terms(place, axis, squared, squares)
        lanes = (rows_at(1 - place[axis], half), rows_at(place[axis], half))
        for qy in range(2):
            for qx in range(2):
                right = jnp.concatenate([grads[b, 2 * qy + qx] for b in range(images)], 0)
                for shift_y, tap_y in UP_TAPS[qy]:
                    for shift_x, tap_x in UP_TAPS[qx]:
                        ref = moved if shift_x else scaled
                        left = [
                            rows_from(jnp.concatenate([ref[b, :, at] for at in lanes], 1), shift_y)
                            for b in range(images)
                        ]
                        total = dot(jnp.concatenate(left, 0), right, 0, 0)
                        tap = 3 * tap_y + tap_x
                        add_term(total, place, axis, kernel, tap, column, terms, outs)


def input_two_grad(
    place,
    g_own,
    g_other,
    kernel,
    conv,
    demod,
    add,
    weights,
    styles,
    grad_scaled,
    grad_conv,
    square,
):
    share = g_own.shape[3]
    mine = pl.multiple_of(place[2] * share, share)
    theirs = pl.multiple_of((1 - place[2]) * share, share)

    def one(image):
        products = None
        for py in range(2):
            for px in range(2):
                plane = 2 * py + px
                terms = {}
                for tap_x in range(3):
                    qx = (px - tap_x + 1) & 1
                    shift_x = source(qx, tap_x)[1]
                    for tap_y in range(3):
                        qy = (py - tap_y + 1) & 1
                        shift_y = source(qy, tap_y)[1]
                        tap = 3 * tap_y + tap_x
                        for grads, start in ((g_own, mine), (g_other, theirs)):
                            left = rows_from(grads[image, 2 * qy + qx], -shift_y)
                            right = kernel[tap, :, pl.ds(start, share)]
                            terms.setdefault(-shift_x, []).append((left, right, 1))
                rows = gather_terms(terms)
                grad_scaled[image, plane] = rows
                values = conv[image, plane]
                half_pre = scale_half(
                    values,
                    add,
                    image,
                    plane,
                    row_of(demod, image),
                    weights[...],
                )
                row = row_of(demod, image) * row_of(styles.at[1], image)
                grad = rows * leaky_slope(half_pre) * row
                grad_conv[image, plane] = grad.astype(BF16)
                product = column_sum(grad * values)
                products = product if products is None else products + product
        square[pl.ds(image, 1), :] = square_grad(products, row_of(demod, image))

    each(g_own.shape[0], one)


def input_one_grad(
    place, g_own, g_other, kernel, features, styles, grad_features, sums
):
    share = g_own.shape[3]
    mine = pl.multiple_of(place[2] * share, share)
    theirs = pl.multiple_of((1 - place[2]) * share, share)
    images = g_own.shape[0]
    terms = {}
    for qy in range(2):
        for qx in range(2):
            for shift_y, tap_y in UP_TAPS[qy]:
                for shift_x, tap_x in UP_TAPS[qx]:
                    tap = 3 * tap_y + tap_x
                    for grads, start in ((g_own, mine), (g_other, theirs)):
                        left = jnp.concatenate(
                            [rows_from(grads[b, 2 * qy + qx], -shift_y) for b in range(images)], 0
                        )
                        right = kernel[tap, :, pl.ds(start, share)]
                        terms.setdefault(-shift_x, []).append((left, right, 1))
    total = gather_terms(terms)
    for image in range(images):
        rows = total[image * PLANE : (image + 1) * PLANE]
        grad_features[image] = rows * styles[0, image : image + 1, :]
        product = rows * features[image].astype(F32)
        sums[image : image + 1, :] = jnp.sum(product, axis=0, keepdims=True)


def noise_rows(add, image, plane, share):
    pick = lax.broadcasted_iota(jnp.int32, (add.shape[2], share), 0) < 3
    return dot(add[image, plane], jnp.where(pick, 1.0, 0.0).astype(BF16), 0, 0)


def point_sums(image, totals, out):
    for row, total in enumerate(totals):
        out[image, row : row + 1, :] = total
    out[image, len(totals) :, :] = jnp.zeros((8 - len(totals), out.shape[2]), F32)


def outputs_two_kernel(
    conv,
    demod,
    valid,
    add,
    weights,
    colours,
    cotangent,
    styles,
    rgb,
    features_out,
    rgb_rows,
    rgb_grad,
    sums,
    wide,
):
    share = conv.shape[3]
    rgb_grad[...] = jnp.zeros_like(rgb_grad)

    def one(image):
        spread(cotangent, image, wide)
        totals = None
        for plane in range(4):
            qy, qx = plane // 2, plane % 2
            rows = conv[image, plane]
            half_pre = scale_half(rows, add, image, plane, row_of(demod, image), weights[...])
            act = smooth_leaky(half_pre)
            style = row_of(styles.at[2], image)
            keep = row_of(valid, image)
            from_rgb = dot(colours[image, plane], rgb[...], 0, 0)
            grad = (read_plane(wide, qy, qx) + from_rgb * style) * keep * leaky_slope(half_pre)
            write_plane(wide, qy, qx, act * keep)
            to_rgb = (act * style).astype(BF16)
            rgb_rows[image, plane] = dot(rgb[...], to_rgb, 1, 1)[:8]
            rgb_grad[...] += dot(colours[image, plane], to_rgb, 1, 0)
            own = [
                column_sum(grad),
                column_sum(grad * noise_rows(add, image, plane, share)),
                column_sum(from_rgb * act),
                column_sum(act * act) * keep,
            ]
            totals = own if totals is None else [a + b for a, b in zip(totals, own)]
        store_raster(wide, features_out, image)
        point_sums(image, totals, sums)

    each(conv.shape[0], one)


def outputs_one_kernel(
    conv, grad_scaled, demod, valid, add, weights, styles, sums
):
    share = conv.shape[3]

    def one(image):
        totals = None
        for plane in range(4):
            rows = conv[image, plane]
            half_pre = scale_half(rows, add, image, plane, row_of(demod, image), weights[...])
            act = smooth_leaky(half_pre)
            back = grad_scaled[image, plane]
            grad = back * row_of(styles.at[1], image) * leaky_slope(half_pre)
            own = [
                column_sum(grad),
                column_sum(grad * noise_rows(add, image, plane, share)),
                column_sum(back * act),
                column_sum(act * act) * row_of(valid, image),
            ]
            totals = own if totals is None else [a + b for a, b in zip(totals, own)]
        point_sums(image, totals, sums)

    each(conv.shape[0], one)


def upsampling(rows, cols):
    line = lax.broadcasted_iota(jnp.int32, (rows, cols), 0)
    column = lax.broadcasted_iota(jnp.int32, (rows, cols), 1)
    centre, near = line // 2, line // 2 + 2 * (line % 2) - 1
    return jnp.where(column == centre, 0.75, 0.0) + jnp.where(column == near, 0.25, 0.0)


def rgb_kernel(valid, bias, own, other, rgb_in, grad_rgb, rgb_out, grad_in, sums, raster):
    images = rgb_in.shape[0]
    double = upsampling(RES, HALF)
    lane = lax.broadcasted_iota(jnp.int32, (HALF, PLANE), 1)
    line = lax.broadcasted_iota(jnp.int32, (HALF, PLANE), 0)
    mask = jnp.where(lane // HALF == line, 1.0, 0.0)
    for qx in range(2):
        pixel = lax.broadcasted_iota(jnp.int32, (PLANE, 128), 0) % HALF
        column = lax.broadcasted_iota(jnp.int32, (PLANE, 128), 1)
        choose = jnp.where(column == 2 * pixel + qx, 1.0, 0.0)
        for qy in range(2):
            plane = 2 * qy + qx
            rows = []
            for image in range(images):
                both = own[image, plane] + other[image, plane]
                rows += [mask * both[colour : colour + 1] for colour in range(3)]
            found = exact(jnp.concatenate(rows, 0), choose, 1, 0)
            for index in range(3 * images):
                cell = found[HALF * index : HALF * (index + 1)]
                place = (index, pl.ds(qy, HALF, stride=2), slice(None))
                raster[place] = cell if qx == 0 else raster[place] + cell
    squares = jnp.zeros((1, 1), F32)
    biases = [jnp.zeros((1, 1), F32) for _ in range(3)]
    for image in range(images):
        keep = valid[image : image + 1, :RES]
        for colour in range(3):
            skip = exact(exact(double, rgb_in[image, colour], 1, 0), double, 1, 1)
            value = (skip + raster[3 * image + colour, :, :RES]) + bias[:, colour : colour + 1]
            value = value * keep
            rgb_out[image, colour] = value
            squares = squares + jnp.sum(value * value, keepdims=True)
            grad = grad_rgb[image, colour].astype(F32) * keep
            grad_in[image, colour] = exact(exact(double, grad, 0, 0), double, 1, 0)
            biases[colour] = biases[colour] + jnp.sum(grad, keepdims=True)
    sums[...] = jnp.concatenate(
        [jnp.broadcast_to(member, (1, 128)) for member in [squares] + biases]
        + [jnp.zeros((4, 128), F32)],
        0,
    )


def style_grads_kernel(
    place,
    own_one,
    other_one,
    own_two,
    other_two,
    squares_one,
    squares_two,
    styles,
    style_sums,
    sums_one,
    sums_two,
    a1,
    a2,
    a3,
    grads,
    crossing,
):
    images, share = style_sums.shape
    mine, theirs = rows_at(place[2], share), rows_at(1 - place[2], share)
    rows = []
    for layer, (own, other, squares, sums) in enumerate(
        ((own_one, other_one, squares_one, style_sums), (own_two, other_two, squares_two, None))
    ):
        back = exact(own[...], squares[:, mine], 1, 1) + exact(
            other[...], squares[:, theirs], 1, 1
        )
        if sums is None:
            direct = jnp.concatenate([sums_one[b, 2:3, :] for b in range(images)], 0)
        else:
            direct = sums[...]
        rows.append(direct + 2.0 * styles[layer] * back)
    rows.append(jnp.concatenate([sums_two[b, 2:3, :] for b in range(images)], 0))
    grads[...] = jnp.concatenate(rows, 0)
    latent = None
    for row, affine in zip(rows, (a1, a2, a3)):
        part = exact(row, affine[...].astype(F32), 1, 1)
        latent = part if latent is None else latent + part
    lane = lax.broadcasted_iota(jnp.int32, (1, share), 1)
    scalars = jnp.zeros((1, share), F32)
    for index, (sums, row) in enumerate(
        ((sums_one, 3), (sums_two, 3), (sums_one, 1), (sums_two, 1))
    ):
        total = sums[0, row : row + 1, :]
        for image in range(1, images):
            total = total + sums[image, row : row + 1, :]
        scalars = scalars + jnp.where(lane == index, jnp.sum(total, keepdims=True), 0.0)
    pieces = [latent[b : b + 1, h * share : (h + 1) * share] for b in range(images) for h in (0, 1)]
    blank = jnp.zeros((crossing.shape[0] - len(pieces) - 1, share), F32)
    crossing[...] = jnp.concatenate(pieces + [scalars, blank], 0)


def pack_kernel(
    valid,
    own,
    other,
    grads,
    latent,
    sums_one,
    sums_two,
    rgb_grad,
    rgb_sums,
    grad_latent,
    pack,
):
    images, share = latent.shape[0], grads.shape[1]
    total = own[...] + other[...]
    count = 2 * images
    for image in range(images):
        grad_latent[image : image + 1, :] = jnp.concatenate(
            [total[2 * image : 2 * image + 1], total[2 * image + 1 : 2 * image + 2]], 1
        )
    values = latent[...].astype(F32)
    rows = [values[:, :share], values[:, share:], grads[...]]
    for sums in (sums_one, sums_two):
        bias = sums[0, 0:1, :]
        for image in range(1, images):
            bias = bias + sums[image, 0:1, :]
        rows.append(bias)
    rows.append(rgb_grad[:3, :])
    lane = lax.broadcasted_iota(jnp.int32, (1, share), 1)
    scalars = total[count : count + 1]
    wide = jnp.concatenate([rgb_sums[...]] * (share // 128), 1)
    for index in range(4):
        scalars = scalars + jnp.where(lane == 4 + index, wide[index : index + 1], 0.0)
    for image in range(images):
        scalars = scalars + jnp.where(lane == 8, valid[image : image + 1, :], 0.0)
    rows.append(scalars)
    used = sum(member.shape[0] for member in rows)
    if used < pack.shape[0]:
        rows.append(jnp.zeros((pack.shape[0] - used, share), F32))
    pack[...] = jnp.concatenate(rows, 0)


def spread_kernel(place, *refs, images):
    packs, outs, parts = refs[:-14], refs[-14:-1], refs[-1]
    grads, biases, points = outs[0:3], outs[3:6], outs[6:8]
    rgb_grad, gains, rms, rgb_bias, everything = outs[8:]
    if len(packs) == 1:
        everything[...] = packs[0][...]
    else:
        own, got_own, other, got_other = packs
        tap, rows = own.shape[0] - 1, everything.shape[1]
        for index in range(8):
            at = pl.ds(rows * index, rows)
            near, far, second = (index >> 1) & 1, index & 1, index >> 2
            line = 8 * far + 4 * near
            for own_ref, other_ref, first_x, first_y in (
                (own, other, place[0], place[1]),
                (got_own, got_other, 1 - place[0], 1 - place[1]),
            ):
                parts[0, line + 2 * second + first_x] = own_ref[tap, at, :].astype(F32)
                parts[1, line + 2 * first_y + second] = other_ref[tap, at, :].astype(F32)
        everything[...] = parts[0] + parts[1]
    count = everything.shape[0]

    def rows(start, size):
        return jnp.concatenate([everything[d, start : start + size, :] for d in range(count)], 0)

    latent = jnp.concatenate([rows(0, images), rows(images, images)], 1)
    at = 2 * images
    for layer in range(3):
        grad = rows(at, images)
        grads[layer][...] = exact(latent, grad, 0, 0)
        biases[layer][...] = jnp.sum(grad, axis=0, keepdims=True)
        at += images
    total = everything[0]
    for device in range(1, count):
        total = total + everything[device]
    points[0][...] = total[at : at + 1]
    points[1][...] = total[at + 1 : at + 2]
    rgb_grad[...] = total[at + 2 : at + 5]
    scalars = total[at + 5 : at + 6]
    lane = lax.broadcasted_iota(jnp.int32, scalars.shape, 1)

    def scalar(index):
        return jnp.sum(jnp.where(lane == index, scalars, 0.0))

    share = scalars.shape[1]
    real = jnp.sum(jnp.where(lane == 8, scalars, 0.0), keepdims=True)
    entries = jnp.where(lane == 4, 3.0 * RES * RES, 2.0 * share * RES * RES)
    roots = jnp.sqrt(scalars / (real * entries))

    def root(index):
        return jnp.sum(jnp.where(lane == index, roots, 0.0))

    for index, lane_at in enumerate((0, 1, 4)):
        rms[index] = root(lane_at)
    for index in range(2):
        gains[index] = scalar(2 + index)
    for index in range(3):
        rgb_bias[index] = scalar(5 + index)


def second_kernel(
    place, keep_own, got_own, keep_other, got_other, s_own, k_own, s_other, k_other
):
    count = s_own.shape[1]
    for axis, keep, got, send, kept in (
        (1, keep_own, got_own, s_own, k_own),
        (0, keep_other, got_other, s_other, k_other),
    ):
        away, here = rows_at(1 - place[axis], count), rows_at(place[axis], count)

        def one(tap, keep=keep, got=got, send=send, kept=kept, away=away, here=here):
            total = keep[tap, away, :] + got[tap, away, :].astype(F32)
            send[tap] = total.astype(BF16)
            kept[tap] = keep[tap, here, :] + got[tap, here, :].astype(F32)

        each(keep.shape[0], one)


def merge_kernel(place, keep_own, got_own, keep_other, got_other, send, keep):
    count = send.shape[2]
    away, here = rows_at(1 - place[3], count), rows_at(place[3], count)
    for order, (kept, got) in enumerate(((keep_own, got_own), (keep_other, got_other))):

        def one(tap, order=order, kept=kept, got=got):
            total = kept[tap, away, :] + got[tap, away, :].astype(F32)
            send[order, tap] = total.astype(BF16)
            keep[order, tap] = kept[tap, here, :] + got[tap, here, :].astype(F32)

        each(kept.shape[0], one)


def across_kernel(kept, got, out):
    for order in range(kept.shape[0]):

        def one(tap, order=order):
            out[order, tap] = (kept[order, tap] + got[order, tap].astype(F32)).astype(BF16)

        each(kept.shape[1], one)


def total_kernel(place, mine, got, *refs):
    packs, out = refs[:-1], refs[-1]
    for index, pack in enumerate(packs):
        rows = rows_at(place[4] if index == 0 else 1 - place[4], pack.shape[0])
        for order, part in enumerate(split_three(pack[...])[:2]):
            out[order, out.shape[1] - 1, rows, :] = part
    for order in range(mine.shape[0]):

        def one(tap, order=order):
            total = mine[order, tap].astype(F32) + got[order, tap].astype(F32)
            out[order, tap] = total.astype(BF16)

        each(mine.shape[1], one)


def join_near_kernel(place, own, got, *outs):
    count = own.shape[2]
    here, away = rows_at(place[3], count), rows_at(1 - place[3], count)
    for order, out in enumerate(outs):

        def one(tap, order=order, out=out):
            out[tap, here, :] = own[order, tap]
            out[tap, away, :] = got[order, tap]

        each(own.shape[1], one)


def join_pair_kernel(place, own, got_own, other, got_other, half_own, half_other):
    count = own.shape[1]
    for axis, mine, theirs, out in ((1, own, got_own, half_own), (0, other, got_other, half_other)):
        here, away = rows_at(place[axis], count), rows_at(1 - place[axis], count)

        def one(tap, mine=mine, theirs=theirs, out=out, here=here, away=away):
            out[tap, here, :] = mine[tap]
            out[tap, away, :] = theirs[tap]

        each(out.shape[0], one)


def finish_kernel(place, own, other, *refs, away, first):
    out, held, sems = refs[-3:]
    _, taps, half, share = held.shape

    def copy(tap, order):
        column, index = (place[2], place[0]) if order == 0 else (1 - place[2], place[1])
        rows = rows_at(1 - index if away else index, half)
        block = out.at[first + tap, rows, rows_at(column, share)]
        return pltpu.make_async_copy(held.at[order, tap], block, sems.at[order, tap])

    def one(tap):
        for order, part in enumerate((own, other)):
            held[order, tap] = part[tap].astype(F32)
            copy(tap, order).start()

    def last(tap):
        for order in range(2):
            copy(tap, order).wait()

    each(taps, one)
    each(taps, last)


def call(body, outs, scratch=(), smem=0, after=(), hbm=(), scalars=(), plain=(), loose=(), whole=(), micros=0, aliases=None):
    outs = outs if isinstance(outs, tuple) else (outs,)
    any_space = pl.BlockSpec(memory_space=pl.ANY)

    def run(*operands):
        count = len(operands)
        spaces = [pltpu.SMEM] * smem + [pltpu.VMEM] * (count - smem)
        for index in loose + whole:
            spaces[index] = pltpu.HBM
        values = [pltpu.with_memory_space_constraint(*pair) for pair in zip(operands, spaces)]

        def inner(*refs):
            body(*refs[:count], *refs[count + len(after) : -1 - len(scratch)], *refs[len(refs) - len(scratch) :])

        results = pl.pallas_call(
            inner,
            out_shape=tuple(
                member if index in hbm + scalars + plain else pltpu.VMEM(member.shape, member.dtype)
                for index, member in enumerate(outs)
            )
            + (shape(8, 128),),
            in_specs=[SMEM] * smem
            + [any_space if index in whole or index in (aliases or {}) else VMEM for index in range(smem, count)]
            + [any_space] * len(after),
            out_specs=tuple(
                any_space if index in hbm else SMEM if index in scalars else VMEM
                for index in range(len(outs))
            )
            + (any_space,),
            scratch_shapes=scratch,
            input_output_aliases=aliases or {},
            compiler_params=pltpu.CompilerParams(vmem_limit_bytes=VMEM_BYTES),
            cost_estimate=pl.CostEstimate(
                flops=2**10 + int(micros * 1.1e9), bytes_accessed=2**10, transcendentals=0
            ),
        )(*values, *after)
        found, token = results[:-1], results[-1]
        return (found if len(found) > 1 else found[0]), token

    return run


def shape(*dims, kind=F32):
    return jax.ShapeDtypeStruct(dims, kind)


def kernel_shapes(taps, rows, cols):
    return (shape(taps, rows, cols, kind=BF16), shape(taps, rows, cols))


def swap(values, axis_name):
    return lax.ppermute(values, axis_name, SWAP)


def part_of(values, axis, index, size):
    return lax.dynamic_slice_in_dim(values, index * size, size, axis)


def place_pair(index, own, other, axis):
    return jnp.where(
        index == 0,
        jnp.concatenate([own, other], axis=axis),
        jnp.concatenate([other, own], axis=axis),
    )


class Reduction:
    def __init__(self, place, parts, first=0):
        self.place, self.first, self.taps = place, first, parts[0].shape[0]
        self.sent_own, self.keep_own, self.sent_other, self.keep_other = parts
        self.got = swap(self.sent_own, "x"), swap(self.sent_other, "y")

    def second(self, token, micros=0):
        taps, rows, cols = self.keep_own.shape
        parts, token = call(
            second_kernel,
            kernel_shapes(taps, rows // 2, cols) * 2,
            smem=1,
            after=(token,),
            micros=micros,
        )(self.place, self.keep_own, self.got[0], self.keep_other, self.got[1])
        sent_own, self.keep_own, sent_other, self.keep_other = parts
        self.got = swap(sent_own, "y"), swap(sent_other, "x")
        return token

    def near(self, token, micros=0):
        taps, rows, cols = self.keep_own.shape
        piece = (2, taps, rows // 2, cols)
        (send, self.keep), token = call(
            merge_kernel, (shape(*piece, kind=BF16), shape(*piece)), smem=1, after=(token,), micros=micros
        )(self.place, self.keep_own, self.got[0], self.keep_other, self.got[1])
        self.got = swap(send, "near")
        return token

    def across(self, token, micros=0):
        out = shape(*self.keep.shape, kind=BF16)
        self.own, token = call(across_kernel, out, after=(token,), micros=micros)(
            self.keep, self.got
        )
        self.got = swap(self.own, "far")
        return token

    def total(self, token, *packs, micros=0):
        if lax.axis_size("block") > 1:
            self.own = lax.psum(self.own.astype(F32) + self.got.astype(F32), "block").astype(BF16)
            self.got = jnp.zeros_like(self.own)
        orders, taps, rows, cols = self.own.shape
        out = shape(orders, taps + min(len(packs), 1), rows, cols, kind=BF16)
        self.own, token = call(total_kernel, out, smem=1, after=(token,), micros=micros)(
            self.place, self.own, self.got, *packs
        )
        self.got = swap(self.own, "near")
        return token

    def join_near(self, token, micros=0):
        _, taps, rows, cols = self.own.shape
        quarter = shape(taps, 2 * rows, cols, kind=BF16)
        self.own, token = call(
            join_near_kernel, (quarter,) * 2, smem=1, after=(token,), micros=micros
        )(self.place, self.own, self.got)
        self.got = swap(self.own[0], "y"), swap(self.own[1], "x")
        return token

    def join_pair(self, token, micros=0):
        taps, rows, cols = self.own[0].shape
        half = shape(taps, 2 * rows, cols, kind=BF16)
        self.own, token = call(
            join_pair_kernel, (half,) * 2, smem=1, after=(token,), micros=micros
        )(
            self.place, self.own[0], self.got[0], self.own[1], self.got[1]
        )
        self.got = swap(self.own[0], "x"), swap(self.own[1], "y")
        return token

    def finish_half(self, token, parts, out, away):
        taps, (_, half, share) = self.taps, parts[0].shape
        return call(
            functools.partial(finish_kernel, away=away, first=self.first),
            shape(9, 2 * half, 2 * share),
            [pltpu.VMEM((2, taps, half, share), F32), pltpu.SemaphoreType.DMA((2, taps))],
            smem=1,
            after=(token,),
            hbm=(0,),
            loose=(3,) if out else (),
            aliases={3: 0} if out else None,
        )(self.place, *parts, *out)

    def finish_own(self, token, out=()):
        return self.finish_half(token, self.own, out, False)

    def finish(self, token, out):
        return self.finish_half(token, self.got, (out,), True)


def gather_packs(pack):
    for axis_name in DP[::-1]:
        pack = lax.all_gather(pack[None] if pack.ndim == 2 else pack, axis_name, axis=0, tiled=True)
    return pack


def per_device(
    counts,
    features_in,
    rgb_in,
    latent,
    affine_one,
    affine_bias_one,
    affine_two,
    affine_bias_two,
    affine_three,
    affine_bias_three,
    kernel_one,
    bias_one,
    kernel_two,
    bias_two,
    rgb_weight,
    rgb_bias,
    noise_gain,
    noise_one,
    noise_two,
    grad_features,
    grad_rgb,
):
    images, share = features_in.shape[0], features_in.shape[3]
    channels = share * lax.axis_size("chan")
    me = lax.axis_index("chan")
    place = jnp.stack([lax.axis_index(name) for name in ("x", "y", "chan", "near", "far")])
    place = place.astype(jnp.int32)
    valid = (jnp.arange(images, dtype=jnp.int32) < counts[0]).astype(F32)
    valid_rows = jnp.broadcast_to(valid[:, None], (images, share))
    features = features_in.reshape(images, PLANE, share)
    flat_one = kernel_one.reshape(9, share, channels)
    flat_two = kernel_two.reshape(9, share, channels)
    plane_shape = (images, 4, PLANE, share)
    half = share // 2
    wide = pltpu.VMEM((share // 128, HALF, 2, RES, 128), F32)

    send_kind = shape(9, share, share, kind=BF16)
    (styles, scaled_one, send_one), token = call(
        style_kernel,
        (shape(3, images, share), shape(images, PLANE, share, kind=BF16), send_kind),
        [pltpu.SemaphoreType.DMA],
        smem=1,
        loose=tuple(range(2, 10)),
        whole=(1,),
    )(
        place,
        flat_one,
        latent,
        affine_one,
        affine_bias_one.reshape(1, -1),
        affine_two,
        affine_bias_two.reshape(1, -1),
        affine_three,
        affine_bias_three.reshape(1, -1),
        features,
    )
    received_one = swap(send_one, "chan")
    scaled_one_other = swap(scaled_one, "chan")

    def layer_squares(layer, kernel, bias, token):
        (squares, mine, theirs, add, colour), token = call(
            functools.partial(squares_kernel, layer=layer),
            (
                shape(share, channels),
                shape(images, share),
                shape(images, share),
                shape(16, share, kind=BF16),
                shape(images, 16, share, kind=BF16),
            ),
            [pltpu.VMEM((images, channels), F32)],
            smem=1,
            after=(token,),
            loose=(3, 4),
        )(place, styles, kernel, bias.reshape(1, -1), rgb_weight)
        return squares, mine, swap(theirs, "chan"), add, colour, token

    squares_one, mine_one, theirs_one, add_one, _, token = layer_squares(
        0, flat_one, bias_one, token
    )
    (noise_planes_one, noise_planes_two, colours, send_two), token = call(
        planes_kernel,
        (shape(images, 4, 16, PLANE, kind=BF16),) * 3 + (send_kind,),
        [pltpu.SemaphoreType.DMA],
        smem=1,
        after=(token,),
        loose=(2, 4, 5, 6),
        whole=(3,),
    )(place, valid_rows, noise_gain.reshape(1, -1), flat_two, noise_one, noise_two, grad_rgb)
    received_two = swap(send_two, "chan")
    rgb_rows_in = jnp.pad(rgb_weight, ((0, 13), (0, 0)))

    (conv_one, scaled_two, demod_one), token = call(
        conv_one_kernel,
        (shape(*plane_shape), shape(*plane_shape, kind=BF16), shape(images, share)),
        smem=1,
        after=(token,),
        micros=STAGE,
    )(
        place,
        scaled_one,
        scaled_one_other,
        flat_one,
        received_one,
        mine_one,
        theirs_one,
        noise_planes_one,
        add_one,
        styles,
    )
    scaled_two_other = swap(scaled_two, "chan")
    squares_two, mine_two, theirs_two, add_two, colour_weights, token = layer_squares(
        1, flat_two, bias_two, token
    )
    (conv_two, grad_conv_two, demod_two, square_two), token = call(
        conv_two_kernel,
        (
            shape(*plane_shape),
            shape(*plane_shape, kind=BF16),
            shape(images, share),
            shape(images, share),
        ),
        [wide],
        smem=1,
        after=(token,),
    )(
        place,
        scaled_two,
        scaled_two_other,
        flat_two,
        received_two,
        mine_two,
        theirs_two,
        valid_rows,
        noise_planes_two,
        add_two,
        colours,
        colour_weights,
        grad_features,
    )
    grad_conv_two_other = swap(grad_conv_two, "chan")
    square_two_other = swap(square_two, "chan")
    shifted_two, token = call(
        shifted_kernel, shape(*plane_shape, kind=BF16), after=(token,)
    )(scaled_two)
    parts_two, token = call(
        kernel_two_grad,
        kernel_shapes(9, half, share) * 2,
        [pltpu.VMEM((images, share), F32)],
        smem=1,
        after=(token,),
    )(
        place,
        scaled_two,
        shifted_two,
        grad_conv_two,
        grad_conv_two_other,
        flat_two,
        styles,
        square_two,
        square_two_other,
    )
    reduce_two = Reduction(place, parts_two)
    (grad_scaled_two, grad_conv_one, square_one), token = call(
        input_two_grad,
        (shape(*plane_shape), shape(*plane_shape, kind=BF16), shape(images, share)),
        smem=1,
        after=(token,),
    )(
        place,
        grad_conv_two,
        grad_conv_two_other,
        flat_two,
        conv_one,
        demod_one,
        noise_planes_one,
        add_one,
        styles,
    )
    grad_conv_one_other = swap(grad_conv_one, "chan")
    square_one_other = swap(square_one, "chan")
    (features_out, rgb_planes, rgb_grad, sums_two), token = call(
        outputs_two_kernel,
        (
            shape(images, RES, RES, share, kind=BF16),
            shape(images, 4, 8, PLANE),
            shape(16, share),
            shape(images, 8, share),
        ),
        [wide],
        after=(token,),
        plain=(0,),
        loose=(6,),
    )(
        conv_two,
        demod_two,
        valid_rows,
        noise_planes_two,
        add_two,
        colours,
        grad_features,
        styles,
        rgb_rows_in,
    )
    rgb_planes_other = swap(rgb_planes, "chan")
    token = reduce_two.second(token, STAGE)
    parts_one, token = call(
        kernel_one_grad,
        kernel_shapes(9, half, share) * 2,
        [pltpu.VMEM((images, PLANE, share), BF16), pltpu.VMEM((images, share), F32)],
        smem=1,
        after=(token,),
    )(
        place,
        scaled_one,
        grad_conv_one,
        grad_conv_one_other,
        flat_one,
        styles,
        square_one,
        square_one_other,
    )
    reduce_one = Reduction(place, parts_one)
    (rgb_out, grad_rgb_in, rgb_sums), token = call(
        rgb_kernel,
        (shape(*grad_rgb.shape), shape(*rgb_in.shape), shape(8, 128)),
        [pltpu.VMEM((3 * images, RES, 128), F32)],
        after=(token,),
        plain=(0, 1),
        loose=(1, 4, 5),
    )(valid_rows, rgb_bias.reshape(1, -1), rgb_planes, rgb_planes_other, rgb_in, grad_rgb)
    token = reduce_two.near(token, STAGE)
    sums_one, token = call(
        outputs_one_kernel, shape(images, 8, share), after=(token,)
    )(
        conv_one,
        grad_scaled_two,
        demod_one,
        valid_rows,
        noise_planes_one,
        add_one,
        styles,
    )
    (grad_features_in, style_sums), token = call(
        input_one_grad,
        (shape(images, PLANE, share), shape(images, share)),
        smem=1,
        after=(token,),
        plain=(0,),
        loose=(4,),
    )(place, grad_conv_one, grad_conv_one_other, flat_one, features, styles)
    (style_grads, crossing), token = call(
        style_grads_kernel,
        (shape(3 * images, share), shape(-(-(2 * images + 1) // 8) * 8, share)),
        smem=1,
        after=(token,),
        loose=(11, 12, 13),
    )(
        place,
        square_one,
        square_one_other,
        square_two,
        square_two_other,
        squares_one,
        squares_two,
        styles,
        style_sums,
        sums_one,
        sums_two,
        affine_one,
        affine_two,
        affine_three,
    )
    crossing_other = swap(crossing, "chan")
    token = reduce_two.across(token)
    token = reduce_one.second(token)
    (grad_latent, pack), token = call(
        pack_kernel,
        (shape(images, channels), shape(-(-(5 * images + 6) // 8) * 8, share)),
        after=(token,),
        plain=(0,),
    )(
        valid_rows,
        crossing,
        crossing_other,
        style_grads,
        latent,
        sums_one,
        sums_two,
        rgb_grad,
        rgb_sums,
    )
    devices = lax.axis_size(DP)
    alone = lax.axis_size("block") == 1
    packs = [pack, swap(pack, "far")] if alone else []
    token = reduce_two.total(token, *packs, micros=STAGE)
    token = reduce_one.near(token, STAGE)
    token = reduce_two.join_near(token, STAGE)
    token = reduce_one.across(token, STAGE)
    token = reduce_two.join_pair(token, STAGE)
    token = reduce_one.total(token, micros=STAGE)
    sum_two, token = reduce_two.finish_own(token)
    token = reduce_one.join_near(token)
    sum_two, token = reduce_two.finish(token, sum_two)
    if alone:
        packs = [reduce_two.own[0], reduce_two.got[0], reduce_two.own[1], reduce_two.got[1]]
    else:
        packs = [gather_packs(pack)]
    token = reduce_one.join_pair(token, STAGE)
    sum_one, token = reduce_one.finish_own(token)
    spread_out, token = call(
        functools.partial(spread_kernel, images=images),
        (shape(channels, share),) * 3
        + (shape(1, share),) * 5
        + (shape(3, share), shape(2), shape(3), shape(3)),
        [pltpu.VMEM((devices,) + pack.shape, F32), pltpu.VMEM((2, devices) + pack.shape, F32)],
        smem=1,
        after=(token,),
        scalars=(9, 10, 11),
        plain=tuple(range(9)),
    )(place, *packs)
    affine_grads, affine_biases, points = spread_out[0:3], spread_out[3:6], spread_out[6:8]
    rgb_total, gains, rms_values, rgb_bias_grad = spread_out[8:]
    sum_one, token = reduce_one.finish(token, sum_one)
    affine_outs = []
    for grad, bias in zip(affine_grads, affine_biases):
        affine_outs += [grad, bias.reshape(-1)]
    return (
        features_out,
        rgb_out,
        grad_features_in.reshape(features_in.shape),
        grad_rgb_in,
        grad_latent,
        *affine_outs,
        sum_one.reshape(kernel_one.shape),
        points[0].reshape(-1),
        sum_two.reshape(kernel_two.shape),
        points[1].reshape(-1),
        rgb_total,
        rgb_bias_grad,
        gains,
        rms_values,
    )


def solution(mesh):
    blocks = mesh.shape["dp"] // 16
    grid = mesh.devices.reshape(blocks, 2, 2, 2, 2, mesh.shape["chan"])
    split_mesh = Mesh(grid, DP + ("chan",))
    in_specs = (
        P(DP),
        P(DP, None, None, "chan"),
        P(DP, None, None, None),
        P(DP, None),
        P(None, "chan"),
        P("chan"),
        P(None, "chan"),
        P("chan"),
        P(None, "chan"),
        P("chan"),
        P(None, None, "chan", None),
        P("chan"),
        P(None, None, "chan", None),
        P("chan"),
        P(None, "chan"),
        P(),
        P(),
        P(DP, None, None),
        P(DP, None, None),
        P(DP, None, None, "chan"),
        P(DP, None, None, None),
    )
    out_specs = (
        P(DP, None, None, "chan"),
        P(DP, None, None, None),
        P(DP, None, None, "chan"),
        P(DP, None, None, None),
        P(DP, None),
        P(None, "chan"),
        P("chan"),
        P(None, "chan"),
        P("chan"),
        P(None, "chan"),
        P("chan"),
        P(None, None, "chan", None),
        P("chan"),
        P(None, None, "chan", None),
        P("chan"),
        P(None, "chan"),
        P(),
        P(),
        P(),
    )
    return jax.shard_map(
        per_device, mesh=split_mesh, in_specs=in_specs, out_specs=out_specs, check_vma=False
    )
```

```python
import functools

import jax
import jax.numpy as jnp
from jax import lax
from jax.experimental import pallas as pl
from jax.experimental.pallas import tpu as pltpu
from jax.sharding import Mesh, PartitionSpec as P

RES = 32
HALF = 16
PLANE = HALF * HALF
SQRT_TWO = 1.4142135623730951
EPSILON = 1e-08
STAGE = 60
DP = ("block", "far", "near", "y", "x")
SWAP = [(0, 1), (1, 0)]
F32 = jnp.float32
BF16 = jnp.bfloat16
VMEM_BYTES = 16 * 2**20
VMEM = pl.BlockSpec(memory_space=pltpu.VMEM)
SMEM = pl.BlockSpec(memory_space=pltpu.SMEM)
UP_TAPS = (((0, 1),), ((0, 0), (1, 2)))


GROUPS_TWO = ((3, ("x", "y", "near")), (3, ("y", "near", "x")), (3, ("near", "x", "y")))
GROUPS_ONE = ((3, ("x", "y", "near")), (3, ("y", "near", "x")), (3, ("near", "x", "y")))
AT = {"x": 0, "y": 1, "chan": 2, "near": 3, "far": 4}


def dot(left, right, left_dim, right_dim):
    return lax.dot_general(
        left, right, (((left_dim,), (right_dim,)), ((), ())), preferred_element_type=F32
    )


def exact(left, right, left_dim, right_dim):
    return lax.dot_general(
        left,
        right,
        (((left_dim,), (right_dim,)), ((), ())),
        precision=lax.Precision.HIGHEST,
        preferred_element_type=F32,
    )


def source(parity, tap):
    return (parity + tap - 1) & 1, (parity + tap - 1) >> 1


def each(count, body):
    lax.fori_loop(0, count, lambda index, carry: (body(index), carry)[1], 0)


def row_of(ref, index):
    return ref[pl.ds(index, 1), :]


def rows_at(index, count):
    return pl.ds(pl.multiple_of(index * count, count), count)


def plane_at(image, plane):
    return rows_at(4 * image + plane, PLANE)


def squares_behind(ref, images):
    parts = ref[ref.shape[0] - 16 :, :].astype(F32)
    return jnp.concatenate(
        [jnp.sum(parts[3 * b : 3 * b + 3], axis=0, keepdims=True) for b in range(images)], 0
    )


def rows_from(values, shift):
    if shift == 0:
        return values
    blank = jnp.zeros((HALF, values.shape[1]), values.dtype)
    if shift == 1:
        return jnp.concatenate([values[HALF:], blank], 0)
    return jnp.concatenate([blank, values[:-HALF]], 0)


def columns_from(values, shift):
    if shift == 0:
        return values
    moved = pltpu.roll(values, (-shift) % values.shape[0], 0)
    column = lax.broadcasted_iota(jnp.int32, values.shape, 0) % HALF
    return jnp.where(column == (HALF - 1 if shift == 1 else 0), 0.0, moved)


def gather_terms(terms):
    total = None
    for shift, group in terms.items():
        part = None
        for left, right, right_dim in group:
            product = dot(left, right, 1, right_dim)
            part = product if part is None else part + product
        part = columns_from(part, shift)
        total = part if total is None else total + part
    return total


def split_three(values):
    high = values.astype(BF16)
    rest = values - high.astype(F32)
    middle = rest.astype(BF16)
    low = (rest - middle.astype(F32)).astype(BF16)
    return high, middle, low


def fetch(place, kernel, out, sem):
    share = out.shape[2]
    return pltpu.make_async_copy(kernel.at[:, :, rows_at(1 - place[2], share)], out, sem)


def split_rows(values, count):
    rows = []
    for index in range(values.shape[0]):
        rows += [part.astype(F32) for part in split_three(values[index : index + 1, :])]
    blank = jnp.zeros((count - len(rows), values.shape[1]), F32)
    return jnp.concatenate(rows + [blank], 0).astype(BF16)


def style_kernel(
    place, kernel, latent, a1, b1, a2, b2, a3, b3, features, styles, scaled, send, sem
):
    fetch(place, kernel, send, sem).start()
    for index, (affine, bias) in enumerate(((a1, b1), (a2, b2), (a3, b3))):
        styles[index] = dot(latent[...], affine[...], 1, 0) + bias[...]
    for image in range(features.shape[0]):
        row = styles[0, image : image + 1, :]
        scaled[image] = (features[image].astype(F32) * row).astype(BF16)
    fetch(place, kernel, send, sem).wait()


def pixel_planes(rasters):
    count = len(rasters)
    stacked = jnp.concatenate(rasters, 0)
    lane = lax.broadcasted_iota(jnp.int32, (RES, PLANE), 1)
    line = lax.broadcasted_iota(jnp.int32, (RES, PLANE), 0)
    found = [[None] * 4 for _ in range(count)]
    for qx in range(2):
        choose = jnp.where(line == 2 * (lane % HALF) + qx, 1.0, 0.0).astype(BF16)
        spread_out = dot(stacked, choose, 1, 0)
        for qy in range(2):
            mask = jnp.where(line == 2 * (lane // HALF) + qy, 1.0, 0.0)
            for index in range(count):
                block = spread_out[RES * index : RES * (index + 1)]
                found[index][2 * qy + qx] = jnp.sum(block * mask, axis=0, keepdims=True)
    return found


def planes_kernel(
    place,
    valid,
    gain,
    kernel,
    noise_one,
    noise_two,
    grad_rgb,
    planes_one,
    planes_two,
    colours,
    send,
    sem,
):
    fetch(place, kernel, send, sem).start()
    images = noise_one.shape[0]
    ones = jnp.ones((3, PLANE), F32)
    blank = jnp.zeros((7, PLANE), F32)
    for image in range(images):
        rasters = []
        for index, noise in enumerate((noise_one, noise_two)):
            value = noise[image]
            rasters += list(split_three(value)) + list(split_three(value * gain[:, index : index + 1]))
        keep = valid[image : image + 1, :RES]
        for colour in range(3):
            rasters.append((grad_rgb[image, colour].astype(F32) * keep).astype(BF16))
        found = pixel_planes(rasters)
        for plane in range(4):
            rows = [member[plane] for member in found]
            planes_one[image, plane] = jnp.concatenate(rows[:6] + [ones, blank], 0).astype(BF16)
            planes_two[image, plane] = jnp.concatenate(rows[6:12] + [ones, blank], 0).astype(BF16)
            colours[image, plane] = jnp.concatenate(rows[12:] * 3 + [blank], 0).astype(BF16)
    fetch(place, kernel, send, sem).wait()


def squares_kernel(
    place, styles, kernel, bias, rgb, squares, mine, theirs, add, colour, parts, *, layer
):
    total = None
    for tap in range(kernel.shape[0]):
        value = kernel[tap].astype(F32)
        total = value * value if total is None else total + value * value
    squares[...] = total
    style = styles[layer]
    parts[...] = lax.dot_general(
        style * style,
        total,
        (((1,), (0,)), ((), ())),
        precision=lax.Precision.HIGHEST,
        preferred_element_type=F32,
    )
    share = bias.shape[1]
    mine[...] = parts[:, pl.ds(pl.multiple_of(place[2] * share, share), share)]
    theirs[...] = parts[:, pl.ds(pl.multiple_of((1 - place[2]) * share, share), share)]
    add[...] = jnp.concatenate(
        [jnp.zeros((3, share), F32), jnp.full((3, share), 0.5, F32)]
        + [part.astype(F32) for part in split_three(0.5 * bias[...])]
        + [jnp.zeros((7, share), F32)],
        0,
    ).astype(BF16)
    for image in range(styles.shape[1]):
        weight = rgb[...].astype(F32) * styles[2, image : image + 1, :]
        colour[image] = jnp.concatenate(
            [part.astype(F32) for part in split_three(weight)] + [jnp.zeros((7, share), F32)], 0
        ).astype(BF16)


def scale_half(rows, add, image, plane, demod, weights):
    return rows * (0.5 * demod) + dot(add[image, plane], weights, 0, 0)


def smooth_leaky(half_pre):
    size = jnp.abs(half_pre)
    soft = jnp.maximum(half_pre, 0.0) * 2.0 + jnp.log(1.0 + jnp.exp(-2.0 * size))
    return (0.4 * SQRT_TWO) * half_pre + (0.8 * SQRT_TWO) * soft


def leaky_slope(half_pre):
    return (0.6 * SQRT_TWO) + (0.4 * SQRT_TWO) * jnp.tanh(half_pre)


def column_sum(values):
    return jnp.sum(values, axis=0, keepdims=True)


def square_grad(products, demod):
    return -0.5 * products * demod * demod


def conv_one_kernel(
    place,
    own,
    other,
    k_own,
    k_other,
    sums_own,
    sums_other,
    add,
    weights,
    styles,
    conv,
    scaled,
    demod,
):
    share = own.shape[-1]
    columns = pl.ds(pl.multiple_of(place[2] * share, share), share)
    demod[...] = lax.rsqrt(sums_own[...] + sums_other[...] + EPSILON)
    for qy in range(2):
        for qx in range(2):
            plane = 2 * qy + qx
            terms = {}
            for shift_y, tap_y in UP_TAPS[qy]:
                for shift_x, tap_x in UP_TAPS[qx]:
                    tap = 3 * tap_y + tap_x
                    for source_ref, right in (
                        (own, k_own[tap, :, columns]),
                        (other, k_other[tap]),
                    ):
                        left = jnp.concatenate(
                            [rows_from(source_ref[b], shift_y) for b in range(own.shape[0])], 0
                        )
                        terms.setdefault(shift_x, []).append((left, right, 0))
            total = gather_terms(terms)
            for image in range(own.shape[0]):
                rows = total[image * PLANE : (image + 1) * PLANE]
                conv[image, plane] = rows
                half_pre = scale_half(
                    rows, add, image, plane, demod[image : image + 1, :], weights[...]
                )
                act = smooth_leaky(half_pre)
                scaled[image, plane] = (act * styles[1, image : image + 1, :]).astype(BF16)


def spread(raster, image, wide):
    for block in range(wide.shape[0]):
        lanes = raster[image, :, :, block * 128 : (block + 1) * 128]
        wide[block] = lanes.reshape(wide.shape[1:]).astype(F32)


def read_plane(wide, qy, qx):
    cells = [wide[block, :, qy, pl.ds(qx, HALF, stride=2), :] for block in range(wide.shape[0])]
    return jnp.concatenate([cell.reshape(PLANE, 128) for cell in cells], 1)


def write_plane(wide, qy, qx, values):
    for block in range(wide.shape[0]):
        cell = values[:, block * 128 : (block + 1) * 128].reshape(HALF, HALF, 128)
        wide[block, :, qy, pl.ds(qx, HALF, stride=2), :] = cell


def store_raster(wide, out, image):
    for block in range(wide.shape[0]):
        lanes = wide[block].reshape(RES, RES, 128)
        out[image, :, :, block * 128 : (block + 1) * 128] = lanes.astype(out.dtype)


def conv_two_kernel(
    place,
    own,
    other,
    k_own,
    k_other,
    sums_own,
    sums_other,
    valid,
    add,
    weights,
    colours,
    colour_weights,
    cotangent,
    conv,
    grad_conv,
    demod,
    wide,
    square,
):
    share = own.shape[-1]
    columns = pl.ds(pl.multiple_of(place[2] * share, share), share)
    demod[...] = lax.rsqrt(sums_own[...] + sums_other[...] + EPSILON)

    def one(image):
        spread(cotangent, image, wide)
        products = None
        for qy in range(2):
            for qx in range(2):
                plane = 2 * qy + qx
                terms = {}
                for tap_x in range(3):
                    px, shift_x = source(qx, tap_x)
                    for tap_y in range(3):
                        py, shift_y = source(qy, tap_y)
                        tap = 3 * tap_y + tap_x
                        for source_ref, right in (
                            (own, k_own[tap, :, columns]),
                            (other, k_other[tap]),
                        ):
                            left = rows_from(source_ref[image, 2 * py + px], shift_y)
                            terms.setdefault(shift_x, []).append((left, right, 0))
                rows = gather_terms(terms)
                conv[image, plane] = rows
                half_pre = scale_half(
                    rows, add, image, plane, row_of(demod, image), weights[...]
                )
                grad = read_plane(wide, qy, qx) + dot(colours[image, plane], colour_weights[image], 0, 0)
                row = row_of(demod, image) * row_of(valid, image)
                grad = grad * leaky_slope(half_pre) * row
                grad_conv[plane_at(image, plane), :] = grad.astype(BF16)
                product = column_sum(grad * rows)
                products = product if products is None else products + product
        square[pl.ds(image, 1), :] = square_grad(products, row_of(demod, image))

    each(own.shape[0], one)
    grad_conv[4 * PLANE * own.shape[0] :, :] = split_rows(square[...], 16)


def group_of(groups, tap):
    for index, (count, _) in enumerate(groups):
        if tap < count:
            return index, tap
        tap -= count


def first_taps(groups):
    return [sum(count for count, _ in groups[:index]) for index in range(len(groups))]


def add_term(groups, total, place, kernel, tap, column, lanes, terms, outs):
    group, at = group_of(groups, tap)
    axis = AT[groups[group][1][0]]
    send, keep = outs[2 * group : 2 * group + 2]
    half, share = send.shape[1], total.shape[1]
    columns = rows_at(column, share)
    for start, index, out in ((0, 1 - place[axis], send), (half, place[axis], keep)):
        rows = rows_at(index, half)
        weight = kernel[tap, rows, columns].astype(F32)
        value = total[start : start + half] + weight * terms[rows, :]
        out[at, :, lanes] = value.astype(out.dtype)


def shifted_kernel(scaled, moved):
    def one(image):
        for plane in range(scaled.shape[1]):
            value = scaled[image, plane].astype(F32)
            moved[image, plane] = columns_from(value, 1 if plane % 2 == 0 else -1).astype(BF16)

    each(scaled.shape[0], one)


def kernel_two_grad(place, scaled, moved, g_own, g_other, kernel, styles, *refs):
    outs, terms = refs[:-1], refs[-1]
    half = scaled.shape[3] // 2
    share = g_own.shape[1]
    squared = styles[1] * styles[1]
    for index, (column, grads) in enumerate(((place[2], g_own), (1 - place[2], g_other))):
        terms[...] = 2.0 * exact(squared, squares_behind(grads, scaled.shape[0]), 0, 0)
        for tap in range(9):
            tap_y, tap_x = tap // 3, tap % 3
            axis = AT[GROUPS_TWO[group_of(GROUPS_TWO, tap)[0]][1][0]]
            lanes = (rows_at(1 - place[axis], half), rows_at(place[axis], half))
            left, right = [], []
            for image in range(scaled.shape[0]):
                for qy in range(2):
                    for qx in range(2):
                        py, shift_y = source(qy, tap_y)
                        px, shift_x = source(qx, tap_x)
                        ref = scaled if shift_x == 0 else moved
                        value = jnp.concatenate([ref[image, 2 * py + px, :, at] for at in lanes], 1)
                        left.append(rows_from(value, shift_y))
                        right.append(grads[plane_at(image, 2 * qy + qx), :])
            total = dot(jnp.concatenate(left, 0), jnp.concatenate(right, 0), 0, 0)
            columns = slice(index * share, (index + 1) * share)
            add_term(GROUPS_TWO, total, place, kernel, tap, column, columns, terms, outs)


def kernel_one_grad(place, scaled, g_own, g_other, kernel, styles, *refs):
    outs, (moved, terms) = refs[:-2], refs[-2:]
    half = scaled.shape[2] // 2
    images, share = scaled.shape[0], g_own.shape[1]
    for image in range(images):
        moved[image] = columns_from(scaled[image].astype(F32), 1).astype(BF16)
    squared = styles[0] * styles[0]
    for index, (column, grads) in enumerate(((place[2], g_own), (1 - place[2], g_other))):
        terms[...] = 2.0 * exact(squared, squares_behind(grads, images), 0, 0)
        for qy in range(2):
            for qx in range(2):
                planes = [grads[plane_at(b, 2 * qy + qx), :] for b in range(images)]
                right = jnp.concatenate(planes, 0)
                for shift_y, tap_y in UP_TAPS[qy]:
                    for shift_x, tap_x in UP_TAPS[qx]:
                        tap = 3 * tap_y + tap_x
                        axis = AT[GROUPS_ONE[group_of(GROUPS_ONE, tap)[0]][1][0]]
                        lanes = (rows_at(1 - place[axis], half), rows_at(place[axis], half))
                        ref = moved if shift_x else scaled
                        left = [
                            rows_from(jnp.concatenate([ref[b, :, at] for at in lanes], 1), shift_y)
                            for b in range(images)
                        ]
                        total = dot(jnp.concatenate(left, 0), right, 0, 0)
                        columns = slice(index * share, (index + 1) * share)
                        add_term(GROUPS_ONE, total, place, kernel, tap, column, columns, terms, outs)


def input_two_grad(
    place,
    g_own,
    g_other,
    kernel,
    conv,
    demod,
    add,
    weights,
    styles,
    grad_scaled,
    grad_conv,
    square,
):
    share = g_own.shape[1]
    images = conv.shape[0]
    mine = pl.multiple_of(place[2] * share, share)
    theirs = pl.multiple_of((1 - place[2]) * share, share)

    def one(image):
        products = None
        for py in range(2):
            for px in range(2):
                plane = 2 * py + px
                terms = {}
                for tap_x in range(3):
                    qx = (px - tap_x + 1) & 1
                    shift_x = source(qx, tap_x)[1]
                    for tap_y in range(3):
                        qy = (py - tap_y + 1) & 1
                        shift_y = source(qy, tap_y)[1]
                        tap = 3 * tap_y + tap_x
                        for grads, start in ((g_own, mine), (g_other, theirs)):
                            left = rows_from(grads[plane_at(image, 2 * qy + qx), :], -shift_y)
                            right = kernel[tap, :, pl.ds(start, share)]
                            terms.setdefault(-shift_x, []).append((left, right, 1))
                rows = gather_terms(terms)
                grad_scaled[image, plane] = rows
                values = conv[image, plane]
                half_pre = scale_half(
                    values,
                    add,
                    image,
                    plane,
                    row_of(demod, image),
                    weights[...],
                )
                row = row_of(demod, image) * row_of(styles.at[1], image)
                grad = rows * leaky_slope(half_pre) * row
                grad_conv[plane_at(image, plane), :] = grad.astype(BF16)
                product = column_sum(grad * values)
                products = product if products is None else products + product
        square[pl.ds(image, 1), :] = square_grad(products, row_of(demod, image))

    each(images, one)
    grad_conv[4 * PLANE * images :, :] = split_rows(square[...], 16)


def input_one_grad(
    place, g_own, g_other, kernel, features, styles, grad_features, sums
):
    share = g_own.shape[1]
    mine = pl.multiple_of(place[2] * share, share)
    theirs = pl.multiple_of((1 - place[2]) * share, share)
    images = features.shape[0]
    terms = {}
    for qy in range(2):
        for qx in range(2):
            for shift_y, tap_y in UP_TAPS[qy]:
                for shift_x, tap_x in UP_TAPS[qx]:
                    tap = 3 * tap_y + tap_x
                    for grads, start in ((g_own, mine), (g_other, theirs)):
                        left = jnp.concatenate(
                            [
                                rows_from(grads[plane_at(b, 2 * qy + qx), :], -shift_y)
                                for b in range(images)
                            ], 0
                        )
                        right = kernel[tap, :, pl.ds(start, share)]
                        terms.setdefault(-shift_x, []).append((left, right, 1))
    total = gather_terms(terms)
    for image in range(images):
        rows = total[image * PLANE : (image + 1) * PLANE]
        grad_features[image] = rows * styles[0, image : image + 1, :]
        product = rows * features[image].astype(F32)
        sums[image : image + 1, :] = jnp.sum(product, axis=0, keepdims=True)


def noise_rows(add, image, plane, share):
    pick = lax.broadcasted_iota(jnp.int32, (add.shape[2], share), 0) < 3
    return dot(add[image, plane], jnp.where(pick, 1.0, 0.0).astype(BF16), 0, 0)


def point_sums(image, totals, out):
    for row, total in enumerate(totals):
        out[image, row : row + 1, :] = total
    out[image, len(totals) :, :] = jnp.zeros((8 - len(totals), out.shape[2]), F32)


def outputs_two_kernel(
    conv,
    demod,
    valid,
    add,
    weights,
    colours,
    cotangent,
    styles,
    rgb,
    features_out,
    rgb_rows,
    rgb_grad,
    sums,
    wide,
):
    share = conv.shape[3]
    rgb_grad[...] = jnp.zeros_like(rgb_grad)

    def one(image):
        spread(cotangent, image, wide)
        totals = None
        for plane in range(4):
            qy, qx = plane // 2, plane % 2
            rows = conv[image, plane]
            half_pre = scale_half(rows, add, image, plane, row_of(demod, image), weights[...])
            act = smooth_leaky(half_pre)
            style = row_of(styles.at[2], image)
            keep = row_of(valid, image)
            from_rgb = dot(colours[image, plane], rgb[...], 0, 0)
            grad = (read_plane(wide, qy, qx) + from_rgb * style) * keep * leaky_slope(half_pre)
            write_plane(wide, qy, qx, act * keep)
            to_rgb = (act * style).astype(BF16)
            rgb_rows[image, plane] = dot(rgb[...], to_rgb, 1, 1)[:8]
            rgb_grad[...] += dot(colours[image, plane], to_rgb, 1, 0)
            own = [
                column_sum(grad),
                column_sum(grad * noise_rows(add, image, plane, share)),
                column_sum(from_rgb * act),
                column_sum(act * act) * keep,
            ]
            totals = own if totals is None else [a + b for a, b in zip(totals, own)]
        store_raster(wide, features_out, image)
        point_sums(image, totals, sums)

    each(conv.shape[0], one)


def outputs_one_kernel(
    conv, grad_scaled, demod, valid, add, weights, styles, sums
):
    share = conv.shape[3]

    def one(image):
        totals = None
        for plane in range(4):
            rows = conv[image, plane]
            half_pre = scale_half(rows, add, image, plane, row_of(demod, image), weights[...])
            act = smooth_leaky(half_pre)
            back = grad_scaled[image, plane]
            grad = back * row_of(styles.at[1], image) * leaky_slope(half_pre)
            own = [
                column_sum(grad),
                column_sum(grad * noise_rows(add, image, plane, share)),
                column_sum(back * act),
                column_sum(act * act) * row_of(valid, image),
            ]
            totals = own if totals is None else [a + b for a, b in zip(totals, own)]
        point_sums(image, totals, sums)

    each(conv.shape[0], one)


def upsampling(rows, cols):
    line = lax.broadcasted_iota(jnp.int32, (rows, cols), 0)
    column = lax.broadcasted_iota(jnp.int32, (rows, cols), 1)
    centre, near = line // 2, line // 2 + 2 * (line % 2) - 1
    return jnp.where(column == centre, 0.75, 0.0) + jnp.where(column == near, 0.25, 0.0)


def rgb_kernel(
    valid, bias, own, other, rgb_in, grad_rgb, rgb_out, grad_in, grad_latent, pack, raster
):
    images = rgb_in.shape[0]
    double = upsampling(RES, HALF)
    lane = lax.broadcasted_iota(jnp.int32, (HALF, PLANE), 1)
    line = lax.broadcasted_iota(jnp.int32, (HALF, PLANE), 0)
    mask = jnp.where(lane // HALF == line, 1.0, 0.0)
    for qx in range(2):
        pixel = lax.broadcasted_iota(jnp.int32, (PLANE, 128), 0) % HALF
        column = lax.broadcasted_iota(jnp.int32, (PLANE, 128), 1)
        choose = jnp.where(column == 2 * pixel + qx, 1.0, 0.0)
        for qy in range(2):
            plane = 2 * qy + qx
            rows = []
            for image in range(images):
                rows_here = rows_at(1 + 4 * image + plane, 8)
                both = own[rows_here, :] + other[rows_here, :]
                rows += [mask * both[colour : colour + 1] for colour in range(3)]
            found = exact(jnp.concatenate(rows, 0), choose, 1, 0)
            for index in range(3 * images):
                cell = found[HALF * index : HALF * (index + 1)]
                place = (index, pl.ds(qy, HALF, stride=2), slice(None))
                raster[place] = cell if qx == 0 else raster[place] + cell
    squares = jnp.zeros((1, 1), F32)
    biases = [jnp.zeros((1, 1), F32) for _ in range(3)]
    for image in range(images):
        keep = valid[image : image + 1, :RES]
        for colour in range(3):
            skip = exact(exact(double, rgb_in[image, colour], 1, 0), double, 1, 1)
            value = (skip + raster[3 * image + colour, :, :RES]) + bias[:, colour : colour + 1]
            value = value * keep
            rgb_out[image, colour] = value
            squares = squares + jnp.sum(value * value, keepdims=True)
            grad = grad_rgb[image, colour].astype(F32) * keep
            grad_in[image, colour] = exact(exact(double, grad, 0, 0), double, 1, 0)
            biases[colour] = biases[colour] + jnp.sum(grad, keepdims=True)
    total = own[:8, :] + other[:8, :]
    for image in range(images):
        grad_latent[image : image + 1, :] = jnp.concatenate(
            [total[2 * image : 2 * image + 1], total[2 * image + 1 : 2 * image + 2]], 1
        )
    scalars = total[2 * images : 2 * images + 1]
    lane = lax.broadcasted_iota(jnp.int32, scalars.shape, 1)
    for index, value in enumerate([squares] + biases):
        scalars = scalars + jnp.where(lane == 4 + index, value, 0.0)
    for image in range(images):
        scalars = scalars + jnp.where(lane == 8, valid[image : image + 1, :], 0.0)
    pack[...] = jnp.concatenate([scalars, jnp.zeros((15, scalars.shape[1]), F32)], 0)


def style_grads_kernel(
    place,
    own_one,
    other_one,
    own_two,
    other_two,
    squares_one,
    squares_two,
    styles,
    style_sums,
    sums_one,
    sums_two,
    a1,
    a2,
    a3,
    latent,
    rgb_grad,
    planes,
    pack,
    crossing,
):
    images, share = style_sums.shape
    mine, theirs = rows_at(place[2], share), rows_at(1 - place[2], share)
    rows = []
    for layer, (own, other, squares, sums) in enumerate(
        ((own_one, other_one, squares_one, style_sums), (own_two, other_two, squares_two, None))
    ):
        back = exact(squares_behind(own, images), squares[:, mine], 1, 1) + exact(
            squares_behind(other, images), squares[:, theirs], 1, 1
        )
        if sums is None:
            direct = jnp.concatenate([sums_one[b, 2:3, :] for b in range(images)], 0)
        else:
            direct = sums[...]
        rows.append(direct + 2.0 * styles[layer] * back)
    rows.append(jnp.concatenate([sums_two[b, 2:3, :] for b in range(images)], 0))
    grad_latent = None
    for row, affine in zip(rows, (a1, a2, a3)):
        part = exact(row, affine[...].astype(F32), 1, 1)
        grad_latent = part if grad_latent is None else grad_latent + part
    lane = lax.broadcasted_iota(jnp.int32, (1, share), 1)
    scalars = jnp.zeros((1, share), F32)
    for index, (sums, row) in enumerate(
        ((sums_one, 3), (sums_two, 3), (sums_one, 1), (sums_two, 1))
    ):
        total = sums[0, row : row + 1, :]
        for image in range(1, images):
            total = total + sums[image, row : row + 1, :]
        scalars = scalars + jnp.where(lane == index, jnp.sum(total, keepdims=True), 0.0)
    pieces = [grad_latent[b : b + 1, h * share : (h + 1) * share] for b in range(images) for h in (0, 1)]
    blank = jnp.zeros((8 - len(pieces) - 1, share), F32)
    crossing[:8, :] = jnp.concatenate(pieces + [scalars, blank], 0)
    for image in range(images):
        for plane in range(4):
            crossing[rows_at(1 + 4 * image + plane, 8), :] = planes[image, plane]
    values = latent[...].astype(F32)
    packed = [values[:, :share], values[:, share:]] + rows
    for sums in (sums_one, sums_two):
        bias = sums[0, 0:1, :]
        for image in range(1, images):
            bias = bias + sums[image, 0:1, :]
        packed.append(bias)
    packed += [rgb_grad[:3, :], jnp.zeros((1, share), F32)]
    pack[...] = jnp.concatenate(packed, 0)


def relay_kernel(source, out):
    out[...] = source[...]


def collect(place, packs, groups, everything):
    if len(packs) == 1:
        everything[...] = packs[0][...]
        return
    taps, order = groups[0]
    weight = {"far": 8, "near": 4, "y": 2, "x": 1}
    rows, share = everything.shape[1:]
    for index in range(8):
        at = pl.ds(rows * index, rows)
        device = (
            weight["far"] * (index & 1)
            + weight[order[2]] * ((index >> 1) & 1)
            + weight[order[1]] * (index >> 2)
        )
        mine = place[AT[order[0]]]
        for ref, first in zip(packs, (mine, 1 - mine)):
            both = ref[taps, at, :].astype(F32)
            everything[device + weight[order[0]] * first] = both[:, :share] + both[:, share:]


def spread_kernel(place, *refs, images, groups):
    packs, outs, everything = refs[:-10], refs[-10:-1], refs[-1]
    collect(place, packs, groups, everything)
    count = everything.shape[0]

    def rows(start, size):
        return jnp.concatenate([everything[d, start : start + size, :] for d in range(count)], 0)

    latent = jnp.concatenate([rows(0, images), rows(images, images)], 1)
    at = 2 * images
    for layer in range(3):
        grad = rows(at, images)
        outs[layer][...] = exact(latent, grad, 0, 0)
        outs[3 + layer][...] = jnp.sum(grad, axis=0, keepdims=True)
        at += images
    total = everything[0]
    for device in range(1, count):
        total = total + everything[device]
    outs[6][...] = total[at : at + 1]
    outs[7][...] = total[at + 1 : at + 2]
    outs[8][...] = total[at + 2 : at + 5]


def scalars_kernel(place, *refs, groups):
    packs, (gains, rms, rgb_bias, everything) = refs[:-4], refs[-4:]
    collect(place, packs, groups, everything)
    scalars = everything[0, 0:1, :]
    for device in range(1, everything.shape[0]):
        scalars = scalars + everything[device, 0:1, :]
    lane = lax.broadcasted_iota(jnp.int32, scalars.shape, 1)
    share = scalars.shape[1]
    real = jnp.sum(jnp.where(lane == 8, scalars, 0.0), keepdims=True)
    entries = jnp.where(lane == 4, 3.0 * RES * RES, 2.0 * share * RES * RES)
    roots = jnp.sqrt(jnp.abs(scalars) / (real * entries))

    def pick(values, index):
        return jnp.sum(jnp.where(lane == index, values, 0.0))

    for index, at in enumerate((0, 1, 4)):
        rms[index] = pick(roots, at)
    for index in range(2):
        gains[index] = pick(scalars, 2 + index)
    for index in range(3):
        rgb_bias[index] = pick(scalars, 5 + index)


def fold_kernel(place, *refs, groups, stage):
    count = len(groups)
    sources, outs = refs[: 2 * count], refs[2 * count :]
    for group, (taps, order) in enumerate(groups):
        kept, got = sources[2 * group : 2 * group + 2]
        send, keep = outs[2 * group : 2 * group + 2]
        index = place[AT[order[stage]]]
        away, here = rows_at(1 - index, send.shape[1]), rows_at(index, send.shape[1])

        def one(tap, kept=kept, got=got, send=send, keep=keep, away=away, here=here):
            total = kept[tap, away, :] + got[tap, away, :].astype(F32)
            send[tap] = total.astype(BF16)
            keep[tap] = kept[tap, here, :] + got[tap, here, :].astype(F32)

        each(kept.shape[0], one)


def put_pack(out, tap, place_far, pack):
    for order, part in enumerate(split_three(pack[...])[:2]):
        columns = slice(order * pack.shape[1], (order + 1) * pack.shape[1])
        out[tap, rows_at(place_far, pack.shape[0]), columns] = part


def across_kernel(place, *refs, groups):
    out = refs[-1]
    for group, first in enumerate(first_taps(groups)):
        kept, got = refs[2 * group : 2 * group + 2]

        def one(tap, kept=kept, got=got, first=first):
            out[first + tap] = (kept[tap] + got[tap].astype(F32)).astype(BF16)

        each(kept.shape[0], one)
    if len(refs) > 2 * len(groups) + 1:
        out[9] = jnp.zeros(out.shape[1:], BF16)
        put_pack(out, 9, place[4], refs[-2])


def total_kernel(place, mine, got, *refs, groups):
    packs, outs = refs[: -len(groups)], refs[-len(groups) :]
    extra = groups[0][0]
    for index, pack in enumerate(packs):
        put_pack(outs[0], extra, place[4] if index == 0 else 1 - place[4], pack)
    if mine.shape[0] > 9:
        outs[0][extra] = (mine[9].astype(F32) + got[9].astype(F32)).astype(BF16)
    for out, first, (taps, _) in zip(outs, first_taps(groups), groups):

        def one(tap, out=out, first=first):
            total = mine[first + tap].astype(F32) + got[first + tap].astype(F32)
            out[tap] = total.astype(BF16)

        each(taps, one)


def join_kernel(place, *refs, groups, stage):
    count = len(groups)
    sources, outs = refs[: 2 * count], refs[2 * count :]
    for group, (taps, order) in enumerate(groups):
        own, got = sources[2 * group : 2 * group + 2]
        out = outs[group]
        index = place[AT[order[stage]]]
        here, away = rows_at(index, own.shape[1]), rows_at(1 - index, own.shape[1])

        def one(tap, own=own, got=got, out=out, here=here, away=away):
            out[tap, here, :] = own[tap]
            out[tap, away, :] = got[tap]

        each(out.shape[0], one)


def finish_kernel(place, *refs, groups, away, between=None):
    parts, (out, held, sems) = refs[: len(groups)], refs[-3:]
    _, half, channels = held.shape
    share = channels // 2
    starts = first_taps(groups)
    for part, first, (taps, order) in zip(parts, starts, groups):
        index = place[AT[order[0]]]
        rows = rows_at(1 - index if away else index, half)

        def copy(tap, rows=rows):
            return pltpu.make_async_copy(held.at[tap], out.at[tap, rows, :], sems.at[tap])

        def one(tap, part=part, first=first, copy=copy):
            for side, column in enumerate((place[2], 1 - place[2])):
                value = part[tap, :, side * share : (side + 1) * share]
                held[first + tap, :, rows_at(column, share)] = value.astype(F32)
            copy(first + tap).start()

        each(taps, one)
    if between is not None:
        between()
    for first, (taps, order) in zip(starts, groups):
        index = place[AT[order[0]]]
        rows = rows_at(1 - index if away else index, half)

        def last(tap, rows=rows, first=first):
            pltpu.make_async_copy(
                held.at[first + tap], out.at[first + tap, rows, :], sems.at[first + tap]
            ).wait()

        each(taps, last)


def finish_scalars_kernel(place, *refs, groups):
    count = len(groups)
    parts, own, (out, gains, rms, rgb_bias, held, sems, everything) = (
        refs[:count],
        refs[count + 1],
        refs[-7:],
    )

    def between():
        scalars_kernel(place, own, parts[0], gains, rms, rgb_bias, everything, groups=groups)

    finish_kernel(place, *parts, out, held, sems, groups=groups, away=True, between=between)


def call(body, outs, scratch=(), smem=0, after=(), hbm=(), scalars=(), plain=(), loose=(), whole=(), micros=0, aliases=None):
    outs = outs if isinstance(outs, tuple) else (outs,)
    any_space = pl.BlockSpec(memory_space=pl.ANY)

    def run(*operands):
        count = len(operands)
        spaces = [pltpu.SMEM] * smem + [pltpu.VMEM] * (count - smem)
        for index in loose + whole:
            spaces[index] = pltpu.HBM
        values = [pltpu.with_memory_space_constraint(*pair) for pair in zip(operands, spaces)]

        def inner(*refs):
            body(*refs[:count], *refs[count + len(after) : -1 - len(scratch)], *refs[len(refs) - len(scratch) :])

        results = pl.pallas_call(
            inner,
            out_shape=tuple(
                member if index in hbm + scalars + plain else pltpu.VMEM(member.shape, member.dtype)
                for index, member in enumerate(outs)
            )
            + (shape(8, 128),),
            in_specs=[SMEM] * smem
            + [any_space if index in whole or index in (aliases or {}) else VMEM for index in range(smem, count)]
            + [any_space] * len(after),
            out_specs=tuple(
                any_space if index in hbm else SMEM if index in scalars else VMEM
                for index in range(len(outs))
            )
            + (any_space,),
            scratch_shapes=scratch,
            input_output_aliases=aliases or {},
            name=getattr(body, "func", body).__name__,
            compiler_params=pltpu.CompilerParams(vmem_limit_bytes=VMEM_BYTES),
            cost_estimate=pl.CostEstimate(
                flops=2**10 + int(micros * 1.1e9), bytes_accessed=2**10, transcendentals=0
            ),
        )(*values, *after)
        found, token = results[:-1], results[-1]
        return (found if len(found) > 1 else found[0]), token

    return run


def shape(*dims, kind=F32):
    return jax.ShapeDtypeStruct(dims, kind)


def group_shapes(groups, rows, cols):
    found = ()
    for taps, _ in groups:
        found += (shape(taps, rows, cols, kind=BF16), shape(taps, rows, cols))
    return found


def swap(values, axis_name):
    return lax.ppermute(values, axis_name, SWAP)


def part_of(values, axis, index, size):
    return lax.dynamic_slice_in_dim(values, index * size, size, axis)


def place_pair(index, own, other, axis):
    return jnp.where(
        index == 0,
        jnp.concatenate([own, other], axis=axis),
        jnp.concatenate([other, own], axis=axis),
    )


class Reduction:
    def __init__(self, place, groups, parts):
        self.place, self.groups = place, groups
        self.exchange(parts[0::2], 0)
        self.keep = parts[1::2]

    def exchange(self, parts, stage):
        self.got = [swap(part, order[stage]) for part, (_, order) in zip(parts, self.groups)]

    def pairs(self, own):
        return [member for pair in zip(own, self.got) for member in pair]

    def fold(self, token, stage, micros=STAGE):
        _, rows, cols = self.keep[0].shape
        parts, token = call(
            functools.partial(fold_kernel, groups=self.groups, stage=stage),
            group_shapes(self.groups, rows // 2, cols),
            smem=1,
            after=token if isinstance(token, tuple) else (token,),
            micros=micros,
        )(self.place, *self.pairs(self.keep))
        self.exchange(parts[0::2], stage)
        self.keep = parts[1::2]
        return token

    def across(self, token, *packs, micros=STAGE):
        _, rows, cols = self.keep[0].shape
        self.own, token = call(
            functools.partial(across_kernel, groups=self.groups),
            shape(9 + len(packs), rows, cols, kind=BF16),
            smem=1,
            after=token if isinstance(token, tuple) else (token,),
            micros=micros,
        )(self.place, *self.pairs(self.keep), *packs)
        self.got = swap(self.own, "far")
        return token

    def total(self, token, *packs, micros=STAGE):
        if lax.axis_size("block") > 1:
            self.own = lax.psum(self.own.astype(F32) + self.got.astype(F32), "block").astype(BF16)
            self.got = jnp.zeros_like(self.own)
        taps, rows, cols = self.own.shape
        outs = [shape(count, rows, cols, kind=BF16) for count, _ in self.groups]
        if packs or taps > 9:
            outs[0] = shape(self.groups[0][0] + 1, rows, cols, kind=BF16)
        self.own, token = call(
            functools.partial(total_kernel, groups=self.groups),
            tuple(outs),
            smem=1,
            after=token if isinstance(token, tuple) else (token,),
            micros=micros,
        )(self.place, self.own, self.got, *packs)
        self.exchange(self.own, 2)
        return token

    def join(self, token, stage, micros=STAGE):
        outs = tuple(
            shape(part.shape[0], 2 * part.shape[1], part.shape[2], kind=BF16) for part in self.own
        )
        self.own, token = call(
            functools.partial(join_kernel, groups=self.groups, stage=stage),
            outs,
            smem=1,
            after=token if isinstance(token, tuple) else (token,),
            micros=micros,
        )(self.place, *self.pairs(self.own))
        self.exchange(self.own, stage - 1)
        return token

    def finish_half(self, token, parts, out, away):
        _, half, cols = parts[0].shape
        last = 1 + len(parts)
        return call(
            functools.partial(finish_kernel, groups=self.groups, away=away),
            shape(9, 2 * half, cols),
            [pltpu.VMEM((9, half, cols), F32), pltpu.SemaphoreType.DMA((9,))],
            smem=1,
            after=token if isinstance(token, tuple) else (token,),
            hbm=(0,),
            loose=(last,) if out else (),
            aliases={last: 0} if out else None,
            micros=0,
        )(self.place, *parts, *out)

    def finish_own(self, token):
        return self.finish_half(token, self.own, (), False)

    def finish(self, token, out):
        return self.finish_half(token, self.got, (out,), True)

    def finish_scalars(self, token, out, devices):
        _, half, cols = self.got[0].shape
        last = 1 + len(self.got)
        return call(
            functools.partial(finish_scalars_kernel, groups=self.groups),
            (shape(9, 2 * half, cols), shape(2), shape(3), shape(3)),
            [
                pltpu.VMEM((9, half, cols), F32),
                pltpu.SemaphoreType.DMA((9,)),
                pltpu.VMEM((devices, 16, cols // 2), F32),
            ],
            smem=1,
            after=(token,),
            hbm=(0,),
            scalars=(1, 2, 3),
            loose=(last,),
            aliases={last: 0},
        )(self.place, *self.got, out, self.own[0])


def gather_packs(pack):
    for axis_name in DP[::-1]:
        pack = lax.all_gather(pack[None] if pack.ndim == 2 else pack, axis_name, axis=0, tiled=True)
    return pack


def per_device(
    counts,
    features_in,
    rgb_in,
    latent,
    affine_one,
    affine_bias_one,
    affine_two,
    affine_bias_two,
    affine_three,
    affine_bias_three,
    kernel_one,
    bias_one,
    kernel_two,
    bias_two,
    rgb_weight,
    rgb_bias,
    noise_gain,
    noise_one,
    noise_two,
    grad_features,
    grad_rgb,
):
    images, share = features_in.shape[0], features_in.shape[3]
    channels = share * lax.axis_size("chan")
    me = lax.axis_index("chan")
    place = jnp.stack([lax.axis_index(name) for name in ("x", "y", "chan", "near", "far")])
    place = place.astype(jnp.int32)
    valid = (jnp.arange(images, dtype=jnp.int32) < counts[0]).astype(F32)
    valid_rows = jnp.broadcast_to(valid[:, None], (images, share))
    features = features_in.reshape(images, PLANE, share)
    flat_one = kernel_one.reshape(9, share, channels)
    flat_two = kernel_two.reshape(9, share, channels)
    plane_shape = (images, 4, PLANE, share)
    grad_kind = shape(images * 4 * PLANE + 16, share, kind=BF16)
    half = share // 2
    wide = pltpu.VMEM((share // 128, HALF, 2, RES, 128), F32)

    send_kind = shape(9, share, share, kind=BF16)
    (styles, scaled_one, send_one), token = call(
        style_kernel,
        (
            shape(3, images, share),
            shape(images, PLANE, share, kind=BF16),
            send_kind,
        ),
        [pltpu.SemaphoreType.DMA],
        smem=1,
        loose=tuple(range(2, 10)),
        whole=(1,),
    )(
        place,
        flat_one,
        latent,
        affine_one,
        affine_bias_one.reshape(1, -1),
        affine_two,
        affine_bias_two.reshape(1, -1),
        affine_three,
        affine_bias_three.reshape(1, -1),
        features,
    )
    received_one = swap(send_one, "chan")
    scaled_one_other = swap(scaled_one, "chan")

    def layer_squares(layer, kernel, bias, token):
        (squares, mine, theirs, add, colour), token = call(
            functools.partial(squares_kernel, layer=layer),
            (
                shape(share, channels),
                shape(images, share),
                shape(images, share),
                shape(16, share, kind=BF16),
                shape(images, 16, share, kind=BF16),
            ),
            [pltpu.VMEM((images, channels), F32)],
            smem=1,
            after=(token,),
            loose=(3, 4),
        )(place, styles, kernel, bias.reshape(1, -1), rgb_weight)
        return squares, mine, swap(theirs, "chan"), add, colour, token

    squares_one, mine_one, theirs_one, add_one, _, token = layer_squares(
        0, flat_one, bias_one, token
    )
    (noise_planes_one, noise_planes_two, colours, send_two), token = call(
        planes_kernel,
        (shape(images, 4, 16, PLANE, kind=BF16),) * 3 + (send_kind,),
        [pltpu.SemaphoreType.DMA],
        smem=1,
        after=(token,),
        loose=(2, 4, 5, 6),
        whole=(3,),
    )(place, valid_rows, noise_gain.reshape(1, -1), flat_two, noise_one, noise_two, grad_rgb)
    received_two = swap(send_two, "chan")
    rgb_rows_in = jnp.pad(rgb_weight, ((0, 13), (0, 0)))

    (conv_one, scaled_two, demod_one), token = call(
        conv_one_kernel,
        (shape(*plane_shape), shape(*plane_shape, kind=BF16), shape(images, share)),
        smem=1,
        after=(token,),
        micros=STAGE,
    )(
        place,
        scaled_one,
        scaled_one_other,
        flat_one,
        received_one,
        mine_one,
        theirs_one,
        noise_planes_one,
        add_one,
        styles,
    )
    scaled_two_other = swap(scaled_two, "chan")
    squares_two, mine_two, theirs_two, add_two, colour_weights, token = layer_squares(
        1, flat_two, bias_two, token
    )
    (conv_two, grad_conv_two, demod_two), token = call(
        conv_two_kernel,
        (shape(*plane_shape), grad_kind, shape(images, share)),
        [wide, pltpu.VMEM((images, share), F32)],
        smem=1,
        after=(token,),
    )(
        place,
        scaled_two,
        scaled_two_other,
        flat_two,
        received_two,
        mine_two,
        theirs_two,
        valid_rows,
        noise_planes_two,
        add_two,
        colours,
        colour_weights,
        grad_features,
    )
    grad_conv_two_other = swap(grad_conv_two, "chan")
    shifted_two, token = call(
        shifted_kernel, shape(*plane_shape, kind=BF16), after=(token,)
    )(scaled_two)
    devices = lax.axis_size(DP)
    alone = lax.axis_size("block") == 1
    parts_two, token = call(
        kernel_two_grad,
        group_shapes(GROUPS_TWO, half, channels),
        [pltpu.VMEM((share, share), F32)],
        smem=1,
        after=(token,),
    )(
        place,
        scaled_two,
        shifted_two,
        grad_conv_two,
        grad_conv_two_other,
        flat_two,
        styles,
    )
    reduce_two = Reduction(place, GROUPS_TWO, parts_two)
    (grad_scaled_two, grad_conv_one), token = call(
        input_two_grad,
        (shape(*plane_shape), grad_kind),
        [pltpu.VMEM((images, share), F32)],
        smem=1,
        after=(token,),
    )(
        place,
        grad_conv_two,
        grad_conv_two_other,
        flat_two,
        conv_one,
        demod_one,
        noise_planes_one,
        add_one,
        styles,
    )
    grad_conv_one_other = swap(grad_conv_one, "chan")
    sums_one, token = call(
        outputs_one_kernel, shape(images, 8, share), after=(token,)
    )(
        conv_one,
        grad_scaled_two,
        demod_one,
        valid_rows,
        noise_planes_one,
        add_one,
        styles,
    )
    token = reduce_two.fold(token, 1)
    (grad_features_in, style_sums), token = call(
        input_one_grad,
        (shape(images, PLANE, share), shape(images, share)),
        smem=1,
        after=(token,),
        plain=(0,),
        loose=(4,),
    )(place, grad_conv_one, grad_conv_one_other, flat_one, features, styles)
    token = reduce_two.fold(token, 2)
    parts_one, token = call(
        kernel_one_grad,
        group_shapes(GROUPS_ONE, half, channels),
        [pltpu.VMEM((images, PLANE, share), BF16), pltpu.VMEM((share, share), F32)],
        smem=1,
        after=(token,),
        micros=STAGE,
    )(place, scaled_one, grad_conv_one, grad_conv_one_other, flat_one, styles)
    reduce_one = Reduction(place, GROUPS_ONE, parts_one)
    token = reduce_two.across(token)
    (features_out, rgb_planes, rgb_grad, sums_two), token = call(
        outputs_two_kernel,
        (
            shape(images, RES, RES, share, kind=BF16),
            shape(images, 4, 8, PLANE),
            shape(16, share),
            shape(images, 8, share),
        ),
        [wide],
        after=(token,),
        plain=(0,),
        loose=(6,),
    )(
        conv_two,
        demod_two,
        valid_rows,
        noise_planes_two,
        add_two,
        colours,
        grad_features,
        styles,
        rgb_rows_in,
    )
    (pack, crossing), token = call(
        style_grads_kernel,
        (shape(16, share), shape(8 + 32 * images, share)),
        smem=1,
        after=(token,),
        loose=(11, 12, 13),
    )(
        place,
        grad_conv_one,
        grad_conv_one_other,
        grad_conv_two,
        grad_conv_two_other,
        squares_one,
        squares_two,
        styles,
        style_sums,
        sums_one,
        sums_two,
        affine_one,
        affine_two,
        affine_three,
        latent,
        rgb_grad,
        rgb_planes,
    )
    packs = [pack, swap(pack, "far")] if alone else []
    token = reduce_one.fold(token, 1, micros=0)
    token = reduce_two.total(token, *packs)
    token = reduce_one.fold(token, 2)
    token = reduce_two.join(token, 2)
    token = reduce_one.across(token)
    relayed, token = call(relay_kernel, shape(8 + 32 * images, share), after=(token,))(crossing)
    crossing_other = swap(relayed, "chan")
    token = reduce_two.join(token, 1)
    (rgb_out, grad_rgb_in, grad_latent, scalars), token = call(
        rgb_kernel,
        (
            shape(*grad_rgb.shape),
            shape(*rgb_in.shape),
            shape(images, channels),
            shape(16, share),
        ),
        [pltpu.VMEM((3 * images, RES, 128), F32)],
        after=(token,),
        plain=(0, 1, 2),
        loose=(1, 4, 5),
    )(valid_rows, rgb_bias.reshape(1, -1), crossing, crossing_other, rgb_in, grad_rgb)
    rows = [scalars, swap(scalars, "far")] if alone else []
    sum_two, token = reduce_two.finish_own(token)
    token = reduce_one.total(token, *rows)
    sum_two, token = reduce_two.finish(token, sum_two)
    token = reduce_one.join(token, 2)
    if alone:
        packs = [reduce_two.own[0], reduce_two.got[0]]
    else:
        packs = [gather_packs(pack)]
    spread_out, token = call(
        functools.partial(spread_kernel, images=images, groups=GROUPS_TWO),
        (shape(channels, share),) * 3 + (shape(1, share),) * 5 + (shape(3, share),),
        [pltpu.VMEM((devices, 16, share), F32)],
        smem=1,
        after=(token,),
        plain=tuple(range(9)),
    )(place, *packs)
    token = reduce_one.join(token, 1)
    sum_one, token = reduce_one.finish_own(token)
    affine_grads, affine_biases, points = spread_out[0:3], spread_out[3:6], spread_out[6:8]
    rgb_total = spread_out[8]
    if alone:
        found, token = reduce_one.finish_scalars(token, sum_one, devices)
        sum_one, gains, rms_values, rgb_bias_grad = found
    else:
        rows = [gather_packs(scalars)]
        (gains, rms_values, rgb_bias_grad), token = call(
            functools.partial(scalars_kernel, groups=GROUPS_ONE),
            (shape(2), shape(3), shape(3)),
            [pltpu.VMEM((devices, 16, share), F32)],
            smem=1,
            after=(token,),
            scalars=(0, 1, 2),
        )(place, *rows)
        sum_one, token = reduce_one.finish(token, sum_one)
    affine_outs = []
    for grad, bias in zip(affine_grads, affine_biases):
        affine_outs += [grad, bias.reshape(-1)]
    return (
        features_out,
        rgb_out,
        grad_features_in.reshape(features_in.shape),
        grad_rgb_in,
        grad_latent,
        *affine_outs,
        sum_one.reshape(kernel_one.shape),
        points[0].reshape(-1),
        sum_two.reshape(kernel_two.shape),
        points[1].reshape(-1),
        rgb_total,
        rgb_bias_grad,
        gains,
        rms_values,
    )


def solution(mesh):
    blocks = mesh.shape["dp"] // 16
    grid = mesh.devices.reshape(blocks, 2, 2, 2, 2, mesh.shape["chan"])
    split_mesh = Mesh(grid, DP + ("chan",))
    in_specs = (
        P(DP),
        P(DP, None, None, "chan"),
        P(DP, None, None, None),
        P(DP, None),
        P(None, "chan"),
        P("chan"),
        P(None, "chan"),
        P("chan"),
        P(None, "chan"),
        P("chan"),
        P(None, None, "chan", None),
        P("chan"),
        P(None, None, "chan", None),
        P("chan"),
        P(None, "chan"),
        P(),
        P(),
        P(DP, None, None),
        P(DP, None, None),
        P(DP, None, None, "chan"),
        P(DP, None, None, None),
    )
    out_specs = (
        P(DP, None, None, "chan"),
        P(DP, None, None, None),
        P(DP, None, None, "chan"),
        P(DP, None, None, None),
        P(DP, None),
        P(None, "chan"),
        P("chan"),
        P(None, "chan"),
        P("chan"),
        P(None, "chan"),
        P("chan"),
        P(None, None, "chan", None),
        P("chan"),
        P(None, None, "chan", None),
        P("chan"),
        P(None, "chan"),
        P(),
        P(),
        P(),
    )
    return jax.shard_map(
        per_device, mesh=split_mesh, in_specs=in_specs, out_specs=out_specs, check_vma=False
    )
```

```python
import functools

import jax
import jax.numpy as jnp
from jax import lax
from jax.experimental import pallas as pl
from jax.experimental.pallas import tpu as pltpu
from jax.sharding import Mesh, PartitionSpec as P

RES = 32
HALF = 16
PLANE = HALF * HALF
SQRT_TWO = 1.4142135623730951
EPSILON = 1e-08
STAGE = 60
DP = ("block", "far", "near", "y", "x")
SWAP = [(0, 1), (1, 0)]
F32 = jnp.float32
BF16 = jnp.bfloat16
VMEM_BYTES = 16 * 2**20
VMEM = pl.BlockSpec(memory_space=pltpu.VMEM)
SMEM = pl.BlockSpec(memory_space=pltpu.SMEM)
UP_TAPS = (((0, 1),), ((0, 0), (1, 2)))


GROUPS_TWO = ((3, ("x", "y", "near")), (3, ("y", "near", "x")), (3, ("near", "x", "y")))
GROUPS_ONE = ((3, ("x", "y", "near")), (3, ("y", "near", "x")), (3, ("near", "x", "y")))
AT = {"x": 0, "y": 1, "chan": 2, "near": 3, "far": 4}


def dot(left, right, left_dim, right_dim):
    return lax.dot_general(
        left, right, (((left_dim,), (right_dim,)), ((), ())), preferred_element_type=F32
    )


def exact(left, right, left_dim, right_dim):
    return lax.dot_general(
        left,
        right,
        (((left_dim,), (right_dim,)), ((), ())),
        precision=lax.Precision.HIGHEST,
        preferred_element_type=F32,
    )


def source(parity, tap):
    return (parity + tap - 1) & 1, (parity + tap - 1) >> 1


def each(count, body):
    lax.fori_loop(0, count, lambda index, carry: (body(index), carry)[1], 0)


def row_of(ref, index):
    return ref[pl.ds(index, 1), :]


def rows_at(index, count):
    return pl.ds(pl.multiple_of(index * count, count), count)


def plane_at(image, plane):
    return rows_at(4 * image + plane, PLANE)


def squares_behind(ref, images):
    parts = ref[ref.shape[0] - 16 :, :].astype(F32)
    return jnp.concatenate(
        [jnp.sum(parts[3 * b : 3 * b + 3], axis=0, keepdims=True) for b in range(images)], 0
    )


def rows_from(values, shift):
    if shift == 0:
        return values
    blank = jnp.zeros((HALF, values.shape[1]), values.dtype)
    if shift == 1:
        return jnp.concatenate([values[HALF:], blank], 0)
    return jnp.concatenate([blank, values[:-HALF]], 0)


def columns_from(values, shift):
    if shift == 0:
        return values
    moved = pltpu.roll(values, (-shift) % values.shape[0], 0)
    column = lax.broadcasted_iota(jnp.int32, values.shape, 0) % HALF
    return jnp.where(column == (HALF - 1 if shift == 1 else 0), 0.0, moved)


def gather_terms(terms):
    total = None
    for shift, group in terms.items():
        part = None
        for left, right, right_dim in group:
            product = dot(left, right, 1, right_dim)
            part = product if part is None else part + product
        part = columns_from(part, shift)
        total = part if total is None else total + part
    return total


def split_three(values):
    high = values.astype(BF16)
    rest = values - high.astype(F32)
    middle = rest.astype(BF16)
    low = (rest - middle.astype(F32)).astype(BF16)
    return high, middle, low


def fetch(place, kernel, out, sem):
    share = out.shape[2]
    return pltpu.make_async_copy(kernel.at[:, :, rows_at(1 - place[2], share)], out, sem)


def split_rows(values, count):
    rows = []
    for index in range(values.shape[0]):
        rows += [part.astype(F32) for part in split_three(values[index : index + 1, :])]
    blank = jnp.zeros((count - len(rows), values.shape[1]), F32)
    return jnp.concatenate(rows + [blank], 0).astype(BF16)


def style_kernel(
    place, kernel, latent, a1, b1, a2, b2, a3, b3, features, styles, scaled, send, sem
):
    fetch(place, kernel, send, sem).start()
    for index, (affine, bias) in enumerate(((a1, b1), (a2, b2), (a3, b3))):
        styles[index] = dot(latent[...], affine[...], 1, 0) + bias[...]
    for image in range(features.shape[0]):
        row = styles[0, image : image + 1, :]
        scaled[image] = (features[image].astype(F32) * row).astype(BF16)
    fetch(place, kernel, send, sem).wait()


def pixel_planes(rasters):
    count = len(rasters)
    stacked = jnp.concatenate(rasters, 0)
    lane = lax.broadcasted_iota(jnp.int32, (RES, PLANE), 1)
    line = lax.broadcasted_iota(jnp.int32, (RES, PLANE), 0)
    found = [[None] * 4 for _ in range(count)]
    for qx in range(2):
        choose = jnp.where(line == 2 * (lane % HALF) + qx, 1.0, 0.0).astype(BF16)
        spread_out = dot(stacked, choose, 1, 0)
        for qy in range(2):
            mask = jnp.where(line == 2 * (lane // HALF) + qy, 1.0, 0.0)
            for index in range(count):
                block = spread_out[RES * index : RES * (index + 1)]
                found[index][2 * qy + qx] = jnp.sum(block * mask, axis=0, keepdims=True)
    return found


def planes_kernel(
    place,
    valid,
    gain,
    kernel,
    noise_one,
    noise_two,
    grad_rgb,
    planes_one,
    planes_two,
    colours,
    send,
    sem,
):
    fetch(place, kernel, send, sem).start()
    images = noise_one.shape[0]
    ones = jnp.ones((3, PLANE), F32)
    blank = jnp.zeros((7, PLANE), F32)
    for image in range(images):
        rasters = []
        for index, noise in enumerate((noise_one, noise_two)):
            value = noise[image]
            rasters += list(split_three(value)) + list(split_three(value * gain[:, index : index + 1]))
        keep = valid[image : image + 1, :RES]
        for colour in range(3):
            rasters.append((grad_rgb[image, colour].astype(F32) * keep).astype(BF16))
        found = pixel_planes(rasters)
        for plane in range(4):
            rows = [member[plane] for member in found]
            planes_one[image, plane] = jnp.concatenate(rows[:6] + [ones, blank], 0).astype(BF16)
            planes_two[image, plane] = jnp.concatenate(rows[6:12] + [ones, blank], 0).astype(BF16)
            colours[image, plane] = jnp.concatenate(rows[12:] * 3 + [blank], 0).astype(BF16)
    fetch(place, kernel, send, sem).wait()


def squares_kernel(
    place, styles, kernel, bias, rgb, squares, mine, theirs, add, colour, parts, *, layer
):
    total = None
    for tap in range(kernel.shape[0]):
        value = kernel[tap].astype(F32)
        total = value * value if total is None else total + value * value
    squares[...] = total
    style = styles[layer]
    parts[...] = lax.dot_general(
        style * style,
        total,
        (((1,), (0,)), ((), ())),
        precision=lax.Precision.HIGHEST,
        preferred_element_type=F32,
    )
    share = bias.shape[1]
    mine[...] = parts[:, pl.ds(pl.multiple_of(place[2] * share, share), share)]
    theirs[...] = parts[:, pl.ds(pl.multiple_of((1 - place[2]) * share, share), share)]
    add[...] = jnp.concatenate(
        [jnp.zeros((3, share), F32), jnp.full((3, share), 0.5, F32)]
        + [part.astype(F32) for part in split_three(0.5 * bias[...])]
        + [jnp.zeros((7, share), F32)],
        0,
    ).astype(BF16)
    for image in range(styles.shape[1]):
        weight = rgb[...].astype(F32) * styles[2, image : image + 1, :]
        colour[image] = jnp.concatenate(
            [part.astype(F32) for part in split_three(weight)] + [jnp.zeros((7, share), F32)], 0
        ).astype(BF16)


def scale_half(rows, add, image, plane, demod, weights):
    return rows * (0.5 * demod) + dot(add[image, plane], weights, 0, 0)


def smooth_leaky(half_pre):
    size = jnp.abs(half_pre)
    soft = jnp.maximum(half_pre, 0.0) * 2.0 + jnp.log(1.0 + jnp.exp(-2.0 * size))
    return (0.4 * SQRT_TWO) * half_pre + (0.8 * SQRT_TWO) * soft


def leaky_slope(half_pre):
    return (0.6 * SQRT_TWO) + (0.4 * SQRT_TWO) * jnp.tanh(half_pre)


def column_sum(values):
    return jnp.sum(values, axis=0, keepdims=True)


def square_grad(products, demod):
    return -0.5 * products * demod * demod


def conv_one_kernel(
    place,
    own,
    other,
    k_own,
    k_other,
    sums_own,
    sums_other,
    add,
    weights,
    styles,
    conv,
    scaled,
    demod,
):
    share = own.shape[-1]
    columns = pl.ds(pl.multiple_of(place[2] * share, share), share)
    demod[...] = lax.rsqrt(sums_own[...] + sums_other[...] + EPSILON)
    for qy in range(2):
        for qx in range(2):
            plane = 2 * qy + qx
            terms = {}
            for shift_y, tap_y in UP_TAPS[qy]:
                for shift_x, tap_x in UP_TAPS[qx]:
                    tap = 3 * tap_y + tap_x
                    for source_ref, right in (
                        (own, k_own[tap, :, columns]),
                        (other, k_other[tap]),
                    ):
                        left = jnp.concatenate(
                            [rows_from(source_ref[b], shift_y) for b in range(own.shape[0])], 0
                        )
                        terms.setdefault(shift_x, []).append((left, right, 0))
            total = gather_terms(terms)
            for image in range(own.shape[0]):
                rows = total[image * PLANE : (image + 1) * PLANE]
                conv[image, plane] = rows
                half_pre = scale_half(
                    rows, add, image, plane, demod[image : image + 1, :], weights[...]
                )
                act = smooth_leaky(half_pre)
                scaled[image, plane] = (act * styles[1, image : image + 1, :]).astype(BF16)


def spread(raster, image, wide):
    for block in range(wide.shape[0]):
        lanes = raster[image, :, :, block * 128 : (block + 1) * 128]
        wide[block] = lanes.reshape(wide.shape[1:]).astype(F32)


def read_plane(wide, qy, qx):
    cells = [wide[block, :, qy, pl.ds(qx, HALF, stride=2), :] for block in range(wide.shape[0])]
    return jnp.concatenate([cell.reshape(PLANE, 128) for cell in cells], 1)


def write_plane(wide, qy, qx, values):
    for block in range(wide.shape[0]):
        cell = values[:, block * 128 : (block + 1) * 128].reshape(HALF, HALF, 128)
        wide[block, :, qy, pl.ds(qx, HALF, stride=2), :] = cell


def store_raster(wide, out, image):
    for block in range(wide.shape[0]):
        lanes = wide[block].reshape(RES, RES, 128)
        out[image, :, :, block * 128 : (block + 1) * 128] = lanes.astype(out.dtype)


def conv_two_kernel(
    place,
    own,
    other,
    k_own,
    k_other,
    sums_own,
    sums_other,
    valid,
    add,
    weights,
    colours,
    colour_weights,
    cotangent,
    conv,
    grad_conv,
    demod,
    wide,
    square,
):
    share = own.shape[-1]
    columns = pl.ds(pl.multiple_of(place[2] * share, share), share)
    demod[...] = lax.rsqrt(sums_own[...] + sums_other[...] + EPSILON)

    def one(image):
        spread(cotangent, image, wide)
        products = None
        for qy in range(2):
            for qx in range(2):
                plane = 2 * qy + qx
                terms = {}
                for tap_x in range(3):
                    px, shift_x = source(qx, tap_x)
                    for tap_y in range(3):
                        py, shift_y = source(qy, tap_y)
                        tap = 3 * tap_y + tap_x
                        for source_ref, right in (
                            (own, k_own[tap, :, columns]),
                            (other, k_other[tap]),
                        ):
                            left = rows_from(source_ref[image, 2 * py + px], shift_y)
                            terms.setdefault(shift_x, []).append((left, right, 0))
                rows = gather_terms(terms)
                conv[image, plane] = rows
                half_pre = scale_half(
                    rows, add, image, plane, row_of(demod, image), weights[...]
                )
                grad = read_plane(wide, qy, qx) + dot(colours[image, plane], colour_weights[image], 0, 0)
                row = row_of(demod, image) * row_of(valid, image)
                grad = grad * leaky_slope(half_pre) * row
                grad_conv[plane_at(image, plane), :] = grad.astype(BF16)
                product = column_sum(grad * rows)
                products = product if products is None else products + product
        square[pl.ds(image, 1), :] = square_grad(products, row_of(demod, image))

    each(own.shape[0], one)
    grad_conv[4 * PLANE * own.shape[0] :, :] = split_rows(square[...], 16)


def group_of(groups, tap):
    for index, (count, _) in enumerate(groups):
        if tap < count:
            return index, tap
        tap -= count


def first_taps(groups):
    return [sum(count for count, _ in groups[:index]) for index in range(len(groups))]


def add_term(groups, total, place, kernel, tap, column, lanes, terms, outs):
    group, at = group_of(groups, tap)
    axis = AT[groups[group][1][0]]
    send, keep = outs[2 * group : 2 * group + 2]
    half, share = send.shape[1], total.shape[1]
    columns = rows_at(column, share)
    for start, index, out in ((0, 1 - place[axis], send), (half, place[axis], keep)):
        rows = rows_at(index, half)
        weight = kernel[tap, rows, columns].astype(F32)
        value = total[start : start + half] + weight * terms[rows, :]
        out[at, :, lanes] = value.astype(out.dtype)


def shifted_kernel(scaled, moved):
    def one(image):
        for plane in range(scaled.shape[1]):
            value = scaled[image, plane].astype(F32)
            moved[image, plane] = columns_from(value, 1 if plane % 2 == 0 else -1).astype(BF16)

    each(scaled.shape[0], one)


def kernel_two_grad(place, scaled, moved, g_own, g_other, kernel, styles, *refs):
    outs, terms = refs[:-1], refs[-1]
    half = scaled.shape[3] // 2
    share = g_own.shape[1]
    squared = styles[1] * styles[1]
    for index, (column, grads) in enumerate(((place[2], g_own), (1 - place[2], g_other))):
        terms[...] = 2.0 * exact(squared, squares_behind(grads, scaled.shape[0]), 0, 0)
        for tap in range(9):
            tap_y, tap_x = tap // 3, tap % 3
            axis = AT[GROUPS_TWO[group_of(GROUPS_TWO, tap)[0]][1][0]]
            lanes = (rows_at(1 - place[axis], half), rows_at(place[axis], half))
            left, right = [], []
            for image in range(scaled.shape[0]):
                for qy in range(2):
                    for qx in range(2):
                        py, shift_y = source(qy, tap_y)
                        px, shift_x = source(qx, tap_x)
                        ref = scaled if shift_x == 0 else moved
                        value = jnp.concatenate([ref[image, 2 * py + px, :, at] for at in lanes], 1)
                        left.append(rows_from(value, shift_y))
                        right.append(grads[plane_at(image, 2 * qy + qx), :])
            total = dot(jnp.concatenate(left, 0), jnp.concatenate(right, 0), 0, 0)
            columns = slice(index * share, (index + 1) * share)
            add_term(GROUPS_TWO, total, place, kernel, tap, column, columns, terms, outs)


def kernel_one_grad(place, scaled, g_own, g_other, kernel, styles, *refs):
    outs, (moved, terms) = refs[:-2], refs[-2:]
    half = scaled.shape[2] // 2
    images, share = scaled.shape[0], g_own.shape[1]
    for image in range(images):
        moved[image] = columns_from(scaled[image].astype(F32), 1).astype(BF16)
    squared = styles[0] * styles[0]
    for index, (column, grads) in enumerate(((place[2], g_own), (1 - place[2], g_other))):
        terms[...] = 2.0 * exact(squared, squares_behind(grads, images), 0, 0)
        for qy in range(2):
            for qx in range(2):
                planes = [grads[plane_at(b, 2 * qy + qx), :] for b in range(images)]
                right = jnp.concatenate(planes, 0)
                for shift_y, tap_y in UP_TAPS[qy]:
                    for shift_x, tap_x in UP_TAPS[qx]:
                        tap = 3 * tap_y + tap_x
                        axis = AT[GROUPS_ONE[group_of(GROUPS_ONE, tap)[0]][1][0]]
                        lanes = (rows_at(1 - place[axis], half), rows_at(place[axis], half))
                        ref = moved if shift_x else scaled
                        left = [
                            rows_from(jnp.concatenate([ref[b, :, at] for at in lanes], 1), shift_y)
                            for b in range(images)
                        ]
                        total = dot(jnp.concatenate(left, 0), right, 0, 0)
                        columns = slice(index * share, (index + 1) * share)
                        add_term(GROUPS_ONE, total, place, kernel, tap, column, columns, terms, outs)


def input_two_grad(
    place,
    g_own,
    g_other,
    kernel,
    conv,
    demod,
    add,
    weights,
    styles,
    grad_scaled,
    grad_conv,
    square,
):
    share = g_own.shape[1]
    images = conv.shape[0]
    mine = pl.multiple_of(place[2] * share, share)
    theirs = pl.multiple_of((1 - place[2]) * share, share)

    def one(image):
        products = None
        for py in range(2):
            for px in range(2):
                plane = 2 * py + px
                terms = {}
                for tap_x in range(3):
                    qx = (px - tap_x + 1) & 1
                    shift_x = source(qx, tap_x)[1]
                    for tap_y in range(3):
                        qy = (py - tap_y + 1) & 1
                        shift_y = source(qy, tap_y)[1]
                        tap = 3 * tap_y + tap_x
                        for grads, start in ((g_own, mine), (g_other, theirs)):
                            left = rows_from(grads[plane_at(image, 2 * qy + qx), :], -shift_y)
                            right = kernel[tap, :, pl.ds(start, share)]
                            terms.setdefault(-shift_x, []).append((left, right, 1))
                rows = gather_terms(terms)
                grad_scaled[image, plane] = rows
                values = conv[image, plane]
                half_pre = scale_half(
                    values,
                    add,
                    image,
                    plane,
                    row_of(demod, image),
                    weights[...],
                )
                row = row_of(demod, image) * row_of(styles.at[1], image)
                grad = rows * leaky_slope(half_pre) * row
                grad_conv[plane_at(image, plane), :] = grad.astype(BF16)
                product = column_sum(grad * values)
                products = product if products is None else products + product
        square[pl.ds(image, 1), :] = square_grad(products, row_of(demod, image))

    each(images, one)
    grad_conv[4 * PLANE * images :, :] = split_rows(square[...], 16)


def input_one_grad(
    place, g_own, g_other, kernel, features, styles, grad_features, sums
):
    share = g_own.shape[1]
    mine = pl.multiple_of(place[2] * share, share)
    theirs = pl.multiple_of((1 - place[2]) * share, share)
    images = features.shape[0]
    terms = {}
    for qy in range(2):
        for qx in range(2):
            for shift_y, tap_y in UP_TAPS[qy]:
                for shift_x, tap_x in UP_TAPS[qx]:
                    tap = 3 * tap_y + tap_x
                    for grads, start in ((g_own, mine), (g_other, theirs)):
                        left = jnp.concatenate(
                            [
                                rows_from(grads[plane_at(b, 2 * qy + qx), :], -shift_y)
                                for b in range(images)
                            ], 0
                        )
                        right = kernel[tap, :, pl.ds(start, share)]
                        terms.setdefault(-shift_x, []).append((left, right, 1))
    total = gather_terms(terms)
    for image in range(images):
        rows = total[image * PLANE : (image + 1) * PLANE]
        grad_features[image] = rows * styles[0, image : image + 1, :]
        product = rows * features[image].astype(F32)
        sums[image : image + 1, :] = jnp.sum(product, axis=0, keepdims=True)


def noise_rows(add, image, plane, share):
    pick = lax.broadcasted_iota(jnp.int32, (add.shape[2], share), 0) < 3
    return dot(add[image, plane], jnp.where(pick, 1.0, 0.0).astype(BF16), 0, 0)


def point_sums(image, totals, out):
    for row, total in enumerate(totals):
        out[image, row : row + 1, :] = total
    out[image, len(totals) :, :] = jnp.zeros((8 - len(totals), out.shape[2]), F32)


def outputs_two_kernel(
    conv,
    demod,
    valid,
    add,
    weights,
    colours,
    cotangent,
    styles,
    rgb,
    features_out,
    rgb_rows,
    rgb_grad,
    sums,
    wide,
):
    share = conv.shape[3]
    rgb_grad[...] = jnp.zeros_like(rgb_grad)

    def one(image):
        spread(cotangent, image, wide)
        totals = None
        for plane in range(4):
            qy, qx = plane // 2, plane % 2
            rows = conv[image, plane]
            half_pre = scale_half(rows, add, image, plane, row_of(demod, image), weights[...])
            act = smooth_leaky(half_pre)
            style = row_of(styles.at[2], image)
            keep = row_of(valid, image)
            from_rgb = dot(colours[image, plane], rgb[...], 0, 0)
            grad = (read_plane(wide, qy, qx) + from_rgb * style) * keep * leaky_slope(half_pre)
            write_plane(wide, qy, qx, act * keep)
            to_rgb = (act * style).astype(BF16)
            rgb_rows[image, plane] = dot(rgb[...], to_rgb, 1, 1)[:8]
            rgb_grad[...] += dot(colours[image, plane], to_rgb, 1, 0)
            own = [
                column_sum(grad),
                column_sum(grad * noise_rows(add, image, plane, share)),
                column_sum(from_rgb * act),
                column_sum(act * act) * keep,
            ]
            totals = own if totals is None else [a + b for a, b in zip(totals, own)]
        store_raster(wide, features_out, image)
        point_sums(image, totals, sums)

    each(conv.shape[0], one)


def outputs_one_kernel(
    conv, grad_scaled, demod, valid, add, weights, styles, sums
):
    share = conv.shape[3]

    def one(image):
        totals = None
        for plane in range(4):
            rows = conv[image, plane]
            half_pre = scale_half(rows, add, image, plane, row_of(demod, image), weights[...])
            act = smooth_leaky(half_pre)
            back = grad_scaled[image, plane]
            grad = back * row_of(styles.at[1], image) * leaky_slope(half_pre)
            own = [
                column_sum(grad),
                column_sum(grad * noise_rows(add, image, plane, share)),
                column_sum(back * act),
                column_sum(act * act) * row_of(valid, image),
            ]
            totals = own if totals is None else [a + b for a, b in zip(totals, own)]
        point_sums(image, totals, sums)

    each(conv.shape[0], one)


def upsampling(rows, cols):
    line = lax.broadcasted_iota(jnp.int32, (rows, cols), 0)
    column = lax.broadcasted_iota(jnp.int32, (rows, cols), 1)
    centre, near = line // 2, line // 2 + 2 * (line % 2) - 1
    return jnp.where(column == centre, 0.75, 0.0) + jnp.where(column == near, 0.25, 0.0)


def rgb_kernel(valid, bias, own, other, rgb_in, grad_rgb, rgb_out, grad_in, sums, raster):
    images = rgb_in.shape[0]
    double = upsampling(RES, HALF)
    lane = lax.broadcasted_iota(jnp.int32, (HALF, PLANE), 1)
    line = lax.broadcasted_iota(jnp.int32, (HALF, PLANE), 0)
    mask = jnp.where(lane // HALF == line, 1.0, 0.0)
    for qx in range(2):
        pixel = lax.broadcasted_iota(jnp.int32, (PLANE, 128), 0) % HALF
        column = lax.broadcasted_iota(jnp.int32, (PLANE, 128), 1)
        choose = jnp.where(column == 2 * pixel + qx, 1.0, 0.0)
        for qy in range(2):
            plane = 2 * qy + qx
            rows = []
            for image in range(images):
                both = own[image, plane] + other[image, plane]
                rows += [mask * both[colour : colour + 1] for colour in range(3)]
            found = exact(jnp.concatenate(rows, 0), choose, 1, 0)
            for index in range(3 * images):
                cell = found[HALF * index : HALF * (index + 1)]
                place = (index, pl.ds(qy, HALF, stride=2), slice(None))
                raster[place] = cell if qx == 0 else raster[place] + cell
    squares = jnp.zeros((1, 1), F32)
    biases = [jnp.zeros((1, 1), F32) for _ in range(3)]
    for image in range(images):
        keep = valid[image : image + 1, :RES]
        for colour in range(3):
            skip = exact(exact(double, rgb_in[image, colour], 1, 0), double, 1, 1)
            value = (skip + raster[3 * image + colour, :, :RES]) + bias[:, colour : colour + 1]
            value = value * keep
            rgb_out[image, colour] = value
            squares = squares + jnp.sum(value * value, keepdims=True)
            grad = grad_rgb[image, colour].astype(F32) * keep
            grad_in[image, colour] = exact(exact(double, grad, 0, 0), double, 1, 0)
            biases[colour] = biases[colour] + jnp.sum(grad, keepdims=True)
    sums[...] = jnp.concatenate(
        [jnp.broadcast_to(member, (1, 128)) for member in [squares] + biases]
        + [jnp.zeros((4, 128), F32)],
        0,
    )


def style_grads_kernel(
    place,
    own_one,
    other_one,
    own_two,
    other_two,
    squares_one,
    squares_two,
    styles,
    style_sums,
    sums_one,
    sums_two,
    a1,
    a2,
    a3,
    latent,
    rgb_grad,
    rgb_sums,
    valid,
    pack,
    crossing,
):
    images, share = style_sums.shape
    mine, theirs = rows_at(place[2], share), rows_at(1 - place[2], share)
    rows = []
    for layer, (own, other, squares, sums) in enumerate(
        ((own_one, other_one, squares_one, style_sums), (own_two, other_two, squares_two, None))
    ):
        back = exact(squares_behind(own, images), squares[:, mine], 1, 1) + exact(
            squares_behind(other, images), squares[:, theirs], 1, 1
        )
        if sums is None:
            direct = jnp.concatenate([sums_one[b, 2:3, :] for b in range(images)], 0)
        else:
            direct = sums[...]
        rows.append(direct + 2.0 * styles[layer] * back)
    rows.append(jnp.concatenate([sums_two[b, 2:3, :] for b in range(images)], 0))
    grad_latent = None
    for row, affine in zip(rows, (a1, a2, a3)):
        part = exact(row, affine[...].astype(F32), 1, 1)
        grad_latent = part if grad_latent is None else grad_latent + part
    lane = lax.broadcasted_iota(jnp.int32, (1, share), 1)
    scalars = jnp.zeros((1, share), F32)
    for index, (sums, row) in enumerate(
        ((sums_one, 3), (sums_two, 3), (sums_one, 1), (sums_two, 1))
    ):
        total = sums[0, row : row + 1, :]
        for image in range(1, images):
            total = total + sums[image, row : row + 1, :]
        scalars = scalars + jnp.where(lane == index, jnp.sum(total, keepdims=True), 0.0)
    wide = jnp.concatenate([rgb_sums[...]] * (share // 128), 1)
    for index in range(4):
        scalars = scalars + jnp.where(lane == 4 + index, wide[index : index + 1], 0.0)
    for image in range(images):
        scalars = scalars + jnp.where(lane == 8, valid[image : image + 1, :], 0.0)
    pieces = [grad_latent[b : b + 1, h * share : (h + 1) * share] for b in range(images) for h in (0, 1)]
    blank = jnp.zeros((crossing.shape[0] - len(pieces), share), F32)
    crossing[...] = jnp.concatenate(pieces + [blank], 0)
    values = latent[...].astype(F32)
    packed = [values[:, :share], values[:, share:]] + rows
    for sums in (sums_one, sums_two):
        bias = sums[0, 0:1, :]
        for image in range(1, images):
            bias = bias + sums[image, 0:1, :]
        packed.append(bias)
    packed += [rgb_grad[:3, :], scalars]
    pack[...] = jnp.concatenate(packed, 0)


def latent_kernel(own, other, out):
    total = own[...] + other[...]
    for image in range(out.shape[0]):
        halves = [total[2 * image + half : 2 * image + half + 1] for half in range(2)]
        out[image : image + 1, :] = jnp.concatenate(halves, 1)


def relay_kernel(source, out):
    out[...] = source[...]


def collect(place, packs, groups, everything):
    if len(packs) == 1:
        everything[...] = packs[0][...]
        return
    taps, order = groups[0]
    weight = {"far": 8, "near": 4, "y": 2, "x": 1}
    rows, share = everything.shape[1:]
    for index in range(8):
        at = pl.ds(rows * index, rows)
        device = (
            weight["far"] * (index & 1)
            + weight[order[2]] * ((index >> 1) & 1)
            + weight[order[1]] * (index >> 2)
        )
        mine = place[AT[order[0]]]
        for ref, first in zip(packs, (mine, 1 - mine)):
            both = ref[taps, at, :].astype(F32)
            everything[device + weight[order[0]] * first] = both[:, :share] + both[:, share:]


def spread_kernel(place, *refs, images, groups):
    packs, outs, everything = refs[:-11], refs[-11:-1], refs[-1]
    collect(place, packs, groups, everything)
    count = everything.shape[0]

    def rows(start, size):
        return jnp.concatenate([everything[d, start : start + size, :] for d in range(count)], 0)

    latent = jnp.concatenate([rows(0, images), rows(images, images)], 1)
    at = 2 * images
    for layer in range(3):
        grad = rows(at, images)
        outs[layer][...] = exact(latent, grad, 0, 0)
        outs[3 + layer][...] = jnp.sum(grad, axis=0, keepdims=True)
        at += images
    total = everything[0]
    for device in range(1, count):
        total = total + everything[device]
    outs[6][...] = total[at : at + 1]
    outs[7][...] = total[at + 1 : at + 2]
    outs[8][...] = total[at + 2 : at + 5]
    outs[9][...] = total[total.shape[0] - 1 :]


def scalars_kernel(own, other, gains, rms, rgb_bias):
    lane = lax.broadcasted_iota(jnp.int32, own.shape, 1)
    scalars = own[...] + jnp.where(lane < 4, other[...], 0.0)
    share = scalars.shape[1]
    real = jnp.sum(jnp.where(lane == 8, scalars, 0.0), keepdims=True)
    entries = jnp.where(lane == 4, 3.0 * RES * RES, 2.0 * share * RES * RES)
    roots = jnp.sqrt(jnp.abs(scalars) / (real * entries))

    def pick(values, index):
        return jnp.sum(jnp.where(lane == index, values, 0.0))

    for index, at in enumerate((0, 1, 4)):
        rms[index] = pick(roots, at)
    for index in range(2):
        gains[index] = pick(scalars, 2 + index)
    for index in range(3):
        rgb_bias[index] = pick(scalars, 5 + index)


def fold_kernel(place, *refs, groups, stage):
    count = len(groups)
    sources, outs = refs[: 2 * count], refs[2 * count :]
    for group, (taps, order) in enumerate(groups):
        kept, got = sources[2 * group : 2 * group + 2]
        send, keep = outs[2 * group : 2 * group + 2]
        index = place[AT[order[stage]]]
        away, here = rows_at(1 - index, send.shape[1]), rows_at(index, send.shape[1])

        def one(tap, kept=kept, got=got, send=send, keep=keep, away=away, here=here):
            total = kept[tap, away, :] + got[tap, away, :].astype(F32)
            send[tap] = total.astype(BF16)
            keep[tap] = kept[tap, here, :] + got[tap, here, :].astype(F32)

        each(kept.shape[0], one)


def put_pack(out, tap, place_far, pack):
    for order, part in enumerate(split_three(pack[...])[:2]):
        columns = slice(order * pack.shape[1], (order + 1) * pack.shape[1])
        out[tap, rows_at(place_far, pack.shape[0]), columns] = part


def across_kernel(place, *refs, groups):
    out = refs[-1]
    for group, first in enumerate(first_taps(groups)):
        kept, got = refs[2 * group : 2 * group + 2]

        def one(tap, kept=kept, got=got, first=first):
            out[first + tap] = (kept[tap] + got[tap].astype(F32)).astype(BF16)

        each(kept.shape[0], one)
    if len(refs) > 2 * len(groups) + 1:
        out[9] = jnp.zeros(out.shape[1:], BF16)
        put_pack(out, 9, place[4], refs[-2])


def total_kernel(place, mine, got, *refs, groups):
    packs, outs = refs[: -len(groups)], refs[-len(groups) :]
    extra = groups[0][0]
    for index, pack in enumerate(packs):
        put_pack(outs[0], extra, place[4] if index == 0 else 1 - place[4], pack)
    if mine.shape[0] > 9:
        outs[0][extra] = (mine[9].astype(F32) + got[9].astype(F32)).astype(BF16)
    for out, first, (taps, _) in zip(outs, first_taps(groups), groups):

        def one(tap, out=out, first=first):
            total = mine[first + tap].astype(F32) + got[first + tap].astype(F32)
            out[tap] = total.astype(BF16)

        each(taps, one)


def join_kernel(place, *refs, groups, stage):
    count = len(groups)
    sources, outs = refs[: 2 * count], refs[2 * count :]
    for group, (taps, order) in enumerate(groups):
        own, got = sources[2 * group : 2 * group + 2]
        out = outs[group]
        index = place[AT[order[stage]]]
        here, away = rows_at(index, own.shape[1]), rows_at(1 - index, own.shape[1])

        def one(tap, own=own, got=got, out=out, here=here, away=away):
            out[tap, here, :] = own[tap]
            out[tap, away, :] = got[tap]

        each(out.shape[0], one)


def finish_kernel(place, *refs, groups, away, between=None):
    parts, (out, held, sems) = refs[: len(groups)], refs[-3:]
    _, half, channels = held.shape
    share = channels // 2
    starts = first_taps(groups)
    for part, first, (taps, order) in zip(parts, starts, groups):
        index = place[AT[order[0]]]
        rows = rows_at(1 - index if away else index, half)

        def copy(tap, rows=rows):
            return pltpu.make_async_copy(held.at[tap], out.at[tap, rows, :], sems.at[tap])

        def one(tap, part=part, first=first, copy=copy):
            for side, column in enumerate((place[2], 1 - place[2])):
                value = part[tap, :, side * share : (side + 1) * share]
                held[first + tap, :, rows_at(column, share)] = value.astype(F32)
            copy(first + tap).start()

        each(taps, one)
    if between is not None:
        between()
    for first, (taps, order) in zip(starts, groups):
        index = place[AT[order[0]]]
        rows = rows_at(1 - index if away else index, half)

        def last(tap, rows=rows, first=first):
            pltpu.make_async_copy(
                held.at[first + tap], out.at[first + tap, rows, :], sems.at[first + tap]
            ).wait()

        each(taps, last)


def finish_scalars_kernel(place, *refs, groups):
    count = len(groups)
    parts, (own, other, out, gains, rms, rgb_bias, held, sems) = refs[:count], refs[count + 1 :]

    def between():
        scalars_kernel(own, other, gains, rms, rgb_bias)

    finish_kernel(place, *parts, out, held, sems, groups=groups, away=True, between=between)


def call(body, outs, scratch=(), smem=0, after=(), hbm=(), scalars=(), plain=(), loose=(), whole=(), micros=0, aliases=None):
    outs = outs if isinstance(outs, tuple) else (outs,)
    any_space = pl.BlockSpec(memory_space=pl.ANY)

    def run(*operands):
        count = len(operands)
        spaces = [pltpu.SMEM] * smem + [pltpu.VMEM] * (count - smem)
        for index in loose + whole:
            spaces[index] = pltpu.HBM
        values = [pltpu.with_memory_space_constraint(*pair) for pair in zip(operands, spaces)]

        def inner(*refs):
            body(*refs[:count], *refs[count + len(after) : -1 - len(scratch)], *refs[len(refs) - len(scratch) :])

        results = pl.pallas_call(
            inner,
            out_shape=tuple(
                member if index in hbm + scalars + plain else pltpu.VMEM(member.shape, member.dtype)
                for index, member in enumerate(outs)
            )
            + (shape(8, 128),),
            in_specs=[SMEM] * smem
            + [any_space if index in whole or index in (aliases or {}) else VMEM for index in range(smem, count)]
            + [any_space] * len(after),
            out_specs=tuple(
                any_space if index in hbm else SMEM if index in scalars else VMEM
                for index in range(len(outs))
            )
            + (any_space,),
            scratch_shapes=scratch,
            input_output_aliases=aliases or {},
            name=getattr(body, "func", body).__name__,
            compiler_params=pltpu.CompilerParams(vmem_limit_bytes=VMEM_BYTES),
            cost_estimate=pl.CostEstimate(
                flops=2**10 + int(micros * 1.1e9), bytes_accessed=2**10, transcendentals=0
            ),
        )(*values, *after)
        found, token = results[:-1], results[-1]
        return (found if len(found) > 1 else found[0]), token

    return run


def shape(*dims, kind=F32):
    return jax.ShapeDtypeStruct(dims, kind)


def group_shapes(groups, rows, cols):
    found = ()
    for taps, _ in groups:
        found += (shape(taps, rows, cols, kind=BF16), shape(taps, rows, cols))
    return found


def swap(values, axis_name):
    return lax.ppermute(values, axis_name, SWAP)


def part_of(values, axis, index, size):
    return lax.dynamic_slice_in_dim(values, index * size, size, axis)


def place_pair(index, own, other, axis):
    return jnp.where(
        index == 0,
        jnp.concatenate([own, other], axis=axis),
        jnp.concatenate([other, own], axis=axis),
    )


class Reduction:
    def __init__(self, place, groups, parts):
        self.place, self.groups = place, groups
        self.exchange(parts[0::2], 0)
        self.keep = parts[1::2]

    def exchange(self, parts, stage):
        self.got = [swap(part, order[stage]) for part, (_, order) in zip(parts, self.groups)]

    def pairs(self, own):
        return [member for pair in zip(own, self.got) for member in pair]

    def fold(self, token, stage, micros=STAGE):
        _, rows, cols = self.keep[0].shape
        parts, token = call(
            functools.partial(fold_kernel, groups=self.groups, stage=stage),
            group_shapes(self.groups, rows // 2, cols),
            smem=1,
            after=token if isinstance(token, tuple) else (token,),
            micros=micros,
        )(self.place, *self.pairs(self.keep))
        self.exchange(parts[0::2], stage)
        self.keep = parts[1::2]
        return token

    def across(self, token, *packs, micros=STAGE):
        _, rows, cols = self.keep[0].shape
        self.own, token = call(
            functools.partial(across_kernel, groups=self.groups),
            shape(9 + len(packs), rows, cols, kind=BF16),
            smem=1,
            after=token if isinstance(token, tuple) else (token,),
            micros=micros,
        )(self.place, *self.pairs(self.keep), *packs)
        self.got = swap(self.own, "far")
        return token

    def total(self, token, *packs, micros=STAGE):
        if lax.axis_size("block") > 1:
            self.own = lax.psum(self.own.astype(F32) + self.got.astype(F32), "block").astype(BF16)
            self.got = jnp.zeros_like(self.own)
        taps, rows, cols = self.own.shape
        outs = [shape(count, rows, cols, kind=BF16) for count, _ in self.groups]
        if packs or taps > 9:
            outs[0] = shape(self.groups[0][0] + 1, rows, cols, kind=BF16)
        self.own, token = call(
            functools.partial(total_kernel, groups=self.groups),
            tuple(outs),
            smem=1,
            after=token if isinstance(token, tuple) else (token,),
            micros=micros,
        )(self.place, self.own, self.got, *packs)
        self.exchange(self.own, 2)
        return token

    def join(self, token, stage, micros=STAGE):
        outs = tuple(
            shape(part.shape[0], 2 * part.shape[1], part.shape[2], kind=BF16) for part in self.own
        )
        self.own, token = call(
            functools.partial(join_kernel, groups=self.groups, stage=stage),
            outs,
            smem=1,
            after=token if isinstance(token, tuple) else (token,),
            micros=micros,
        )(self.place, *self.pairs(self.own))
        self.exchange(self.own, stage - 1)
        return token

    def finish_half(self, token, parts, out, away):
        _, half, cols = parts[0].shape
        last = 1 + len(parts)
        return call(
            functools.partial(finish_kernel, groups=self.groups, away=away),
            shape(9, 2 * half, cols),
            [pltpu.VMEM((9, half, cols), F32), pltpu.SemaphoreType.DMA((9,))],
            smem=1,
            after=token if isinstance(token, tuple) else (token,),
            hbm=(0,),
            loose=(last,) if out else (),
            aliases={last: 0} if out else None,
            micros=0,
        )(self.place, *parts, *out)

    def finish_own(self, token):
        return self.finish_half(token, self.own, (), False)

    def finish(self, token, out):
        return self.finish_half(token, self.got, (out,), True)

    def finish_scalars(self, token, out, own, other):
        _, half, cols = self.got[0].shape
        last = 1 + len(self.got)
        return call(
            functools.partial(finish_scalars_kernel, groups=self.groups),
            (shape(9, 2 * half, cols), shape(2), shape(3), shape(3)),
            [pltpu.VMEM((9, half, cols), F32), pltpu.SemaphoreType.DMA((9,))],
            smem=1,
            after=(token,),
            hbm=(0,),
            scalars=(1, 2, 3),
            loose=(last,),
            aliases={last: 0},
        )(self.place, *self.got, out, own, other)


def gather_packs(pack):
    for axis_name in DP[::-1]:
        pack = lax.all_gather(pack[None] if pack.ndim == 2 else pack, axis_name, axis=0, tiled=True)
    return pack


def per_device(
    counts,
    features_in,
    rgb_in,
    latent,
    affine_one,
    affine_bias_one,
    affine_two,
    affine_bias_two,
    affine_three,
    affine_bias_three,
    kernel_one,
    bias_one,
    kernel_two,
    bias_two,
    rgb_weight,
    rgb_bias,
    noise_gain,
    noise_one,
    noise_two,
    grad_features,
    grad_rgb,
):
    images, share = features_in.shape[0], features_in.shape[3]
    channels = share * lax.axis_size("chan")
    me = lax.axis_index("chan")
    place = jnp.stack([lax.axis_index(name) for name in ("x", "y", "chan", "near", "far")])
    place = place.astype(jnp.int32)
    valid = (jnp.arange(images, dtype=jnp.int32) < counts[0]).astype(F32)
    valid_rows = jnp.broadcast_to(valid[:, None], (images, share))
    features = features_in.reshape(images, PLANE, share)
    flat_one = kernel_one.reshape(9, share, channels)
    flat_two = kernel_two.reshape(9, share, channels)
    plane_shape = (images, 4, PLANE, share)
    grad_kind = shape(images * 4 * PLANE + 16, share, kind=BF16)
    half = share // 2
    wide = pltpu.VMEM((share // 128, HALF, 2, RES, 128), F32)

    send_kind = shape(9, share, share, kind=BF16)
    (styles, scaled_one, send_one), token = call(
        style_kernel,
        (
            shape(3, images, share),
            shape(images, PLANE, share, kind=BF16),
            send_kind,
        ),
        [pltpu.SemaphoreType.DMA],
        smem=1,
        loose=tuple(range(2, 10)),
        whole=(1,),
    )(
        place,
        flat_one,
        latent,
        affine_one,
        affine_bias_one.reshape(1, -1),
        affine_two,
        affine_bias_two.reshape(1, -1),
        affine_three,
        affine_bias_three.reshape(1, -1),
        features,
    )
    received_one = swap(send_one, "chan")
    scaled_one_other = swap(scaled_one, "chan")

    def layer_squares(layer, kernel, bias, token):
        (squares, mine, theirs, add, colour), token = call(
            functools.partial(squares_kernel, layer=layer),
            (
                shape(share, channels),
                shape(images, share),
                shape(images, share),
                shape(16, share, kind=BF16),
                shape(images, 16, share, kind=BF16),
            ),
            [pltpu.VMEM((images, channels), F32)],
            smem=1,
            after=(token,),
            loose=(3, 4),
        )(place, styles, kernel, bias.reshape(1, -1), rgb_weight)
        return squares, mine, swap(theirs, "chan"), add, colour, token

    squares_one, mine_one, theirs_one, add_one, _, token = layer_squares(
        0, flat_one, bias_one, token
    )
    (noise_planes_one, noise_planes_two, colours, send_two), token = call(
        planes_kernel,
        (shape(images, 4, 16, PLANE, kind=BF16),) * 3 + (send_kind,),
        [pltpu.SemaphoreType.DMA],
        smem=1,
        after=(token,),
        loose=(2, 4, 5, 6),
        whole=(3,),
    )(place, valid_rows, noise_gain.reshape(1, -1), flat_two, noise_one, noise_two, grad_rgb)
    received_two = swap(send_two, "chan")
    rgb_rows_in = jnp.pad(rgb_weight, ((0, 13), (0, 0)))

    (conv_one, scaled_two, demod_one), token = call(
        conv_one_kernel,
        (shape(*plane_shape), shape(*plane_shape, kind=BF16), shape(images, share)),
        smem=1,
        after=(token,),
        micros=STAGE,
    )(
        place,
        scaled_one,
        scaled_one_other,
        flat_one,
        received_one,
        mine_one,
        theirs_one,
        noise_planes_one,
        add_one,
        styles,
    )
    scaled_two_other = swap(scaled_two, "chan")
    squares_two, mine_two, theirs_two, add_two, colour_weights, token = layer_squares(
        1, flat_two, bias_two, token
    )
    (conv_two, grad_conv_two, demod_two), token = call(
        conv_two_kernel,
        (shape(*plane_shape), grad_kind, shape(images, share)),
        [wide, pltpu.VMEM((images, share), F32)],
        smem=1,
        after=(token,),
    )(
        place,
        scaled_two,
        scaled_two_other,
        flat_two,
        received_two,
        mine_two,
        theirs_two,
        valid_rows,
        noise_planes_two,
        add_two,
        colours,
        colour_weights,
        grad_features,
    )
    grad_conv_two_other = swap(grad_conv_two, "chan")
    shifted_two, token = call(
        shifted_kernel, shape(*plane_shape, kind=BF16), after=(token,)
    )(scaled_two)
    devices = lax.axis_size(DP)
    alone = lax.axis_size("block") == 1
    parts_two, token = call(
        kernel_two_grad,
        group_shapes(GROUPS_TWO, half, channels),
        [pltpu.VMEM((share, share), F32)],
        smem=1,
        after=(token,),
    )(
        place,
        scaled_two,
        shifted_two,
        grad_conv_two,
        grad_conv_two_other,
        flat_two,
        styles,
    )
    reduce_two = Reduction(place, GROUPS_TWO, parts_two)
    (grad_scaled_two, grad_conv_one), token = call(
        input_two_grad,
        (shape(*plane_shape), grad_kind),
        [pltpu.VMEM((images, share), F32)],
        smem=1,
        after=(token,),
    )(
        place,
        grad_conv_two,
        grad_conv_two_other,
        flat_two,
        conv_one,
        demod_one,
        noise_planes_one,
        add_one,
        styles,
    )
    grad_conv_one_other = swap(grad_conv_one, "chan")
    sums_one, token = call(
        outputs_one_kernel, shape(images, 8, share), after=(token,)
    )(
        conv_one,
        grad_scaled_two,
        demod_one,
        valid_rows,
        noise_planes_one,
        add_one,
        styles,
    )
    token = reduce_two.fold(token, 1)
    (features_out, rgb_planes, rgb_grad, sums_two), token = call(
        outputs_two_kernel,
        (
            shape(images, RES, RES, share, kind=BF16),
            shape(images, 4, 8, PLANE),
            shape(16, share),
            shape(images, 8, share),
        ),
        [wide],
        after=(token,),
        plain=(0,),
        loose=(6,),
    )(
        conv_two,
        demod_two,
        valid_rows,
        noise_planes_two,
        add_two,
        colours,
        grad_features,
        styles,
        rgb_rows_in,
    )
    rgb_planes_other = swap(rgb_planes, "chan")
    token = reduce_two.fold(token, 2)
    parts_one, token = call(
        kernel_one_grad,
        group_shapes(GROUPS_ONE, half, channels),
        [pltpu.VMEM((images, PLANE, share), BF16), pltpu.VMEM((share, share), F32)],
        smem=1,
        after=(token, rgb_planes_other),
        micros=STAGE,
    )(place, scaled_one, grad_conv_one, grad_conv_one_other, flat_one, styles)
    reduce_one = Reduction(place, GROUPS_ONE, parts_one)
    token = reduce_two.across(token)
    (grad_features_in, style_sums), token = call(
        input_one_grad,
        (shape(images, PLANE, share), shape(images, share)),
        smem=1,
        after=(token,),
        plain=(0,),
        loose=(4,),
    )(place, grad_conv_one, grad_conv_one_other, flat_one, features, styles)
    (rgb_out, grad_rgb_in, rgb_sums), token = call(
        rgb_kernel,
        (shape(*grad_rgb.shape), shape(*rgb_in.shape), shape(8, 128)),
        [pltpu.VMEM((3 * images, RES, 128), F32)],
        after=(token,),
        plain=(0, 1),
        loose=(1, 4, 5),
    )(valid_rows, rgb_bias.reshape(1, -1), rgb_planes, rgb_planes_other, rgb_in, grad_rgb)
    (pack, crossing), token = call(
        style_grads_kernel,
        (shape(16, share), shape(8, share)),
        smem=1,
        after=(token,),
        loose=(11, 12, 13),
    )(
        place,
        grad_conv_one,
        grad_conv_one_other,
        grad_conv_two,
        grad_conv_two_other,
        squares_one,
        squares_two,
        styles,
        style_sums,
        sums_one,
        sums_two,
        affine_one,
        affine_two,
        affine_three,
        latent,
        rgb_grad,
        rgb_sums,
        valid_rows,
    )
    packs = [pack, swap(pack, "far")] if alone else []
    token = reduce_one.fold(token, 1, micros=0)
    token = reduce_two.total(token, *packs)
    token = reduce_one.fold(token, 2)
    token = reduce_two.join(token, 2)
    token = reduce_one.across(token)
    relayed, token = call(relay_kernel, shape(8, share), after=(token,))(crossing)
    crossing_other = swap(relayed, "chan")
    token = reduce_two.join(token, 1)
    grad_latent, token = call(
        latent_kernel, shape(images, channels), after=(token,), plain=(0,)
    )(crossing, crossing_other)
    sum_two, token = reduce_two.finish_own(token)
    token = reduce_one.total(token)
    sum_two, token = reduce_two.finish(token, sum_two)
    token = reduce_one.join(token, 2)
    if alone:
        packs = [reduce_two.own[0], reduce_two.got[0]]
    else:
        packs = [gather_packs(pack)]
    spread_out, token = call(
        functools.partial(spread_kernel, images=images, groups=GROUPS_TWO),
        (shape(channels, share),) * 3
        + (shape(1, share),) * 5
        + (shape(3, share), shape(1, share)),
        [pltpu.VMEM((devices, 16, share), F32)],
        smem=1,
        after=(token,),
        plain=tuple(range(9)),
    )(place, *packs)
    row_other = swap(spread_out[9], "chan")
    token = reduce_one.join(token, 1)
    sum_one, token = reduce_one.finish_own(token)
    affine_grads, affine_biases, points = spread_out[0:3], spread_out[3:6], spread_out[6:8]
    rgb_total = spread_out[8]
    found, token = reduce_one.finish_scalars(token, sum_one, spread_out[9], row_other)
    sum_one, gains, rms_values, rgb_bias_grad = found
    affine_outs = []
    for grad, bias in zip(affine_grads, affine_biases):
        affine_outs += [grad, bias.reshape(-1)]
    return (
        features_out,
        rgb_out,
        grad_features_in.reshape(features_in.shape),
        grad_rgb_in,
        grad_latent,
        *affine_outs,
        sum_one.reshape(kernel_one.shape),
        points[0].reshape(-1),
        sum_two.reshape(kernel_two.shape),
        points[1].reshape(-1),
        rgb_total,
        rgb_bias_grad,
        gains,
        rms_values,
    )


def solution(mesh):
    blocks = mesh.shape["dp"] // 16
    grid = mesh.devices.reshape(blocks, 2, 2, 2, 2, mesh.shape["chan"])
    split_mesh = Mesh(grid, DP + ("chan",))
    in_specs = (
        P(DP),
        P(DP, None, None, "chan"),
        P(DP, None, None, None),
        P(DP, None),
        P(None, "chan"),
        P("chan"),
        P(None, "chan"),
        P("chan"),
        P(None, "chan"),
        P("chan"),
        P(None, None, "chan", None),
        P("chan"),
        P(None, None, "chan", None),
        P("chan"),
        P(None, "chan"),
        P(),
        P(),
        P(DP, None, None),
        P(DP, None, None),
        P(DP, None, None, "chan"),
        P(DP, None, None, None),
    )
    out_specs = (
        P(DP, None, None, "chan"),
        P(DP, None, None, None),
        P(DP, None, None, "chan"),
        P(DP, None, None, None),
        P(DP, None),
        P(None, "chan"),
        P("chan"),
        P(None, "chan"),
        P("chan"),
        P(None, "chan"),
        P("chan"),
        P(None, None, "chan", None),
        P("chan"),
        P(None, None, "chan", None),
        P("chan"),
        P(None, "chan"),
        P(),
        P(),
        P(),
    )
    return jax.shard_map(
        per_device, mesh=split_mesh, in_specs=in_specs, out_specs=out_specs, check_vma=False
    )
```

```python
import functools

import jax
import jax.numpy as jnp
from jax import lax
from jax.experimental import pallas as pl
from jax.experimental.pallas import tpu as pltpu
from jax.sharding import Mesh, PartitionSpec as P

RES = 32
HALF = 16
PLANE = HALF * HALF
SQRT_TWO = 1.4142135623730951
EPSILON = 1e-08
STAGE = 60
DP = ("block", "far", "near", "y", "x")
SWAP = [(0, 1), (1, 0)]
F32 = jnp.float32
BF16 = jnp.bfloat16
VMEM_BYTES = 16 * 2**20
VMEM = pl.BlockSpec(memory_space=pltpu.VMEM)
SMEM = pl.BlockSpec(memory_space=pltpu.SMEM)
UP_TAPS = (((0, 1),), ((0, 0), (1, 2)))


GROUPS_TWO = ((3, ("x", "y", "near")), (3, ("y", "near", "x")), (3, ("near", "x", "y")))
GROUPS_ONE = ((3, ("x", "y", "near")), (3, ("y", "near", "x")), (3, ("near", "x", "y")))
AT = {"x": 0, "y": 1, "chan": 2, "near": 3, "far": 4}


def dot(left, right, left_dim, right_dim):
    return lax.dot_general(
        left, right, (((left_dim,), (right_dim,)), ((), ())), preferred_element_type=F32
    )


def exact(left, right, left_dim, right_dim):
    return lax.dot_general(
        left,
        right,
        (((left_dim,), (right_dim,)), ((), ())),
        precision=lax.Precision.HIGHEST,
        preferred_element_type=F32,
    )


def source(parity, tap):
    return (parity + tap - 1) & 1, (parity + tap - 1) >> 1


def each(count, body):
    lax.fori_loop(0, count, lambda index, carry: (body(index), carry)[1], 0)


def row_of(ref, index):
    return ref[pl.ds(index, 1), :]


def rows_at(index, count):
    return pl.ds(pl.multiple_of(index * count, count), count)


def plane_at(image, plane):
    return rows_at(4 * image + plane, PLANE)


def squares_behind(ref, images):
    parts = ref[ref.shape[0] - 16 :, :].astype(F32)
    return jnp.concatenate(
        [jnp.sum(parts[3 * b : 3 * b + 3], axis=0, keepdims=True) for b in range(images)], 0
    )


def rows_from(values, shift):
    if shift == 0:
        return values
    blank = jnp.zeros((HALF, values.shape[1]), values.dtype)
    if shift == 1:
        return jnp.concatenate([values[HALF:], blank], 0)
    return jnp.concatenate([blank, values[:-HALF]], 0)


def columns_from(values, shift):
    if shift == 0:
        return values
    moved = pltpu.roll(values, (-shift) % values.shape[0], 0)
    column = lax.broadcasted_iota(jnp.int32, values.shape, 0) % HALF
    return jnp.where(column == (HALF - 1 if shift == 1 else 0), 0.0, moved)


def gather_terms(terms):
    total = None
    for shift, group in terms.items():
        part = None
        for left, right, right_dim in group:
            product = dot(left, right, 1, right_dim)
            part = product if part is None else part + product
        part = columns_from(part, shift)
        total = part if total is None else total + part
    return total


def split_three(values):
    high = values.astype(BF16)
    rest = values - high.astype(F32)
    middle = rest.astype(BF16)
    low = (rest - middle.astype(F32)).astype(BF16)
    return high, middle, low


def fetch(place, kernel, out, sem):
    share = out.shape[2]
    return pltpu.make_async_copy(kernel.at[:, :, rows_at(1 - place[2], share)], out, sem)


def split_rows(values, count):
    rows = []
    for index in range(values.shape[0]):
        rows += [part.astype(F32) for part in split_three(values[index : index + 1, :])]
    blank = jnp.zeros((count - len(rows), values.shape[1]), F32)
    return jnp.concatenate(rows + [blank], 0).astype(BF16)


def style_kernel(
    place, kernel, latent, a1, b1, a2, b2, a3, b3, features, styles, scaled, send, sem
):
    fetch(place, kernel, send, sem).start()
    for index, (affine, bias) in enumerate(((a1, b1), (a2, b2), (a3, b3))):
        styles[index] = dot(latent[...], affine[...], 1, 0) + bias[...]
    for image in range(features.shape[0]):
        row = styles[0, image : image + 1, :]
        scaled[image] = (features[image].astype(F32) * row).astype(BF16)
    fetch(place, kernel, send, sem).wait()


def pixel_planes(rasters):
    count = len(rasters)
    stacked = jnp.concatenate(rasters, 0)
    lane = lax.broadcasted_iota(jnp.int32, (RES, PLANE), 1)
    line = lax.broadcasted_iota(jnp.int32, (RES, PLANE), 0)
    found = [[None] * 4 for _ in range(count)]
    for qx in range(2):
        choose = jnp.where(line == 2 * (lane % HALF) + qx, 1.0, 0.0).astype(BF16)
        spread_out = dot(stacked, choose, 1, 0)
        for qy in range(2):
            mask = jnp.where(line == 2 * (lane // HALF) + qy, 1.0, 0.0)
            for index in range(count):
                block = spread_out[RES * index : RES * (index + 1)]
                found[index][2 * qy + qx] = jnp.sum(block * mask, axis=0, keepdims=True)
    return found


def planes_kernel(
    place,
    valid,
    gain,
    kernel,
    noise_one,
    noise_two,
    grad_rgb,
    planes_one,
    planes_two,
    colours,
    send,
    sem,
):
    fetch(place, kernel, send, sem).start()
    images = noise_one.shape[0]
    ones = jnp.ones((3, PLANE), F32)
    blank = jnp.zeros((7, PLANE), F32)
    for image in range(images):
        rasters = []
        for index, noise in enumerate((noise_one, noise_two)):
            value = noise[image]
            rasters += list(split_three(value)) + list(split_three(value * gain[:, index : index + 1]))
        keep = valid[image : image + 1, :RES]
        for colour in range(3):
            rasters.append((grad_rgb[image, colour].astype(F32) * keep).astype(BF16))
        found = pixel_planes(rasters)
        for plane in range(4):
            rows = [member[plane] for member in found]
            planes_one[image, plane] = jnp.concatenate(rows[:6] + [ones, blank], 0).astype(BF16)
            planes_two[image, plane] = jnp.concatenate(rows[6:12] + [ones, blank], 0).astype(BF16)
            colours[image, plane] = jnp.concatenate(rows[12:] * 3 + [blank], 0).astype(BF16)
    fetch(place, kernel, send, sem).wait()


def squares_kernel(
    place, styles, kernel, bias, rgb, squares, mine, theirs, add, colour, parts, *, layer
):
    total = None
    for tap in range(kernel.shape[0]):
        value = kernel[tap].astype(F32)
        total = value * value if total is None else total + value * value
    squares[...] = total
    style = styles[layer]
    parts[...] = lax.dot_general(
        style * style,
        total,
        (((1,), (0,)), ((), ())),
        precision=lax.Precision.HIGHEST,
        preferred_element_type=F32,
    )
    share = bias.shape[1]
    mine[...] = parts[:, pl.ds(pl.multiple_of(place[2] * share, share), share)]
    theirs[...] = parts[:, pl.ds(pl.multiple_of((1 - place[2]) * share, share), share)]
    add[...] = jnp.concatenate(
        [jnp.zeros((3, share), F32), jnp.full((3, share), 0.5, F32)]
        + [part.astype(F32) for part in split_three(0.5 * bias[...])]
        + [jnp.zeros((7, share), F32)],
        0,
    ).astype(BF16)
    for image in range(styles.shape[1]):
        weight = rgb[...].astype(F32) * styles[2, image : image + 1, :]
        colour[image] = jnp.concatenate(
            [part.astype(F32) for part in split_three(weight)] + [jnp.zeros((7, share), F32)], 0
        ).astype(BF16)


def scale_half(rows, add, image, plane, demod, weights):
    return rows * (0.5 * demod) + dot(add[image, plane], weights, 0, 0)


def smooth_leaky(half_pre):
    size = jnp.abs(half_pre)
    soft = jnp.maximum(half_pre, 0.0) * 2.0 + jnp.log(1.0 + jnp.exp(-2.0 * size))
    return (0.4 * SQRT_TWO) * half_pre + (0.8 * SQRT_TWO) * soft


def leaky_slope(half_pre):
    return (0.6 * SQRT_TWO) + (0.4 * SQRT_TWO) * jnp.tanh(half_pre)


def column_sum(values):
    return jnp.sum(values, axis=0, keepdims=True)


def square_grad(products, demod):
    return -0.5 * products * demod * demod


def conv_one_kernel(
    place,
    own,
    other,
    k_own,
    k_other,
    sums_own,
    sums_other,
    add,
    weights,
    styles,
    conv,
    scaled,
    demod,
):
    share = own.shape[-1]
    columns = pl.ds(pl.multiple_of(place[2] * share, share), share)
    demod[...] = lax.rsqrt(sums_own[...] + sums_other[...] + EPSILON)
    for qy in range(2):
        for qx in range(2):
            plane = 2 * qy + qx
            terms = {}
            for shift_y, tap_y in UP_TAPS[qy]:
                for shift_x, tap_x in UP_TAPS[qx]:
                    tap = 3 * tap_y + tap_x
                    for source_ref, right in (
                        (own, k_own[tap, :, columns]),
                        (other, k_other[tap]),
                    ):
                        left = jnp.concatenate(
                            [rows_from(source_ref[b], shift_y) for b in range(own.shape[0])], 0
                        )
                        terms.setdefault(shift_x, []).append((left, right, 0))
            total = gather_terms(terms)
            for image in range(own.shape[0]):
                rows = total[image * PLANE : (image + 1) * PLANE]
                conv[image, plane] = rows
                half_pre = scale_half(
                    rows, add, image, plane, demod[image : image + 1, :], weights[...]
                )
                act = smooth_leaky(half_pre)
                scaled[image, plane] = (act * styles[1, image : image + 1, :]).astype(BF16)


def spread(raster, image, wide):
    for block in range(wide.shape[0]):
        lanes = raster[image, :, :, block * 128 : (block + 1) * 128]
        wide[block] = lanes.reshape(wide.shape[1:]).astype(F32)


def read_plane(wide, qy, qx):
    cells = [wide[block, :, qy, pl.ds(qx, HALF, stride=2), :] for block in range(wide.shape[0])]
    return jnp.concatenate([cell.reshape(PLANE, 128) for cell in cells], 1)


def write_plane(wide, qy, qx, values):
    for block in range(wide.shape[0]):
        cell = values[:, block * 128 : (block + 1) * 128].reshape(HALF, HALF, 128)
        wide[block, :, qy, pl.ds(qx, HALF, stride=2), :] = cell


def store_raster(wide, out, image):
    for block in range(wide.shape[0]):
        lanes = wide[block].reshape(RES, RES, 128)
        out[image, :, :, block * 128 : (block + 1) * 128] = lanes.astype(out.dtype)


def conv_two_kernel(
    place,
    own,
    other,
    k_own,
    k_other,
    sums_own,
    sums_other,
    valid,
    add,
    weights,
    colours,
    colour_weights,
    cotangent,
    conv,
    grad_conv,
    demod,
    wide,
    square,
):
    share = own.shape[-1]
    columns = pl.ds(pl.multiple_of(place[2] * share, share), share)
    demod[...] = lax.rsqrt(sums_own[...] + sums_other[...] + EPSILON)

    def one(image):
        spread(cotangent, image, wide)
        products = None
        for qy in range(2):
            for qx in range(2):
                plane = 2 * qy + qx
                terms = {}
                for tap_x in range(3):
                    px, shift_x = source(qx, tap_x)
                    for tap_y in range(3):
                        py, shift_y = source(qy, tap_y)
                        tap = 3 * tap_y + tap_x
                        for source_ref, right in (
                            (own, k_own[tap, :, columns]),
                            (other, k_other[tap]),
                        ):
                            left = rows_from(source_ref[image, 2 * py + px], shift_y)
                            terms.setdefault(shift_x, []).append((left, right, 0))
                rows = gather_terms(terms)
                conv[image, plane] = rows
                half_pre = scale_half(
                    rows, add, image, plane, row_of(demod, image), weights[...]
                )
                grad = read_plane(wide, qy, qx) + dot(colours[image, plane], colour_weights[image], 0, 0)
                row = row_of(demod, image) * row_of(valid, image)
                grad = grad * leaky_slope(half_pre) * row
                grad_conv[plane_at(image, plane), :] = grad.astype(BF16)
                product = column_sum(grad * rows)
                products = product if products is None else products + product
        square[pl.ds(image, 1), :] = square_grad(products, row_of(demod, image))

    each(own.shape[0], one)
    grad_conv[4 * PLANE * own.shape[0] :, :] = split_rows(square[...], 16)


def group_of(groups, tap):
    for index, (count, _) in enumerate(groups):
        if tap < count:
            return index, tap
        tap -= count


def first_taps(groups):
    return [sum(count for count, _ in groups[:index]) for index in range(len(groups))]


def add_term(groups, total, place, kernel, tap, column, lanes, terms, outs):
    group, at = group_of(groups, tap)
    axis = AT[groups[group][1][0]]
    send, keep = outs[2 * group : 2 * group + 2]
    half, share = send.shape[1], total.shape[1]
    columns = rows_at(column, share)
    for start, index, out in ((0, 1 - place[axis], send), (half, place[axis], keep)):
        rows = rows_at(index, half)
        weight = kernel[tap, rows, columns].astype(F32)
        value = total[start : start + half] + weight * terms[rows, :]
        out[at, :, lanes] = value.astype(out.dtype)


def shifted_kernel(scaled, moved):
    def one(image):
        for plane in range(scaled.shape[1]):
            value = scaled[image, plane].astype(F32)
            moved[image, plane] = columns_from(value, 1 if plane % 2 == 0 else -1).astype(BF16)

    each(scaled.shape[0], one)


def kernel_two_grad(place, scaled, moved, g_own, g_other, kernel, styles, *refs):
    outs, terms = refs[:-1], refs[-1]
    half = scaled.shape[3] // 2
    share = g_own.shape[1]
    squared = styles[1] * styles[1]
    for index, (column, grads) in enumerate(((place[2], g_own), (1 - place[2], g_other))):
        terms[...] = 2.0 * exact(squared, squares_behind(grads, scaled.shape[0]), 0, 0)
        for tap in range(9):
            tap_y, tap_x = tap // 3, tap % 3
            axis = AT[GROUPS_TWO[group_of(GROUPS_TWO, tap)[0]][1][0]]
            lanes = (rows_at(1 - place[axis], half), rows_at(place[axis], half))
            left, right = [], []
            for image in range(scaled.shape[0]):
                for qy in range(2):
                    for qx in range(2):
                        py, shift_y = source(qy, tap_y)
                        px, shift_x = source(qx, tap_x)
                        ref = scaled if shift_x == 0 else moved
                        value = jnp.concatenate([ref[image, 2 * py + px, :, at] for at in lanes], 1)
                        left.append(rows_from(value, shift_y))
                        right.append(grads[plane_at(image, 2 * qy + qx), :])
            total = dot(jnp.concatenate(left, 0), jnp.concatenate(right, 0), 0, 0)
            columns = slice(index * share, (index + 1) * share)
            add_term(GROUPS_TWO, total, place, kernel, tap, column, columns, terms, outs)


def kernel_one_grad(place, scaled, g_own, g_other, kernel, styles, *refs):
    outs, (moved, terms) = refs[:-2], refs[-2:]
    half = scaled.shape[2] // 2
    images, share = scaled.shape[0], g_own.shape[1]
    for image in range(images):
        moved[image] = columns_from(scaled[image].astype(F32), 1).astype(BF16)
    squared = styles[0] * styles[0]
    for index, (column, grads) in enumerate(((place[2], g_own), (1 - place[2], g_other))):
        terms[...] = 2.0 * exact(squared, squares_behind(grads, images), 0, 0)
        for qy in range(2):
            for qx in range(2):
                planes = [grads[plane_at(b, 2 * qy + qx), :] for b in range(images)]
                right = jnp.concatenate(planes, 0)
                for shift_y, tap_y in UP_TAPS[qy]:
                    for shift_x, tap_x in UP_TAPS[qx]:
                        tap = 3 * tap_y + tap_x
                        axis = AT[GROUPS_ONE[group_of(GROUPS_ONE, tap)[0]][1][0]]
                        lanes = (rows_at(1 - place[axis], half), rows_at(place[axis], half))
                        ref = moved if shift_x else scaled
                        left = [
                            rows_from(jnp.concatenate([ref[b, :, at] for at in lanes], 1), shift_y)
                            for b in range(images)
                        ]
                        total = dot(jnp.concatenate(left, 0), right, 0, 0)
                        columns = slice(index * share, (index + 1) * share)
                        add_term(GROUPS_ONE, total, place, kernel, tap, column, columns, terms, outs)


def input_two_grad(
    place,
    g_own,
    g_other,
    kernel,
    conv,
    demod,
    add,
    weights,
    styles,
    grad_scaled,
    grad_conv,
    square,
):
    share = g_own.shape[1]
    images = conv.shape[0]
    mine = pl.multiple_of(place[2] * share, share)
    theirs = pl.multiple_of((1 - place[2]) * share, share)

    def one(image):
        products = None
        for py in range(2):
            for px in range(2):
                plane = 2 * py + px
                terms = {}
                for tap_x in range(3):
                    qx = (px - tap_x + 1) & 1
                    shift_x = source(qx, tap_x)[1]
                    for tap_y in range(3):
                        qy = (py - tap_y + 1) & 1
                        shift_y = source(qy, tap_y)[1]
                        tap = 3 * tap_y + tap_x
                        for grads, start in ((g_own, mine), (g_other, theirs)):
                            left = rows_from(grads[plane_at(image, 2 * qy + qx), :], -shift_y)
                            right = kernel[tap, :, pl.ds(start, share)]
                            terms.setdefault(-shift_x, []).append((left, right, 1))
                rows = gather_terms(terms)
                grad_scaled[image, plane] = rows
                values = conv[image, plane]
                half_pre = scale_half(
                    values,
                    add,
                    image,
                    plane,
                    row_of(demod, image),
                    weights[...],
                )
                row = row_of(demod, image) * row_of(styles.at[1], image)
                grad = rows * leaky_slope(half_pre) * row
                grad_conv[plane_at(image, plane), :] = grad.astype(BF16)
                product = column_sum(grad * values)
                products = product if products is None else products + product
        square[pl.ds(image, 1), :] = square_grad(products, row_of(demod, image))

    each(images, one)
    grad_conv[4 * PLANE * images :, :] = split_rows(square[...], 16)


def input_one_grad(
    place, g_own, g_other, kernel, features, styles, grad_features, sums
):
    share = g_own.shape[1]
    mine = pl.multiple_of(place[2] * share, share)
    theirs = pl.multiple_of((1 - place[2]) * share, share)
    images = features.shape[0]
    terms = {}
    for qy in range(2):
        for qx in range(2):
            for shift_y, tap_y in UP_TAPS[qy]:
                for shift_x, tap_x in UP_TAPS[qx]:
                    tap = 3 * tap_y + tap_x
                    for grads, start in ((g_own, mine), (g_other, theirs)):
                        left = jnp.concatenate(
                            [
                                rows_from(grads[plane_at(b, 2 * qy + qx), :], -shift_y)
                                for b in range(images)
                            ], 0
                        )
                        right = kernel[tap, :, pl.ds(start, share)]
                        terms.setdefault(-shift_x, []).append((left, right, 1))
    total = gather_terms(terms)
    for image in range(images):
        rows = total[image * PLANE : (image + 1) * PLANE]
        grad_features[image] = rows * styles[0, image : image + 1, :]
        product = rows * features[image].astype(F32)
        sums[image : image + 1, :] = jnp.sum(product, axis=0, keepdims=True)


def noise_rows(add, image, plane, share):
    pick = lax.broadcasted_iota(jnp.int32, (add.shape[2], share), 0) < 3
    return dot(add[image, plane], jnp.where(pick, 1.0, 0.0).astype(BF16), 0, 0)


def point_sums(image, totals, out):
    for row, total in enumerate(totals):
        out[image, row : row + 1, :] = total
    out[image, len(totals) :, :] = jnp.zeros((8 - len(totals), out.shape[2]), F32)


def outputs_two_kernel(
    conv,
    demod,
    valid,
    add,
    weights,
    colours,
    cotangent,
    styles,
    rgb,
    features_out,
    rgb_rows,
    rgb_grad,
    sums,
    wide,
):
    share = conv.shape[3]
    rgb_grad[...] = jnp.zeros_like(rgb_grad)

    def one(image):
        spread(cotangent, image, wide)
        totals = None
        for plane in range(4):
            qy, qx = plane // 2, plane % 2
            rows = conv[image, plane]
            half_pre = scale_half(rows, add, image, plane, row_of(demod, image), weights[...])
            act = smooth_leaky(half_pre)
            style = row_of(styles.at[2], image)
            keep = row_of(valid, image)
            from_rgb = dot(colours[image, plane], rgb[...], 0, 0)
            grad = (read_plane(wide, qy, qx) + from_rgb * style) * keep * leaky_slope(half_pre)
            write_plane(wide, qy, qx, act * keep)
            to_rgb = (act * style).astype(BF16)
            rgb_rows[image, plane] = dot(rgb[...], to_rgb, 1, 1)[:8]
            rgb_grad[...] += dot(colours[image, plane], to_rgb, 1, 0)
            own = [
                column_sum(grad),
                column_sum(grad * noise_rows(add, image, plane, share)),
                column_sum(from_rgb * act),
                column_sum(act * act) * keep,
            ]
            totals = own if totals is None else [a + b for a, b in zip(totals, own)]
        store_raster(wide, features_out, image)
        point_sums(image, totals, sums)

    each(conv.shape[0], one)


def outputs_one_kernel(
    conv, grad_scaled, demod, valid, add, weights, styles, sums
):
    share = conv.shape[3]

    def one(image):
        totals = None
        for plane in range(4):
            rows = conv[image, plane]
            half_pre = scale_half(rows, add, image, plane, row_of(demod, image), weights[...])
            act = smooth_leaky(half_pre)
            back = grad_scaled[image, plane]
            grad = back * row_of(styles.at[1], image) * leaky_slope(half_pre)
            own = [
                column_sum(grad),
                column_sum(grad * noise_rows(add, image, plane, share)),
                column_sum(back * act),
                column_sum(act * act) * row_of(valid, image),
            ]
            totals = own if totals is None else [a + b for a, b in zip(totals, own)]
        point_sums(image, totals, sums)

    each(conv.shape[0], one)


def upsampling(rows, cols):
    line = lax.broadcasted_iota(jnp.int32, (rows, cols), 0)
    column = lax.broadcasted_iota(jnp.int32, (rows, cols), 1)
    centre, near = line // 2, line // 2 + 2 * (line % 2) - 1
    return jnp.where(column == centre, 0.75, 0.0) + jnp.where(column == near, 0.25, 0.0)


def rgb_kernel(valid, bias, own, other, rgb_in, grad_rgb, rgb_out, grad_in, sums, raster):
    images = rgb_in.shape[0]
    double = upsampling(RES, HALF)
    lane = lax.broadcasted_iota(jnp.int32, (HALF, PLANE), 1)
    line = lax.broadcasted_iota(jnp.int32, (HALF, PLANE), 0)
    mask = jnp.where(lane // HALF == line, 1.0, 0.0)
    for qx in range(2):
        pixel = lax.broadcasted_iota(jnp.int32, (PLANE, 128), 0) % HALF
        column = lax.broadcasted_iota(jnp.int32, (PLANE, 128), 1)
        choose = jnp.where(column == 2 * pixel + qx, 1.0, 0.0)
        for qy in range(2):
            plane = 2 * qy + qx
            rows = []
            for image in range(images):
                both = own[image, plane] + other[image, plane]
                rows += [mask * both[colour : colour + 1] for colour in range(3)]
            found = exact(jnp.concatenate(rows, 0), choose, 1, 0)
            for index in range(3 * images):
                cell = found[HALF * index : HALF * (index + 1)]
                place = (index, pl.ds(qy, HALF, stride=2), slice(None))
                raster[place] = cell if qx == 0 else raster[place] + cell
    squares = jnp.zeros((1, 1), F32)
    biases = [jnp.zeros((1, 1), F32) for _ in range(3)]
    for image in range(images):
        keep = valid[image : image + 1, :RES]
        for colour in range(3):
            skip = exact(exact(double, rgb_in[image, colour], 1, 0), double, 1, 1)
            value = (skip + raster[3 * image + colour, :, :RES]) + bias[:, colour : colour + 1]
            value = value * keep
            rgb_out[image, colour] = value
            squares = squares + jnp.sum(value * value, keepdims=True)
            grad = grad_rgb[image, colour].astype(F32) * keep
            grad_in[image, colour] = exact(exact(double, grad, 0, 0), double, 1, 0)
            biases[colour] = biases[colour] + jnp.sum(grad, keepdims=True)
    sums[...] = jnp.concatenate(
        [jnp.broadcast_to(member, (1, 128)) for member in [squares] + biases]
        + [jnp.zeros((4, 128), F32)],
        0,
    )


def style_grads_kernel(
    place,
    own_one,
    other_one,
    own_two,
    other_two,
    squares_one,
    squares_two,
    styles,
    style_sums,
    sums_one,
    sums_two,
    a1,
    a2,
    a3,
    latent,
    rgb_grad,
    rgb_sums,
    valid,
    pack,
    crossing,
):
    images, share = style_sums.shape
    mine, theirs = rows_at(place[2], share), rows_at(1 - place[2], share)
    rows = []
    for layer, (own, other, squares, sums) in enumerate(
        ((own_one, other_one, squares_one, style_sums), (own_two, other_two, squares_two, None))
    ):
        back = exact(squares_behind(own, images), squares[:, mine], 1, 1) + exact(
            squares_behind(other, images), squares[:, theirs], 1, 1
        )
        if sums is None:
            direct = jnp.concatenate([sums_one[b, 2:3, :] for b in range(images)], 0)
        else:
            direct = sums[...]
        rows.append(direct + 2.0 * styles[layer] * back)
    rows.append(jnp.concatenate([sums_two[b, 2:3, :] for b in range(images)], 0))
    grad_latent = None
    for row, affine in zip(rows, (a1, a2, a3)):
        part = exact(row, affine[...].astype(F32), 1, 1)
        grad_latent = part if grad_latent is None else grad_latent + part
    lane = lax.broadcasted_iota(jnp.int32, (1, share), 1)
    scalars = jnp.zeros((1, share), F32)
    for index, (sums, row) in enumerate(
        ((sums_one, 3), (sums_two, 3), (sums_one, 1), (sums_two, 1))
    ):
        total = sums[0, row : row + 1, :]
        for image in range(1, images):
            total = total + sums[image, row : row + 1, :]
        scalars = scalars + jnp.where(lane == index, jnp.sum(total, keepdims=True), 0.0)
    wide = jnp.concatenate([rgb_sums[...]] * (share // 128), 1)
    for index in range(4):
        scalars = scalars + jnp.where(lane == 4 + index, wide[index : index + 1], 0.0)
    for image in range(images):
        scalars = scalars + jnp.where(lane == 8, valid[image : image + 1, :], 0.0)
    pieces = [grad_latent[b : b + 1, h * share : (h + 1) * share] for b in range(images) for h in (0, 1)]
    blank = jnp.zeros((crossing.shape[0] - len(pieces), share), F32)
    crossing[...] = jnp.concatenate(pieces + [blank], 0)
    values = latent[...].astype(F32)
    packed = [values[:, :share], values[:, share:]] + rows
    for sums in (sums_one, sums_two):
        bias = sums[0, 0:1, :]
        for image in range(1, images):
            bias = bias + sums[image, 0:1, :]
        packed.append(bias)
    packed += [rgb_grad[:3, :], scalars]
    pack[...] = jnp.concatenate(packed, 0)


def latent_kernel(own, other, out):
    total = own[...] + other[...]
    for image in range(out.shape[0]):
        halves = [total[2 * image + half : 2 * image + half + 1] for half in range(2)]
        out[image : image + 1, :] = jnp.concatenate(halves, 1)


def relay_kernel(source, out):
    out[...] = source[...]


def collect(place, packs, groups, everything):
    if len(packs) == 1:
        everything[...] = packs[0][...]
        return
    taps, order = groups[0]
    weight = {"far": 8, "near": 4, "y": 2, "x": 1}
    rows, share = everything.shape[1:]
    for index in range(8):
        at = pl.ds(rows * index, rows)
        device = (
            weight["far"] * (index & 1)
            + weight[order[2]] * ((index >> 1) & 1)
            + weight[order[1]] * (index >> 2)
        )
        mine = place[AT[order[0]]]
        for ref, first in zip(packs, (mine, 1 - mine)):
            both = ref[taps, at, :].astype(F32)
            everything[device + weight[order[0]] * first] = both[:, :share] + both[:, share:]


def spread_kernel(place, *refs, images, groups):
    packs, outs, everything = refs[:-11], refs[-11:-1], refs[-1]
    collect(place, packs, groups, everything)
    count = everything.shape[0]

    def rows(start, size):
        return jnp.concatenate([everything[d, start : start + size, :] for d in range(count)], 0)

    latent = jnp.concatenate([rows(0, images), rows(images, images)], 1)
    at = 2 * images
    for layer in range(3):
        grad = rows(at, images)
        outs[layer][...] = exact(latent, grad, 0, 0)
        outs[3 + layer][...] = jnp.sum(grad, axis=0, keepdims=True)
        at += images
    total = everything[0]
    for device in range(1, count):
        total = total + everything[device]
    outs[6][...] = total[at : at + 1]
    outs[7][...] = total[at + 1 : at + 2]
    outs[8][...] = total[at + 2 : at + 5]
    outs[9][...] = total[total.shape[0] - 1 :]


def scalars_kernel(own, other, gains, rms, rgb_bias):
    lane = lax.broadcasted_iota(jnp.int32, own.shape, 1)
    scalars = own[...] + jnp.where(lane < 4, other[...], 0.0)
    share = scalars.shape[1]
    real = jnp.sum(jnp.where(lane == 8, scalars, 0.0), keepdims=True)
    entries = jnp.where(lane == 4, 3.0 * RES * RES, 2.0 * share * RES * RES)
    roots = jnp.sqrt(jnp.abs(scalars) / (real * entries))

    def pick(values, index):
        return jnp.sum(jnp.where(lane == index, values, 0.0))

    for index, at in enumerate((0, 1, 4)):
        rms[index] = pick(roots, at)
    for index in range(2):
        gains[index] = pick(scalars, 2 + index)
    for index in range(3):
        rgb_bias[index] = pick(scalars, 5 + index)


def fold_kernel(place, *refs, groups, stage):
    count = len(groups)
    sources, outs = refs[: 2 * count], refs[2 * count :]
    for group, (taps, order) in enumerate(groups):
        kept, got = sources[2 * group : 2 * group + 2]
        send, keep = outs[2 * group : 2 * group + 2]
        index = place[AT[order[stage]]]
        away, here = rows_at(1 - index, send.shape[1]), rows_at(index, send.shape[1])

        def one(tap, kept=kept, got=got, send=send, keep=keep, away=away, here=here):
            total = kept[tap, away, :] + got[tap, away, :].astype(F32)
            send[tap] = total.astype(BF16)
            keep[tap] = kept[tap, here, :] + got[tap, here, :].astype(F32)

        each(kept.shape[0], one)


def put_pack(out, tap, place_far, pack):
    for order, part in enumerate(split_three(pack[...])[:2]):
        columns = slice(order * pack.shape[1], (order + 1) * pack.shape[1])
        out[tap, rows_at(place_far, pack.shape[0]), columns] = part


def across_kernel(place, *refs, groups):
    out = refs[-1]
    for group, first in enumerate(first_taps(groups)):
        kept, got = refs[2 * group : 2 * group + 2]

        def one(tap, kept=kept, got=got, first=first):
            out[first + tap] = (kept[tap] + got[tap].astype(F32)).astype(BF16)

        each(kept.shape[0], one)
    if len(refs) > 2 * len(groups) + 1:
        out[9] = jnp.zeros(out.shape[1:], BF16)
        put_pack(out, 9, place[4], refs[-2])


def total_kernel(place, mine, got, *refs, groups):
    packs, outs = refs[: -len(groups)], refs[-len(groups) :]
    extra = groups[0][0]
    for index, pack in enumerate(packs):
        put_pack(outs[0], extra, place[4] if index == 0 else 1 - place[4], pack)
    if mine.shape[0] > 9:
        outs[0][extra] = (mine[9].astype(F32) + got[9].astype(F32)).astype(BF16)
    for out, first, (taps, _) in zip(outs, first_taps(groups), groups):

        def one(tap, out=out, first=first):
            total = mine[first + tap].astype(F32) + got[first + tap].astype(F32)
            out[tap] = total.astype(BF16)

        each(taps, one)


def join_kernel(place, *refs, groups, stage):
    count = len(groups)
    sources, outs = refs[: 2 * count], refs[2 * count :]
    for group, (taps, order) in enumerate(groups):
        own, got = sources[2 * group : 2 * group + 2]
        out = outs[group]
        index = place[AT[order[stage]]]
        here, away = rows_at(index, own.shape[1]), rows_at(1 - index, own.shape[1])

        def one(tap, own=own, got=got, out=out, here=here, away=away):
            out[tap, here, :] = own[tap]
            out[tap, away, :] = got[tap]

        each(out.shape[0], one)


def finish_kernel(place, *refs, groups, away, between=None):
    parts, (out, held, sems) = refs[: len(groups)], refs[-3:]
    _, half, channels = held.shape
    share = channels // 2
    starts = first_taps(groups)
    for part, first, (taps, order) in zip(parts, starts, groups):
        index = place[AT[order[0]]]
        rows = rows_at(1 - index if away else index, half)

        def copy(tap, rows=rows):
            return pltpu.make_async_copy(held.at[tap], out.at[tap, rows, :], sems.at[tap])

        def one(tap, part=part, first=first, copy=copy):
            for side, column in enumerate((place[2], 1 - place[2])):
                value = part[tap, :, side * share : (side + 1) * share]
                held[first + tap, :, rows_at(column, share)] = value.astype(F32)
            copy(first + tap).start()

        each(taps, one)
    if between is not None:
        between()
    for first, (taps, order) in zip(starts, groups):
        index = place[AT[order[0]]]
        rows = rows_at(1 - index if away else index, half)

        def last(tap, rows=rows, first=first):
            pltpu.make_async_copy(
                held.at[first + tap], out.at[first + tap, rows, :], sems.at[first + tap]
            ).wait()

        each(taps, last)


def finish_scalars_kernel(place, *refs, groups):
    count = len(groups)
    parts, (own, other, out, gains, rms, rgb_bias, held, sems) = refs[:count], refs[count + 1 :]

    def between():
        scalars_kernel(own, other, gains, rms, rgb_bias)

    finish_kernel(place, *parts, out, held, sems, groups=groups, away=True, between=between)


def call(body, outs, scratch=(), smem=0, after=(), hbm=(), scalars=(), plain=(), loose=(), whole=(), micros=0, aliases=None):
    outs = outs if isinstance(outs, tuple) else (outs,)
    any_space = pl.BlockSpec(memory_space=pl.ANY)

    def run(*operands):
        count = len(operands)
        spaces = [pltpu.SMEM] * smem + [pltpu.VMEM] * (count - smem)
        for index in loose + whole:
            spaces[index] = pltpu.HBM
        values = [pltpu.with_memory_space_constraint(*pair) for pair in zip(operands, spaces)]

        def inner(*refs):
            body(*refs[:count], *refs[count + len(after) : -1 - len(scratch)], *refs[len(refs) - len(scratch) :])

        results = pl.pallas_call(
            inner,
            out_shape=tuple(
                member if index in hbm + scalars + plain else pltpu.VMEM(member.shape, member.dtype)
                for index, member in enumerate(outs)
            )
            + (shape(8, 128),),
            in_specs=[SMEM] * smem
            + [any_space if index in whole or index in (aliases or {}) else VMEM for index in range(smem, count)]
            + [any_space] * len(after),
            out_specs=tuple(
                any_space if index in hbm else SMEM if index in scalars else VMEM
                for index in range(len(outs))
            )
            + (any_space,),
            scratch_shapes=scratch,
            input_output_aliases=aliases or {},
            name=getattr(body, "func", body).__name__,
            compiler_params=pltpu.CompilerParams(vmem_limit_bytes=VMEM_BYTES),
            cost_estimate=pl.CostEstimate(
                flops=2**10 + int(micros * 1.1e9), bytes_accessed=2**10, transcendentals=0
            ),
        )(*values, *after)
        found, token = results[:-1], results[-1]
        return (found if len(found) > 1 else found[0]), token

    return run


def shape(*dims, kind=F32):
    return jax.ShapeDtypeStruct(dims, kind)


def group_shapes(groups, rows, cols):
    found = ()
    for taps, _ in groups:
        found += (shape(taps, rows, cols, kind=BF16), shape(taps, rows, cols))
    return found


def swap(values, axis_name):
    return lax.ppermute(values, axis_name, SWAP)


def part_of(values, axis, index, size):
    return lax.dynamic_slice_in_dim(values, index * size, size, axis)


def place_pair(index, own, other, axis):
    return jnp.where(
        index == 0,
        jnp.concatenate([own, other], axis=axis),
        jnp.concatenate([other, own], axis=axis),
    )


class Reduction:
    def __init__(self, place, groups, parts):
        self.place, self.groups = place, groups
        self.exchange(parts[0::2], 0)
        self.keep = parts[1::2]

    def exchange(self, parts, stage):
        self.got = [swap(part, order[stage]) for part, (_, order) in zip(parts, self.groups)]

    def pairs(self, own):
        return [member for pair in zip(own, self.got) for member in pair]

    def fold(self, token, stage, micros=STAGE):
        _, rows, cols = self.keep[0].shape
        parts, token = call(
            functools.partial(fold_kernel, groups=self.groups, stage=stage),
            group_shapes(self.groups, rows // 2, cols),
            smem=1,
            after=token if isinstance(token, tuple) else (token,),
            micros=micros,
        )(self.place, *self.pairs(self.keep))
        self.exchange(parts[0::2], stage)
        self.keep = parts[1::2]
        return token

    def across(self, token, *packs, micros=STAGE):
        _, rows, cols = self.keep[0].shape
        self.own, token = call(
            functools.partial(across_kernel, groups=self.groups),
            shape(9 + len(packs), rows, cols, kind=BF16),
            smem=1,
            after=token if isinstance(token, tuple) else (token,),
            micros=micros,
        )(self.place, *self.pairs(self.keep), *packs)
        self.got = swap(self.own, "far")
        return token

    def total(self, token, *packs, micros=STAGE):
        if lax.axis_size("block") > 1:
            self.own = lax.psum(self.own.astype(F32) + self.got.astype(F32), "block").astype(BF16)
            self.got = jnp.zeros_like(self.own)
        taps, rows, cols = self.own.shape
        outs = [shape(count, rows, cols, kind=BF16) for count, _ in self.groups]
        if packs or taps > 9:
            outs[0] = shape(self.groups[0][0] + 1, rows, cols, kind=BF16)
        self.own, token = call(
            functools.partial(total_kernel, groups=self.groups),
            tuple(outs),
            smem=1,
            after=token if isinstance(token, tuple) else (token,),
            micros=micros,
        )(self.place, self.own, self.got, *packs)
        self.exchange(self.own, 2)
        return token

    def join(self, token, stage, micros=STAGE):
        outs = tuple(
            shape(part.shape[0], 2 * part.shape[1], part.shape[2], kind=BF16) for part in self.own
        )
        self.own, token = call(
            functools.partial(join_kernel, groups=self.groups, stage=stage),
            outs,
            smem=1,
            after=token if isinstance(token, tuple) else (token,),
            micros=micros,
        )(self.place, *self.pairs(self.own))
        self.exchange(self.own, stage - 1)
        return token

    def finish_half(self, token, parts, out, away):
        _, half, cols = parts[0].shape
        last = 1 + len(parts)
        return call(
            functools.partial(finish_kernel, groups=self.groups, away=away),
            shape(9, 2 * half, cols),
            [pltpu.VMEM((9, half, cols), F32), pltpu.SemaphoreType.DMA((9,))],
            smem=1,
            after=token if isinstance(token, tuple) else (token,),
            hbm=(0,),
            loose=(last,) if out else (),
            aliases={last: 0} if out else None,
            micros=0,
        )(self.place, *parts, *out)

    def finish_own(self, token):
        return self.finish_half(token, self.own, (), False)

    def finish(self, token, out):
        return self.finish_half(token, self.got, (out,), True)

    def finish_scalars(self, token, out, own, other):
        _, half, cols = self.got[0].shape
        last = 1 + len(self.got)
        return call(
            functools.partial(finish_scalars_kernel, groups=self.groups),
            (shape(9, 2 * half, cols), shape(2), shape(3), shape(3)),
            [pltpu.VMEM((9, half, cols), F32), pltpu.SemaphoreType.DMA((9,))],
            smem=1,
            after=(token,),
            hbm=(0,),
            scalars=(1, 2, 3),
            loose=(last,),
            aliases={last: 0},
        )(self.place, *self.got, out, own, other)


def gather_packs(pack):
    for axis_name in DP[::-1]:
        pack = lax.all_gather(pack[None] if pack.ndim == 2 else pack, axis_name, axis=0, tiled=True)
    return pack


def per_device(
    counts,
    features_in,
    rgb_in,
    latent,
    affine_one,
    affine_bias_one,
    affine_two,
    affine_bias_two,
    affine_three,
    affine_bias_three,
    kernel_one,
    bias_one,
    kernel_two,
    bias_two,
    rgb_weight,
    rgb_bias,
    noise_gain,
    noise_one,
    noise_two,
    grad_features,
    grad_rgb,
):
    images, share = features_in.shape[0], features_in.shape[3]
    channels = share * lax.axis_size("chan")
    me = lax.axis_index("chan")
    place = jnp.stack([lax.axis_index(name) for name in ("x", "y", "chan", "near", "far")])
    place = place.astype(jnp.int32)
    valid = (jnp.arange(images, dtype=jnp.int32) < counts[0]).astype(F32)
    valid_rows = jnp.broadcast_to(valid[:, None], (images, share))
    features = features_in.reshape(images, PLANE, share)
    flat_one = kernel_one.reshape(9, share, channels)
    flat_two = kernel_two.reshape(9, share, channels)
    plane_shape = (images, 4, PLANE, share)
    grad_kind = shape(images * 4 * PLANE + 16, share, kind=BF16)
    half = share // 2
    wide = pltpu.VMEM((share // 128, HALF, 2, RES, 128), F32)

    send_kind = shape(9, share, share, kind=BF16)
    (styles, scaled_one, send_one), token = call(
        style_kernel,
        (
            shape(3, images, share),
            shape(images, PLANE, share, kind=BF16),
            send_kind,
        ),
        [pltpu.SemaphoreType.DMA],
        smem=1,
        loose=tuple(range(2, 10)),
        whole=(1,),
    )(
        place,
        flat_one,
        latent,
        affine_one,
        affine_bias_one.reshape(1, -1),
        affine_two,
        affine_bias_two.reshape(1, -1),
        affine_three,
        affine_bias_three.reshape(1, -1),
        features,
    )
    received_one = swap(send_one, "chan")
    scaled_one_other = swap(scaled_one, "chan")

    def layer_squares(layer, kernel, bias, token):
        (squares, mine, theirs, add, colour), token = call(
            functools.partial(squares_kernel, layer=layer),
            (
                shape(share, channels),
                shape(images, share),
                shape(images, share),
                shape(16, share, kind=BF16),
                shape(images, 16, share, kind=BF16),
            ),
            [pltpu.VMEM((images, channels), F32)],
            smem=1,
            after=(token,),
            loose=(3, 4),
        )(place, styles, kernel, bias.reshape(1, -1), rgb_weight)
        return squares, mine, swap(theirs, "chan"), add, colour, token

    squares_one, mine_one, theirs_one, add_one, _, token = layer_squares(
        0, flat_one, bias_one, token
    )
    (noise_planes_one, noise_planes_two, colours, send_two), token = call(
        planes_kernel,
        (shape(images, 4, 16, PLANE, kind=BF16),) * 3 + (send_kind,),
        [pltpu.SemaphoreType.DMA],
        smem=1,
        after=(token,),
        loose=(2, 4, 5, 6),
        whole=(3,),
    )(place, valid_rows, noise_gain.reshape(1, -1), flat_two, noise_one, noise_two, grad_rgb)
    received_two = swap(send_two, "chan")
    rgb_rows_in = jnp.pad(rgb_weight, ((0, 13), (0, 0)))

    (conv_one, scaled_two, demod_one), token = call(
        conv_one_kernel,
        (shape(*plane_shape), shape(*plane_shape, kind=BF16), shape(images, share)),
        smem=1,
        after=(token,),
        micros=STAGE,
    )(
        place,
        scaled_one,
        scaled_one_other,
        flat_one,
        received_one,
        mine_one,
        theirs_one,
        noise_planes_one,
        add_one,
        styles,
    )
    scaled_two_other = swap(scaled_two, "chan")
    squares_two, mine_two, theirs_two, add_two, colour_weights, token = layer_squares(
        1, flat_two, bias_two, token
    )
    (conv_two, grad_conv_two, demod_two), token = call(
        conv_two_kernel,
        (shape(*plane_shape), grad_kind, shape(images, share)),
        [wide, pltpu.VMEM((images, share), F32)],
        smem=1,
        after=(token,),
    )(
        place,
        scaled_two,
        scaled_two_other,
        flat_two,
        received_two,
        mine_two,
        theirs_two,
        valid_rows,
        noise_planes_two,
        add_two,
        colours,
        colour_weights,
        grad_features,
    )
    grad_conv_two_other = swap(grad_conv_two, "chan")
    shifted_two, token = call(
        shifted_kernel, shape(*plane_shape, kind=BF16), after=(token,)
    )(scaled_two)
    devices = lax.axis_size(DP)
    alone = lax.axis_size("block") == 1
    parts_two, token = call(
        kernel_two_grad,
        group_shapes(GROUPS_TWO, half, channels),
        [pltpu.VMEM((share, share), F32)],
        smem=1,
        after=(token,),
    )(
        place,
        scaled_two,
        shifted_two,
        grad_conv_two,
        grad_conv_two_other,
        flat_two,
        styles,
    )
    reduce_two = Reduction(place, GROUPS_TWO, parts_two)
    (grad_scaled_two, grad_conv_one), token = call(
        input_two_grad,
        (shape(*plane_shape), grad_kind),
        [pltpu.VMEM((images, share), F32)],
        smem=1,
        after=(token,),
    )(
        place,
        grad_conv_two,
        grad_conv_two_other,
        flat_two,
        conv_one,
        demod_one,
        noise_planes_one,
        add_one,
        styles,
    )
    grad_conv_one_other = swap(grad_conv_one, "chan")
    sums_one, token = call(
        outputs_one_kernel, shape(images, 8, share), after=(token,)
    )(
        conv_one,
        grad_scaled_two,
        demod_one,
        valid_rows,
        noise_planes_one,
        add_one,
        styles,
    )
    token = reduce_two.fold(token, 1)
    (features_out, rgb_planes, rgb_grad, sums_two), token = call(
        outputs_two_kernel,
        (
            shape(images, RES, RES, share, kind=BF16),
            shape(images, 4, 8, PLANE),
            shape(16, share),
            shape(images, 8, share),
        ),
        [wide],
        after=(token,),
        plain=(0,),
        loose=(6,),
    )(
        conv_two,
        demod_two,
        valid_rows,
        noise_planes_two,
        add_two,
        colours,
        grad_features,
        styles,
        rgb_rows_in,
    )
    rgb_planes_other = swap(rgb_planes, "chan")
    token = reduce_two.fold(token, 2)
    parts_one, token = call(
        kernel_one_grad,
        group_shapes(GROUPS_ONE, half, channels),
        [pltpu.VMEM((images, PLANE, share), BF16), pltpu.VMEM((share, share), F32)],
        smem=1,
        after=(token, rgb_planes_other),
        micros=STAGE,
    )(place, scaled_one, grad_conv_one, grad_conv_one_other, flat_one, styles)
    reduce_one = Reduction(place, GROUPS_ONE, parts_one)
    token = reduce_two.across(token)
    (grad_features_in, style_sums), token = call(
        input_one_grad,
        (shape(images, PLANE, share), shape(images, share)),
        smem=1,
        after=(token,),
        plain=(0,),
        loose=(4,),
    )(place, grad_conv_one, grad_conv_one_other, flat_one, features, styles)
    (rgb_out, grad_rgb_in, rgb_sums), token = call(
        rgb_kernel,
        (shape(*grad_rgb.shape), shape(*rgb_in.shape), shape(8, 128)),
        [pltpu.VMEM((3 * images, RES, 128), F32)],
        after=(token,),
        plain=(0, 1),
        loose=(1, 4, 5),
    )(valid_rows, rgb_bias.reshape(1, -1), rgb_planes, rgb_planes_other, rgb_in, grad_rgb)
    (pack, crossing), token = call(
        style_grads_kernel,
        (shape(16, share), shape(8, share)),
        smem=1,
        after=(token,),
        loose=(11, 12, 13),
    )(
        place,
        grad_conv_one,
        grad_conv_one_other,
        grad_conv_two,
        grad_conv_two_other,
        squares_one,
        squares_two,
        styles,
        style_sums,
        sums_one,
        sums_two,
        affine_one,
        affine_two,
        affine_three,
        latent,
        rgb_grad,
        rgb_sums,
        valid_rows,
    )
    packs = [pack, swap(pack, "far")] if alone else []
    token = reduce_one.fold(token, 1, micros=0)
    token = reduce_two.total(token, *packs)
    token = reduce_one.fold(token, 2)
    token = reduce_two.join(token, 2)
    token = reduce_one.across(token)
    relayed, token = call(relay_kernel, shape(8, share), after=(token,))(crossing)
    crossing_other = swap(relayed, "chan")
    token = reduce_two.join(token, 1)
    grad_latent, token = call(
        latent_kernel, shape(images, channels), after=(token,), plain=(0,)
    )(crossing, crossing_other)
    sum_two, token = reduce_two.finish_own(token)
    token = reduce_one.total(token)
    _, token = call(relay_kernel, shape(8, share), after=(token, *reduce_two.got))(crossing)
    token = reduce_one.join(token, 2)
    sum_two, token = reduce_two.finish(token, sum_two)
    if alone:
        packs = [reduce_two.own[0], reduce_two.got[0]]
    else:
        packs = [gather_packs(pack)]
    spread_out, token = call(
        functools.partial(spread_kernel, images=images, groups=GROUPS_TWO),
        (shape(channels, share),) * 3
        + (shape(1, share),) * 5
        + (shape(3, share), shape(1, share)),
        [pltpu.VMEM((devices, 16, share), F32)],
        smem=1,
        after=(token,),
        plain=tuple(range(9)),
    )(place, *packs)
    row_other = swap(spread_out[9], "chan")
    token = reduce_one.join(token, 1)
    sum_one, token = reduce_one.finish_own(token)
    affine_grads, affine_biases, points = spread_out[0:3], spread_out[3:6], spread_out[6:8]
    rgb_total = spread_out[8]
    found, token = reduce_one.finish_scalars(token, sum_one, spread_out[9], row_other)
    sum_one, gains, rms_values, rgb_bias_grad = found
    affine_outs = []
    for grad, bias in zip(affine_grads, affine_biases):
        affine_outs += [grad, bias.reshape(-1)]
    return (
        features_out,
        rgb_out,
        grad_features_in.reshape(features_in.shape),
        grad_rgb_in,
        grad_latent,
        *affine_outs,
        sum_one.reshape(kernel_one.shape),
        points[0].reshape(-1),
        sum_two.reshape(kernel_two.shape),
        points[1].reshape(-1),
        rgb_total,
        rgb_bias_grad,
        gains,
        rms_values,
    )


def solution(mesh):
    blocks = mesh.shape["dp"] // 16
    grid = mesh.devices.reshape(blocks, 2, 2, 2, 2, mesh.shape["chan"])
    split_mesh = Mesh(grid, DP + ("chan",))
    in_specs = (
        P(DP),
        P(DP, None, None, "chan"),
        P(DP, None, None, None),
        P(DP, None),
        P(None, "chan"),
        P("chan"),
        P(None, "chan"),
        P("chan"),
        P(None, "chan"),
        P("chan"),
        P(None, None, "chan", None),
        P("chan"),
        P(None, None, "chan", None),
        P("chan"),
        P(None, "chan"),
        P(),
        P(),
        P(DP, None, None),
        P(DP, None, None),
        P(DP, None, None, "chan"),
        P(DP, None, None, None),
    )
    out_specs = (
        P(DP, None, None, "chan"),
        P(DP, None, None, None),
        P(DP, None, None, "chan"),
        P(DP, None, None, None),
        P(DP, None),
        P(None, "chan"),
        P("chan"),
        P(None, "chan"),
        P("chan"),
        P(None, "chan"),
        P("chan"),
        P(None, None, "chan", None),
        P("chan"),
        P(None, None, "chan", None),
        P("chan"),
        P(None, "chan"),
        P(),
        P(),
        P(),
    )
    return jax.shard_map(
        per_device, mesh=split_mesh, in_specs=in_specs, out_specs=out_specs, check_vma=False
    )
```
